32 devices in a mesh: batch: 8 (over y, x, core), slab: 4 (over z).
Axes of the slice: x: 2, y: 2, z: 4, core: 2. Of those that a mesh axis runs over, the one named last changes fastest.
Arguments:
- images: bfloat16 [256, 384, 384], P(('batch', 'slab')), may hold values from -6 to 6
- classes: int32 [256], P(('batch', 'slab')), may hold values from 0 to 767
- shifts: int32 [256, 2], P(('batch', 'slab')), may hold values from -16 to 16
- defocus_class: int32 [256], P(('batch', 'slab')), may hold values from 0 to 15
- defocus: float32 [16], replicated, may hold values from 150 to 600
- run_counts: int32 [256, 4], P(('batch', 'slab')), may hold values from 1 to 192, 384 in all within a row
- dest_map: int32 [768, 384], replicated, may hold values from 0 to 15
- ref: bfloat16 [384, 64, 768], P('batch', 'slab'), may hold values from -6 to 6
Outputs:
- updated: bfloat16 [384, 64, 768], P('batch', 'slab')
The draws below stay inside these ranges and needn't reach their ends.
Inputs may be any that keep to these rules, and one draw needn't show every extreme that they name: `run_counts`: each particle's counts sum to 384; in every particle's row the largest count is exactly 192.
All inputs are finite; a program needn't handle non-finite values.
Results may differ from the reference program's by a relative error of at most 0.0065.
Values may be sent and summed in bfloat16 or wider, within the bound.
No kernel may reach another device: no remote copies, remote signals or barrier semaphores. Data moves between devices by JAX's collectives and lax.ppermute only.
A program may use at most 128 MiB of HBM per device.

```python
import math
import jax
import jax.numpy as jnp
import numpy as np
from jax import lax

K = 384
PL_DEV = 16
NCLS = 768
NDEF = 16
SHIFT = 16
PARTICLES = 256
PLANES = 64
MOST = 192
N_SLAB = 4


def place_ends(entries, rng, least, largest):
    dims = entries.shape
    spot = [jax.random.randint(jax.random.fold_in(rng, axis), (), 0, dims[axis]) for axis in range(len(dims))]
    entries = entries.at[tuple(spot)].set(least)
    longest = dims.index(max(dims))
    spot[longest] = (spot[longest] + 1) % dims[longest]
    return entries.at[tuple(spot)].set(largest)


def shard_levels(key, extent, shards, low, top_value):
    loudness, own = 1.0, jax.random.fold_in(key, 6)
    for position, blocks in shards:
        draws = jnp.exp(jax.random.uniform(jax.random.fold_in(own, position), (blocks,), jnp.float32, low / len(shards), top_value / len(shards)))
        loudness = loudness * jnp.repeat(draws, extent[position] // blocks).reshape([-1 if axis == position else 1 for axis in range(len(extent))])
    return loudness


def length_profile(number_of, total, reach, lean):
    weights = [(1 << 20) // math.isqrt(standing ** lean) + 1 for standing in range(2, number_of + 1)]
    surplus, holding = total - reach - (number_of - 1), [1] * (number_of - 1)
    while surplus > 0:
        movable = [i for i in range(number_of - 1) if holding[i] < reach]
        whole, left = sum([weights[i] for i in movable]), surplus
        for i in movable:
            addition = min(reach - holding[i], max(1, left * weights[i] // whole), surplus)
            holding[i] = holding[i] + addition
            surplus = surplus - addition
    return np.array([reach] + holding)


def uneven_parts(rng, amount, total, bound, slope):
    if amount == 2:
        one = jax.random.randint(rng, (), max(1, total - bound), min(bound, total - 1) + 1)
        return jnp.stack([one, total - one])
    lengths = jnp.asarray(length_profile(amount, total, bound, slope), jnp.int32)
    pairs = (amount - 1) // 2
    source_of, receiver = lengths[1:1 + 2 * pairs:2], lengths[2:2 + 2 * pairs:2]
    room = jnp.minimum(source_of - 1, bound - receiver)
    passed = jax.random.randint(jax.random.fold_in(rng, 1), (pairs,), 0, 1 << 20) % (room + 1)
    lengths = lengths.at[1:1 + 2 * pairs:2].set(source_of - passed).at[2:2 + 2 * pairs:2].set(receiver + passed)
    return lengths[jax.random.permutation(jax.random.fold_in(rng, 2), amount)]


def scatter_about(rng, extent, spread, most, split=(), held_as=jnp.bfloat16):
    drawn = spread * jax.random.normal(rng, extent, jnp.float32)
    if split:
        drawn = drawn * shard_levels(rng, extent, split, -0.22, 0.18)
    return jnp.clip(drawn, -most, most).astype(held_as)


def setup_inputs(seed: int = 0) -> dict:
    arg_keys = jax.random.split(jax.random.key(seed), 9)
    return {
        "images": scatter_about(arg_keys[0], (PARTICLES, K, K), 1.0, 6.0, ((0, 32),)),
        "classes": place_ends(jax.random.randint(arg_keys[1], (PARTICLES,), 0, NCLS), jax.random.fold_in(arg_keys[1], 1), 0, NCLS - 1).astype(jnp.int32),
        "shifts": place_ends(jax.random.randint(arg_keys[2], (PARTICLES, 2), 0 - SHIFT, SHIFT + 1), jax.random.fold_in(arg_keys[2], 1), 0 - SHIFT, SHIFT).astype(jnp.int32),
        "defocus_class": place_ends(jax.random.randint(arg_keys[3], (PARTICLES,), 0, NDEF), jax.random.fold_in(arg_keys[3], 1), 0, NDEF - 1).astype(jnp.int32),
        "defocus": jnp.clip(jnp.exp(jax.random.uniform(arg_keys[4], (NDEF,), jnp.float32, math.log(150.0), math.log(600.0))), 150.0, 600.0),
        "run_counts": jax.vmap(lambda own: uneven_parts(own, N_SLAB, K, MOST, 2))(jax.random.split(arg_keys[5], PARTICLES)).reshape((PARTICLES, N_SLAB)).astype(jnp.int32),
        "dest_map": place_ends(jax.random.randint(arg_keys[6], (NCLS, K), 0, PL_DEV), jax.random.fold_in(arg_keys[6], 1), 0, PL_DEV - 1).astype(jnp.int32),
        "ref": scatter_about(arg_keys[7], (K, PLANES, 2 * K), 1.0, 6.0, ((0, 8), (1, 4))),
    }


TAU_PRIOR = 4.0
PHASE_OFFSET = 0.1

def dft_tables(length):
    index = jnp.arange(length, dtype=jnp.int32)
    turns = index[:, None] * index[None, :] % length
    angle = 2.0 * math.pi / length * turns.astype(jnp.float32)
    factor = 1.0 / math.sqrt(length)
    cosine = jnp.cos(angle) * factor
    sine = jnp.sin(angle) * factor
    table_left = jnp.concatenate([cosine, -sine], axis=0).astype(jnp.bfloat16)
    upper_rows = jnp.concatenate([cosine, -sine], axis=1)
    lower_rows = jnp.concatenate([sine, cosine], axis=1)
    table_right = jnp.concatenate([upper_rows, lower_rows], axis=0).astype(jnp.bfloat16)
    return (table_left, table_right)

def contrast(focus_value, freq_row, freq_col, length):
    half_length = length // 2
    spatial_row = ((freq_row + half_length) % length - half_length).astype(jnp.float32) / length
    spatial_col = ((freq_col + half_length) % length - half_length).astype(jnp.float32) / length
    return -jnp.sin(focus_value * (spatial_row * spatial_row + spatial_col * spatial_col) + PHASE_OFFSET)

def shifted_parts(real_part, imag_part, shift_x, shift_y, freq_row, freq_col, length):
    turns = (freq_col * shift_x + freq_row * shift_y) % length
    angle = 2.0 * math.pi / length * turns.astype(jnp.float32)
    cosine = jnp.cos(angle)
    sine = jnp.sin(angle)
    return (real_part * cosine + imag_part * sine, imag_part * cosine - real_part * sine)

def reference(images, classes, shifts, defocus_class, defocus, run_counts, dest_map, ref):
    table_left, table_right = dft_tables(K)
    left_wide = table_left.astype(jnp.float32)
    right_wide = table_right.astype(jnp.float32)
    rows_all = jnp.arange(K, dtype=jnp.int32)
    freq_row = rows_all[:, None]
    freq_col = rows_all[None, :]

    def insert(carry, inputs):
        numerator, weights = carry
        image, orient, shift, focus, counts = inputs
        section = jnp.dot(left_wide, image.astype(jnp.float32), precision=lax.Precision.HIGHEST).astype(jnp.bfloat16)
        section = lax.optimization_barrier(section)
        joined = jnp.concatenate([section[:K], section[K:]], axis=1).astype(jnp.float32)
        spectrum = jnp.dot(joined, right_wide, precision=lax.Precision.HIGHEST)
        real_part, imag_part = shifted_parts(spectrum[:, :K], spectrum[:, K:], shift[0], shift[1], freq_row, freq_col, K)
        transfer = contrast(defocus[focus], freq_row, freq_col, K)
        weighted = jnp.concatenate([transfer * real_part, transfer * imag_part], axis=1).astype(jnp.bfloat16)
        weighted = lax.optimization_barrier(weighted)
        run_ends = jnp.cumsum(counts)
        owner = lax.optimization_barrier(jnp.sum((rows_all[:, None] >= run_ends[None, :]).astype(jnp.int32), axis=1))
        plane = (owner * PL_DEV + dest_map[orient]).astype(jnp.int32)
        numerator = numerator.at[rows_all, plane].add(weighted.astype(jnp.float32))
        weights = weights.at[rows_all, plane].add(transfer * transfer)
        return ((numerator, weights), None)
    start = (jnp.zeros((K, PLANES, 2 * K), jnp.float32), jnp.zeros((K, PLANES, K), jnp.float32))
    (numerator, weights), unused = lax.scan(insert, start, (images, classes, shifts, defocus_class, run_counts))
    prior = ref.astype(jnp.float32)
    denom = weights + TAU_PRIOR
    real_new = (TAU_PRIOR * prior[..., :K] + numerator[..., :K]) / denom
    imag_new = (TAU_PRIOR * prior[..., K:] + numerator[..., K:]) / denom
    return jnp.concatenate([real_new, imag_new], axis=2).astype(jnp.bfloat16)
```

```python
import math

import jax
import jax.numpy as jnp
import numpy as np
from jax import lax
from jax.experimental import pallas as pl
from jax.experimental.pallas import tpu as pltpu
from jax.sharding import PartitionSpec as P

TAU_PRIOR = 4.0
PHASE_OFFSET = 0.1
CHUNKS = 3
VMEM_LIMIT = 48 * 1024 * 1024


def dft_tables(length):
    index = np.arange(length, dtype=np.int32)
    turns = index[:, None] * index[None, :] % length
    angle = np.float32(2.0 * math.pi / length) * turns.astype(np.float32)
    factor = np.float32(1.0 / math.sqrt(length))
    cosine = np.cos(angle) * factor
    sine = np.sin(angle) * factor
    upper_rows = np.concatenate([cosine, -sine], axis=1)
    lower_rows = np.concatenate([sine, cosine], axis=1)
    table_right = np.concatenate([upper_rows, lower_rows], axis=0)
    return cosine, -sine, table_right


def spectrum_kernel(images, left, right, row_factors, col_factors, out, joined):
    particles, length = images.shape[0], images.shape[1]
    owners, _, rows_each, _ = out.shape
    rows = owners * rows_each
    table = left[...]
    for p in range(particles):
        section = jnp.dot(table, images[p], preferred_element_type=jnp.float32)
        section = section.astype(jnp.bfloat16)
        joined[p * rows : (p + 1) * rows, :length] = section[:rows]
        joined[p * rows : (p + 1) * rows, length:] = section[rows:]
    factors = row_factors[...]
    for first in range(0, particles, 2):
        spectrum = jnp.dot(
            joined[first * rows : (first + 2) * rows, :],
            right[...],
            preferred_element_type=jnp.float32,
        )
        for p in range(first, first + 2):
            part = spectrum[(p - first) * rows : (p - first + 1) * rows]
            real_part, imag_part = part[:, :length], part[:, length:]

            def row(q):
                at = q * particles + p
                return factors[:, at : at + 1]

            def col(q):
                at = q * particles + p
                return col_factors[at : at + 1, :]

            transfer = -(row(2) * col(3) + row(3) * col(2))
            cosine = transfer * (row(1) * col(1) - row(0) * col(0))
            sine = transfer * (row(0) * col(1) + row(1) * col(0))
            real_new = real_part * cosine + imag_part * sine
            imag_new = imag_part * cosine - real_part * sine
            weighted = jnp.concatenate([real_new, imag_new], axis=1).astype(jnp.bfloat16)
            out[:, p] = weighted.reshape(owners, rows_each, 2 * length)


def insert_kernel(received, codes, *outs):
    bins = outs[0].shape[0]
    rows = received[...]
    codes_all = codes[...]
    for k, out in enumerate(outs):
        bin_index = lax.broadcasted_iota(jnp.int32, (bins, 1), 0) + k * bins
        hot = jnp.where(codes_all == bin_index, 1.0, 0.0).astype(jnp.bfloat16)
        out[...] = jnp.dot(hot, rows, preferred_element_type=jnp.float32).astype(out.dtype)


def whole_vmem(count):
    return [pl.BlockSpec(memory_space=pltpu.VMEM)] * count


def lookup(values, indices):
    matches = indices[:, None] == jnp.arange(values.shape[0], dtype=jnp.int32)[None, :]
    return jnp.sum(jnp.where(matches, values[None, :], 0.0), axis=1)


def centred_square(freq, length):
    half_length = length // 2
    value = ((freq + half_length) % length - half_length).astype(jnp.float32) / length
    return value * value


def trig_factors(shift, focus, freq, offset, length, axis):
    if axis == 0:
        freq, shift, focus = freq[:, None], shift[None, :], focus[None, :]
    else:
        freq, shift, focus = freq[None, :], shift[:, None], focus[:, None]
    turns = (freq * shift) % length
    phase = 2.0 * math.pi / length * turns.astype(jnp.float32)
    angle = focus * centred_square(freq, length) + offset
    return jnp.concatenate(
        [jnp.sin(phase), jnp.cos(phase), jnp.sin(angle), jnp.cos(angle)], axis=1 - axis
    )


def slab_sums(parts, slab, slab_count):
    if slab_count != 4:
        merged = jnp.stack(parts)
        order = (jnp.arange(slab_count) - slab) % slab_count
        return lax.psum_scatter(
            jnp.take(merged, order, axis=0), "slab", scatter_dimension=0, tiled=False
        ).astype(jnp.float32)
    edge = jnp.where(slab == 0, parts[3], parts[1])
    edge_in = lax.ppermute(edge, "slab", [(0, 1), (3, 2)])
    right_in = lax.ppermute(parts[1], "slab", [(0, 1), (1, 2), (2, 3)])
    left_in = lax.ppermute(parts[3], "slab", [(1, 0), (2, 1), (3, 2)])
    far = (parts[2].astype(jnp.float32) + edge_in.astype(jnp.float32)).astype(jnp.bfloat16)
    far_in = lax.ppermute(far, "slab", [(0, 2), (1, 3), (2, 0), (3, 1)])
    total = parts[0].astype(jnp.float32) + right_in.astype(jnp.float32)
    return total + left_in.astype(jnp.float32) + far_in.astype(jnp.float32)


def per_device(images, classes, shifts, defocus_class, defocus, run_counts, dest_map, ref):
    particles, length, _ = images.shape
    batch_count = lax.axis_size("batch")
    slab_count = lax.axis_size("slab")
    batch = lax.axis_index("batch")
    slab = lax.axis_index("slab")
    rows, planes, _ = ref.shape
    each = rows // CHUNKS
    chunk_rows = batch_count * each
    freq = jnp.arange(length, dtype=jnp.int32)

    ends = jnp.cumsum(run_counts, axis=1)
    meta = jnp.concatenate([classes[:, None], defocus_class[:, None], ends], axis=1)
    meta_all = lax.all_gather(meta, ("batch", "slab"), axis=0, tiled=True)

    cosine, minus_sine, table_right = dft_tables(length)
    order = np.arange(length).reshape(batch_count, CHUNKS, each).transpose(1, 0, 2)
    order = order.reshape(CHUNKS, chunk_rows)
    table_right = jnp.asarray(table_right.astype(jnp.bfloat16))
    focus = lookup(defocus, defocus_class)
    row_factors = trig_factors(shifts[:, 1], focus, freq, PHASE_OFFSET, length, 0)
    col_factors = trig_factors(shifts[:, 0], focus, freq, 0.0, length, 1)
    row_factors = row_factors.reshape(batch_count, CHUNKS, each, 4 * particles)
    row_factors = row_factors.transpose(1, 0, 2, 3).reshape(CHUNKS, chunk_rows, 4 * particles)
    received = []
    for c in range(CHUNKS):
        left = np.concatenate([cosine[order[c]], minus_sine[order[c]]], axis=0)
        weighted = pl.pallas_call(
            spectrum_kernel,
            out_shape=jax.ShapeDtypeStruct(
                (batch_count, particles, each, 2 * length), jnp.bfloat16
            ),
            in_specs=whole_vmem(5),
            out_specs=pl.BlockSpec(memory_space=pltpu.VMEM),
            scratch_shapes=[pltpu.VMEM((particles * chunk_rows, 2 * length), jnp.bfloat16)],
            compiler_params=pltpu.CompilerParams(vmem_limit_bytes=VMEM_LIMIT),
            cost_estimate=pl.CostEstimate(
                flops=2 * particles * chunk_rows * 2 * length * 3 * length,
                bytes_accessed=6 * 1024 * 1024,
                transcendentals=0,
            ),
            name="spectrum",
        )(
            images,
            jnp.asarray(left.astype(jnp.bfloat16)),
            table_right,
            row_factors[c],
            col_factors,
        )
        received.append(lax.all_to_all(weighted, "batch", 0, 0, tiled=True))

    class_count = dest_map.shape[0]
    own_dest = lax.dynamic_slice_in_dim(dest_map, batch * rows, rows, 1).astype(jnp.bfloat16)
    class_hot = (meta_all[:, :1] == jnp.arange(class_count)[None, :]).astype(jnp.bfloat16)
    local_plane = jnp.dot(class_hot, own_dest, preferred_element_type=jnp.float32)
    local_plane = local_plane.astype(jnp.int32)
    own_freq = batch * rows + jnp.arange(rows, dtype=jnp.int32)
    owner = jnp.sum(
        (own_freq[None, :, None] >= meta_all[:, None, 2:]).astype(jnp.int32), axis=2
    )

    grouped = (batch_count, slab_count, particles, rows)
    relative = (owner - slab) % slab_count
    local_bin = relative * (each * planes) + (jnp.arange(rows) % each)[None, :] * planes
    codes = lax.dynamic_index_in_dim(
        (local_bin + local_plane).reshape(grouped), slab, 1, keepdims=False
    )
    codes = codes.reshape(batch_count * particles, CHUNKS, each).transpose(1, 0, 2)
    codes = codes.reshape(CHUNKS, 1, batch_count * particles * each)

    focus_count = defocus.shape[0]
    focus_hot = (meta_all[:, 1:2] == jnp.arange(focus_count)[None, :]).astype(jnp.bfloat16)
    own_plane = jnp.where(owner == slab, local_plane, -1)
    bin_hot = (own_plane.T[:, None, :] == jnp.arange(planes)[None, :, None]).astype(jnp.bfloat16)
    counts = jnp.einsum("kzp,pd->kzd", bin_hot, focus_hot, preferred_element_type=jnp.float32)
    row_angle = 2.0 * (
        defocus[None, :] * centred_square(own_freq, length)[:, None] + PHASE_OFFSET
    )
    col_angle = 2.0 * (defocus[:, None] * centred_square(freq, length)[None, :])
    row_side = jnp.concatenate(
        [counts * jnp.cos(row_angle)[:, None, :], counts * jnp.sin(row_angle)[:, None, :]], axis=2
    )
    col_side = jnp.concatenate([jnp.cos(col_angle), -jnp.sin(col_angle)], axis=0)
    double = jnp.einsum("kzd,dx->kzx", row_side, col_side, precision=lax.Precision.HIGHEST)
    weights = 0.5 * (jnp.sum(counts, axis=2, keepdims=True) - double)
    denom = weights + TAU_PRIOR

    bins = each * planes
    updated = []
    for c in range(CHUNKS):
        rows_in = received[c].reshape(batch_count * particles * each, 2 * length)
        parts = pl.pallas_call(
            insert_kernel,
            out_shape=[jax.ShapeDtypeStruct((bins, 2 * length), jnp.bfloat16)] * slab_count,
            in_specs=whole_vmem(2),
            out_specs=whole_vmem(slab_count),
            compiler_params=pltpu.CompilerParams(vmem_limit_bytes=VMEM_LIMIT),
            cost_estimate=pl.CostEstimate(
                flops=2 * bins * slab_count * rows_in.shape[0] * 2 * length,
                bytes_accessed=4 * 1024 * 1024,
                transcendentals=0,
            ),
            name="insert",
        )(rows_in, codes[c])
        sums = slab_sums(parts, slab, slab_count).reshape(each, planes, 2 * length)
        here = slice(c * each, (c + 1) * each)
        prior = ref[here].astype(jnp.float32)
        under = denom[here]
        updated.append(
            (
                (TAU_PRIOR * prior + sums) / jnp.concatenate([under, under], axis=2)
            ).astype(jnp.bfloat16)
        )
    return jnp.concatenate(updated, axis=0)


def solution(mesh):
    placed = (
        P(("batch", "slab"), None, None),
        P(("batch", "slab")),
        P(("batch", "slab"), None),
        P(("batch", "slab")),
        P(),
        P(("batch", "slab"), None),
        P(),
        P("batch", "slab", None),
    )
    return jax.shard_map(
        per_device, mesh=mesh, in_specs=placed, out_specs=P("batch", "slab", None), check_vma=False
    )
```

```python
import math

import jax
import jax.numpy as jnp
import numpy as np
from jax import lax
from jax.experimental import pallas as pl
from jax.experimental.pallas import tpu as pltpu
from jax.sharding import PartitionSpec as P

TAU_PRIOR = 4.0
PHASE_OFFSET = 0.1
CHUNKS = 3
VMEM_LIMIT = 48 * 1024 * 1024


def dft_tables(length):
    index = np.arange(length, dtype=np.int32)
    turns = index[:, None] * index[None, :] % length
    angle = np.float32(2.0 * math.pi / length) * turns.astype(np.float32)
    factor = np.float32(1.0 / math.sqrt(length))
    cosine = np.cos(angle) * factor
    sine = np.sin(angle) * factor
    upper_rows = np.concatenate([cosine, -sine], axis=1)
    lower_rows = np.concatenate([sine, cosine], axis=1)
    table_right = np.concatenate([upper_rows, lower_rows], axis=0)
    return cosine, -sine, table_right


def spectrum_kernel(images, left, right, row_factors, col_factors, out, joined):
    particles, length = images.shape[0], images.shape[1]
    owners, _, rows_each, _ = out.shape
    rows = owners * rows_each
    table = left[...]
    for p in range(particles):
        section = jnp.dot(table, images[p], preferred_element_type=jnp.float32)
        section = section.astype(jnp.bfloat16)
        joined[p * rows : (p + 1) * rows, :length] = section[:rows]
        joined[p * rows : (p + 1) * rows, length:] = section[rows:]
    factors = row_factors[...]
    for first in range(0, particles, 2):
        spectrum = jnp.dot(
            joined[first * rows : (first + 2) * rows, :],
            right[...],
            preferred_element_type=jnp.float32,
        )
        for p in range(first, first + 2):
            part = spectrum[(p - first) * rows : (p - first + 1) * rows]
            real_part, imag_part = part[:, :length], part[:, length:]

            def row(q):
                at = q * particles + p
                return factors[:, at : at + 1]

            def col(q):
                at = q * particles + p
                return col_factors[at : at + 1, :]

            transfer = -(row(2) * col(3) + row(3) * col(2))
            cosine = transfer * (row(1) * col(1) - row(0) * col(0))
            sine = transfer * (row(0) * col(1) + row(1) * col(0))
            real_new = real_part * cosine + imag_part * sine
            imag_new = imag_part * cosine - real_part * sine
            weighted = jnp.concatenate([real_new, imag_new], axis=1).astype(jnp.bfloat16)
            out[:, p] = weighted.reshape(owners, rows_each, 2 * length)


def insert_kernel(received, codes, *outs):
    bins = outs[0].shape[0]
    rows = received[...]
    codes_all = codes[...]
    for k, out in enumerate(outs):
        bin_index = lax.broadcasted_iota(jnp.int32, (bins, 1), 0) + k * bins
        hot = jnp.where(codes_all == bin_index, 1.0, 0.0).astype(jnp.bfloat16)
        out[...] = jnp.dot(hot, rows, preferred_element_type=jnp.float32).astype(out.dtype)


def whole_vmem(count):
    return [pl.BlockSpec(memory_space=pltpu.VMEM)] * count


def lookup(values, indices):
    matches = indices[:, None] == jnp.arange(values.shape[0], dtype=jnp.int32)[None, :]
    return jnp.sum(jnp.where(matches, values[None, :], 0.0), axis=1)


def centred_square(freq, length):
    half_length = length // 2
    value = ((freq + half_length) % length - half_length).astype(jnp.float32) / length
    return value * value


def trig_factors(shift, focus, freq, offset, length, axis):
    if axis == 0:
        freq, shift, focus = freq[:, None], shift[None, :], focus[None, :]
    else:
        freq, shift, focus = freq[None, :], shift[:, None], focus[:, None]
    turns = (freq * shift) % length
    phase = 2.0 * math.pi / length * turns.astype(jnp.float32)
    angle = focus * centred_square(freq, length) + offset
    return jnp.concatenate(
        [jnp.sin(phase), jnp.cos(phase), jnp.sin(angle), jnp.cos(angle)], axis=1 - axis
    )


def slab_sums(parts, place, slab_count, mirror_count):
    def permute(block, pairs):
        perm = []
        for b in range(2 * mirror_count):
            for source, target in pairs:
                if b >= mirror_count:
                    source, target = slab_count - 1 - source, slab_count - 1 - target
                perm.append((b * slab_count + source, b * slab_count + target))
        return lax.ppermute(block, ("batch", "slab"), perm)

    near_in = permute(jnp.where(place == 2, parts[1], parts[0]), [(3, 2), (2, 1), (1, 0)])
    out_in = permute(jnp.where(place == 0, parts[1], parts[2]), [(0, 1), (1, 2)])
    last_in = permute(parts[2], [(3, 2)])
    merged = (parts[0].astype(jnp.float32) + near_in.astype(jnp.float32)).astype(jnp.bfloat16)
    far = jnp.where(place == 0, parts[2], jnp.where(place == 3, parts[1], merged))

    def finish(far):
        far_in = permute(far, [(3, 1), (2, 0), (0, 2)])
        own = jnp.where(place == 0, parts[0], jnp.where(place == 1, parts[1], parts[2]))
        total = jnp.where(place == 3, 0.0, own.astype(jnp.float32))
        total = total + jnp.where(place == 2, 0.0, near_in.astype(jnp.float32))
        total = total + out_in.astype(jnp.float32) + last_in.astype(jnp.float32)
        return total + far_in.astype(jnp.float32)

    return far, finish


def per_device(images, classes, shifts, defocus_class, defocus, run_counts, dest_map, ref):
    particles, length, _ = images.shape
    batch_count = lax.axis_size("batch")
    slab_count = lax.axis_size("slab")
    batch = lax.axis_index("batch")
    slab = lax.axis_index("slab")
    rows, planes, _ = ref.shape
    each = rows // CHUNKS
    chunk_rows = batch_count * each
    freq = jnp.arange(length, dtype=jnp.int32)

    ends = jnp.cumsum(run_counts, axis=1)
    meta = jnp.concatenate([classes[:, None], defocus_class[:, None], ends], axis=1)

    cosine, minus_sine, table_right = dft_tables(length)
    order = np.arange(length).reshape(batch_count, CHUNKS, each).transpose(1, 0, 2)
    order = order.reshape(CHUNKS, chunk_rows)
    table_right = jnp.asarray(table_right.astype(jnp.bfloat16))
    focus = lookup(defocus, defocus_class)
    row_factors = trig_factors(shifts[:, 1], focus, freq, PHASE_OFFSET, length, 0)
    col_factors = trig_factors(shifts[:, 0], focus, freq, 0.0, length, 1)
    row_factors = row_factors.reshape(batch_count, CHUNKS, each, 4 * particles)
    row_factors = row_factors.transpose(1, 0, 2, 3).reshape(CHUNKS, chunk_rows, 4 * particles)
    received = []
    for c in range(CHUNKS):
        left = np.concatenate([cosine[order[c]], minus_sine[order[c]]], axis=0)
        weighted = pl.pallas_call(
            spectrum_kernel,
            out_shape=jax.ShapeDtypeStruct(
                (batch_count, particles, each, 2 * length), jnp.bfloat16
            ),
            in_specs=whole_vmem(5),
            out_specs=pl.BlockSpec(memory_space=pltpu.VMEM),
            scratch_shapes=[pltpu.VMEM((particles * chunk_rows, 2 * length), jnp.bfloat16)],
            compiler_params=pltpu.CompilerParams(vmem_limit_bytes=VMEM_LIMIT),
            cost_estimate=pl.CostEstimate(
                flops=2 * particles * chunk_rows * 2 * length * 3 * length,
                bytes_accessed=6 * 1024 * 1024,
                transcendentals=0,
            ),
            name="spectrum",
        )(
            images,
            jnp.asarray(left.astype(jnp.bfloat16)),
            table_right,
            row_factors[c],
            col_factors,
        )
        received.append(lax.all_to_all(weighted, "batch", 0, 0, tiled=True))
        if c == 0:
            meta_layer = lax.all_to_all(
                jnp.broadcast_to(meta[None], (batch_count, *meta.shape)), "batch", 0, 0, tiled=True
            )
            meta_all = lax.all_to_all(
                jnp.broadcast_to(meta_layer[None], (slab_count, *meta_layer.shape)),
                "slab",
                0,
                0,
                tiled=True,
            )
            meta_layer = meta_layer.reshape(-1, meta.shape[1])
            meta_all = meta_all.reshape(-1, meta.shape[1])

    class_count = dest_map.shape[0]
    own_dest = lax.dynamic_slice_in_dim(dest_map, batch * rows, rows, 1).astype(jnp.bfloat16)
    own_freq = batch * rows + jnp.arange(rows, dtype=jnp.int32)

    def find_planes(table):
        class_hot = (table[:, :1] == jnp.arange(class_count)[None, :]).astype(jnp.bfloat16)
        local_plane = jnp.dot(class_hot, own_dest, preferred_element_type=jnp.float32)
        past = own_freq[None, :, None] >= table[:, None, 2:]
        return jnp.sum(past.astype(jnp.int32), axis=2), local_plane.astype(jnp.int32)

    mirrored = slab_count == 4 and batch_count % 2 == 0
    window_slabs = 3 if mirrored else slab_count
    owner, local_plane = find_planes(meta_layer)
    place = slab
    if mirrored:
        upper = batch >= batch_count // 2
        owner = jnp.where(upper, slab_count - 1 - owner, owner)
        place = jnp.where(upper, slab_count - 1 - slab, slab)
    codes = owner * (each * planes) + (jnp.arange(rows) % each)[None, :] * planes + local_plane
    codes = codes.reshape(batch_count * particles, CHUNKS, each).transpose(1, 0, 2)
    codes = codes.reshape(CHUNKS, 1, batch_count * particles * each)

    owner, local_plane = find_planes(meta_all)
    focus_count = defocus.shape[0]
    focus_hot = (meta_all[:, 1:2] == jnp.arange(focus_count)[None, :]).astype(jnp.bfloat16)
    own_plane = jnp.where(owner == slab, local_plane, -1)
    bin_hot = (own_plane.T[:, None, :] == jnp.arange(planes)[None, :, None]).astype(jnp.bfloat16)
    counts = jnp.einsum("kzp,pd->kzd", bin_hot, focus_hot, preferred_element_type=jnp.float32)
    row_angle = 2.0 * (
        defocus[None, :] * centred_square(own_freq, length)[:, None] + PHASE_OFFSET
    )
    col_angle = 2.0 * (defocus[:, None] * centred_square(freq, length)[None, :])
    row_side = jnp.concatenate(
        [counts * jnp.cos(row_angle)[:, None, :], counts * jnp.sin(row_angle)[:, None, :]], axis=2
    )
    col_side = jnp.concatenate([jnp.cos(col_angle), -jnp.sin(col_angle)], axis=0)
    double = jnp.einsum("kzd,dx->kzx", row_side, col_side, precision=lax.Precision.HIGHEST)
    weights = 0.5 * (jnp.sum(counts, axis=2, keepdims=True) - double)
    denom = weights + TAU_PRIOR

    bins = each * planes
    sums = []
    far = None
    for c in range(CHUNKS):
        rows_in = received[c].reshape(batch_count * particles * each, 2 * length)
        codes_in = codes[c]
        if far is not None:
            codes_in, far = lax.optimization_barrier((codes_in, far))
            sums.append(finish(far))
        parts = pl.pallas_call(
            insert_kernel,
            out_shape=[jax.ShapeDtypeStruct((bins, 2 * length), jnp.bfloat16)] * window_slabs,
            in_specs=whole_vmem(2),
            out_specs=whole_vmem(window_slabs),
            compiler_params=pltpu.CompilerParams(vmem_limit_bytes=VMEM_LIMIT),
            cost_estimate=pl.CostEstimate(
                flops=2 * bins * window_slabs * rows_in.shape[0] * 2 * length,
                bytes_accessed=4 * 1024 * 1024,
                transcendentals=0,
            ),
            name="insert",
        )(rows_in, codes_in)
        if mirrored:
            far, finish = slab_sums(parts, place, slab_count, batch_count // 2)
        else:
            windows = jnp.stack(parts)
            sums.append(lax.psum_scatter(windows, "slab", scatter_dimension=0, tiled=False))
    if far is not None:
        sums.append(finish(far))
    updated = []
    for c in range(CHUNKS):
        here = slice(c * each, (c + 1) * each)
        prior = ref[here].astype(jnp.float32)
        under = denom[here]
        total = sums[c].astype(jnp.float32).reshape(each, planes, 2 * length)
        updated.append(
            (
                (TAU_PRIOR * prior + total) / jnp.concatenate([under, under], axis=2)
            ).astype(jnp.bfloat16)
        )
    return jnp.concatenate(updated, axis=0)


def solution(mesh):
    placed = (
        P(("batch", "slab"), None, None),
        P(("batch", "slab")),
        P(("batch", "slab"), None),
        P(("batch", "slab")),
        P(),
        P(("batch", "slab"), None),
        P(),
        P("batch", "slab", None),
    )
    return jax.shard_map(
        per_device, mesh=mesh, in_specs=placed, out_specs=P("batch", "slab", None), check_vma=False
    )
```

```python
import math

import jax
import jax.numpy as jnp
import numpy as np
from jax import lax
from jax.experimental import pallas as pl
from jax.experimental.pallas import tpu as pltpu
from jax.sharding import PartitionSpec as P

TAU_PRIOR = 4.0
PHASE_OFFSET = 0.1
CHUNKS = 3
META_BASE = 32
META_ROWS = 16
VMEM_LIMIT = 48 * 1024 * 1024


def dft_tables(length):
    index = np.arange(length, dtype=np.int32)
    turns = index[:, None] * index[None, :] % length
    angle = np.float32(2.0 * math.pi / length) * turns.astype(np.float32)
    factor = np.float32(1.0 / math.sqrt(length))
    cosine = np.cos(angle) * factor
    sine = np.sin(angle) * factor
    upper_rows = np.concatenate([cosine, -sine], axis=1)
    lower_rows = np.concatenate([sine, cosine], axis=1)
    table_right = np.concatenate([upper_rows, lower_rows], axis=0)
    return cosine, -sine, table_right


def spectrum_kernel(images, left, right, row_factors, col_factors, *rest):
    *meta, out, joined = rest
    particles, length = images.shape[0], images.shape[1]
    owners = out.shape[0]
    rows = row_factors.shape[0]
    rows_each = rows // owners
    for block in meta:
        for d in range(owners):
            out[d, particles * rows_each :, :] = block[...]
    table = left[...]
    for p in range(particles):
        section = jnp.dot(table, images[p], preferred_element_type=jnp.float32)
        section = section.astype(jnp.bfloat16)
        joined[p * rows : (p + 1) * rows, :length] = section[:rows]
        joined[p * rows : (p + 1) * rows, length:] = section[rows:]
    factors = row_factors[...]
    for first in range(0, particles, 2):
        spectrum = jnp.dot(
            joined[first * rows : (first + 2) * rows, :],
            right[...],
            preferred_element_type=jnp.float32,
        )
        for p in range(first, first + 2):
            part = spectrum[(p - first) * rows : (p - first + 1) * rows]
            real_part, imag_part = part[:, :length], part[:, length:]

            def row(q):
                at = q * particles + p
                return factors[:, at : at + 1]

            def col(q):
                at = q * particles + p
                return col_factors[at : at + 1, :]

            transfer = -(row(2) * col(3) + row(3) * col(2))
            cosine = transfer * (row(1) * col(1) - row(0) * col(0))
            sine = transfer * (row(0) * col(1) + row(1) * col(0))
            real_new = real_part * cosine + imag_part * sine
            imag_new = imag_part * cosine - real_part * sine
            weighted = jnp.concatenate([real_new, imag_new], axis=1).astype(jnp.bfloat16)
            out[:, p * rows_each : (p + 1) * rows_each, :] = weighted.reshape(
                owners, rows_each, 2 * length
            )


def insert_kernel(received, codes, *outs):
    bins = outs[0].shape[0]
    rows = received[...]
    codes_all = codes[...]
    for k, out in enumerate(outs):
        bin_index = lax.broadcasted_iota(jnp.int32, (bins, 1), 0) + k * bins
        hot = jnp.where(codes_all == bin_index, 1.0, 0.0).astype(jnp.bfloat16)
        out[...] = jnp.dot(hot, rows, preferred_element_type=jnp.float32).astype(out.dtype)


def whole_vmem(count):
    return [pl.BlockSpec(memory_space=pltpu.VMEM)] * count


def lookup(values, indices):
    matches = indices[:, None] == jnp.arange(values.shape[0], dtype=jnp.int32)[None, :]
    return jnp.sum(jnp.where(matches, values[None, :], 0.0), axis=1)


def centred_square(freq, length):
    half_length = length // 2
    value = ((freq + half_length) % length - half_length).astype(jnp.float32) / length
    return value * value


def trig_factors(shift, focus, freq, offset, length, axis):
    if axis == 0:
        freq, shift, focus = freq[:, None], shift[None, :], focus[None, :]
    else:
        freq, shift, focus = freq[None, :], shift[:, None], focus[:, None]
    turns = (freq * shift) % length
    phase = 2.0 * math.pi / length * turns.astype(jnp.float32)
    angle = focus * centred_square(freq, length) + offset
    return jnp.concatenate(
        [jnp.sin(phase), jnp.cos(phase), jnp.sin(angle), jnp.cos(angle)], axis=1 - axis
    )


def slab_sums(parts, place, slab_count, mirror_count):
    def permute(block, pairs):
        perm = []
        for b in range(2 * mirror_count):
            for source, target in pairs:
                if b >= mirror_count:
                    source, target = slab_count - 1 - source, slab_count - 1 - target
                perm.append((b * slab_count + source, b * slab_count + target))
        return lax.ppermute(block, ("batch", "slab"), perm)

    near_in = permute(jnp.where(place == 2, parts[1], parts[0]), [(3, 2), (2, 1), (1, 0)])
    out_in = permute(jnp.where(place == 0, parts[1], parts[2]), [(0, 1), (1, 2)])
    merged = (parts[0].astype(jnp.float32) + near_in.astype(jnp.float32)).astype(jnp.bfloat16)
    far = jnp.where(place == 0, parts[2], jnp.where(place == 3, parts[1], merged))
    far, last = lax.optimization_barrier((far, parts[2]))
    far_in = permute(far, [(3, 1), (2, 0), (0, 2)])
    last_in = permute(last, [(3, 2)])
    own = jnp.where(place == 0, parts[0], jnp.where(place == 1, parts[1], parts[2]))
    total = jnp.where(place == 3, 0.0, own.astype(jnp.float32))
    total = total + jnp.where(place == 2, 0.0, near_in.astype(jnp.float32))
    total = total + out_in.astype(jnp.float32) + last_in.astype(jnp.float32)
    return total + far_in.astype(jnp.float32)


def per_device(images, classes, shifts, defocus_class, defocus, run_counts, dest_map, ref):
    particles, length, _ = images.shape
    batch_count = lax.axis_size("batch")
    slab_count = lax.axis_size("slab")
    batch = lax.axis_index("batch")
    slab = lax.axis_index("slab")
    rows, planes, _ = ref.shape
    each = rows // CHUNKS
    chunk_rows = batch_count * each
    freq = jnp.arange(length, dtype=jnp.int32)

    ends = jnp.cumsum(run_counts, axis=1)[:, : slab_count - 1]
    meta = jnp.concatenate([classes[:, None], defocus_class[:, None], ends], axis=1)
    fields = meta.shape[1]
    digits = jnp.concatenate([meta // META_BASE, meta % META_BASE], axis=1).astype(jnp.bfloat16)
    digits = jnp.pad(digits, ((0, META_ROWS - particles), (0, 2 * length - 2 * fields)))

    cosine, minus_sine, table_right = dft_tables(length)
    order = np.arange(length).reshape(batch_count, CHUNKS, each).transpose(1, 0, 2)
    order = order.reshape(CHUNKS, chunk_rows)
    table_right = jnp.asarray(table_right.astype(jnp.bfloat16))
    focus = lookup(defocus, defocus_class)
    row_factors = trig_factors(shifts[:, 1], focus, freq, PHASE_OFFSET, length, 0)
    col_factors = trig_factors(shifts[:, 0], focus, freq, 0.0, length, 1)
    row_factors = row_factors.reshape(batch_count, CHUNKS, each, 4 * particles)
    row_factors = row_factors.transpose(1, 0, 2, 3).reshape(CHUNKS, chunk_rows, 4 * particles)
    received = []
    for c in range(CHUNKS):
        left = np.concatenate([cosine[order[c]], minus_sine[order[c]]], axis=0)
        extra = (digits,) if c == 0 else ()
        block_rows = particles * each + META_ROWS * len(extra)
        weighted = pl.pallas_call(
            spectrum_kernel,
            out_shape=jax.ShapeDtypeStruct((batch_count, block_rows, 2 * length), jnp.bfloat16),
            in_specs=whole_vmem(5 + len(extra)),
            out_specs=pl.BlockSpec(memory_space=pltpu.VMEM),
            scratch_shapes=[pltpu.VMEM((particles * chunk_rows, 2 * length), jnp.bfloat16)],
            compiler_params=pltpu.CompilerParams(vmem_limit_bytes=VMEM_LIMIT),
            cost_estimate=pl.CostEstimate(
                flops=2 * particles * chunk_rows * 2 * length * 3 * length,
                bytes_accessed=6 * 1024 * 1024,
                transcendentals=0,
            ),
            name="spectrum",
        )(
            images,
            jnp.asarray(left.astype(jnp.bfloat16)),
            table_right,
            row_factors[c],
            col_factors,
            *extra,
        )
        received.append(lax.all_to_all(weighted, "batch", 0, 0, tiled=True))

    digits_in = received[0][:, particles * each : particles * (each + 1), : 2 * fields]
    digits_in = digits_in.astype(jnp.int32).reshape(-1, 2 * fields)
    meta_layer = digits_in[:, :fields] * META_BASE + digits_in[:, fields:]
    meta_send, _ = lax.optimization_barrier((meta_layer, received[1]))
    meta_all = lax.all_to_all(
        jnp.broadcast_to(meta_send[None], (slab_count, *meta_send.shape)), "slab", 0, 0, tiled=True
    ).reshape(-1, fields)

    class_count = dest_map.shape[0]
    own_dest = lax.dynamic_slice_in_dim(dest_map, batch * rows, rows, 1).astype(jnp.bfloat16)
    own_freq = batch * rows + jnp.arange(rows, dtype=jnp.int32)

    def find_planes(table):
        class_hot = (table[:, :1] == jnp.arange(class_count)[None, :]).astype(jnp.bfloat16)
        local_plane = jnp.dot(class_hot, own_dest, preferred_element_type=jnp.float32)
        past = own_freq[None, :, None] >= table[:, None, 2:]
        return jnp.sum(past.astype(jnp.int32), axis=2), local_plane.astype(jnp.int32)

    mirrored = slab_count == 4 and batch_count % 2 == 0
    window_slabs = 3 if mirrored else slab_count
    owner, local_plane = find_planes(meta_layer)
    place = slab
    if mirrored:
        upper = batch >= batch_count // 2
        owner = jnp.where(upper, slab_count - 1 - owner, owner)
        place = jnp.where(upper, slab_count - 1 - slab, slab)
    codes = owner * (each * planes) + (jnp.arange(rows) % each)[None, :] * planes + local_plane
    codes = codes.reshape(batch_count * particles, CHUNKS, each).transpose(1, 0, 2)
    codes = codes.reshape(CHUNKS, batch_count, particles * each)

    owner, local_plane = find_planes(meta_all)
    focus_count = defocus.shape[0]
    focus_hot = (meta_all[:, 1:2] == jnp.arange(focus_count)[None, :]).astype(jnp.bfloat16)
    own_plane = jnp.where(owner == slab, local_plane, -1)
    bin_hot = (own_plane.T[:, None, :] == jnp.arange(planes)[None, :, None]).astype(jnp.bfloat16)
    counts = jnp.einsum("kzp,pd->kzd", bin_hot, focus_hot, preferred_element_type=jnp.float32)
    row_angle = 2.0 * (
        defocus[None, :] * centred_square(own_freq, length)[:, None] + PHASE_OFFSET
    )
    col_angle = 2.0 * (defocus[:, None] * centred_square(freq, length)[None, :])
    row_side = jnp.concatenate(
        [counts * jnp.cos(row_angle)[:, None, :], counts * jnp.sin(row_angle)[:, None, :]], axis=2
    )
    col_side = jnp.concatenate([jnp.cos(col_angle), -jnp.sin(col_angle)], axis=0)
    double = jnp.einsum("kzd,dx->kzx", row_side, col_side, precision=lax.Precision.HIGHEST)
    weights = 0.5 * (jnp.sum(counts, axis=2, keepdims=True) - double)
    denom = weights + TAU_PRIOR

    bins = each * planes
    sums = []
    for c in range(CHUNKS):
        rows_in = received[c].reshape(-1, 2 * length)
        codes_in = codes[c]
        if c == 0:
            codes_in = jnp.pad(codes_in, ((0, 0), (0, META_ROWS)), constant_values=-1)
        codes_in = codes_in.reshape(1, -1)
        if c > 0 and mirrored:
            codes_in, sums[-1] = lax.optimization_barrier((codes_in, sums[-1]))
        parts = pl.pallas_call(
            insert_kernel,
            out_shape=[jax.ShapeDtypeStruct((bins, 2 * length), jnp.bfloat16)] * window_slabs,
            in_specs=whole_vmem(2),
            out_specs=whole_vmem(window_slabs),
            compiler_params=pltpu.CompilerParams(vmem_limit_bytes=VMEM_LIMIT),
            cost_estimate=pl.CostEstimate(
                flops=2 * bins * window_slabs * rows_in.shape[0] * 2 * length,
                bytes_accessed=4 * 1024 * 1024,
                transcendentals=0,
            ),
            name="insert",
        )(rows_in, codes_in)
        if mirrored:
            sums.append(slab_sums(parts, place, slab_count, batch_count // 2))
        else:
            windows = jnp.stack(parts)
            sums.append(lax.psum_scatter(windows, "slab", scatter_dimension=0, tiled=False))
    updated = []
    for c in range(CHUNKS):
        here = slice(c * each, (c + 1) * each)
        prior = ref[here].astype(jnp.float32)
        under = denom[here]
        total = sums[c].astype(jnp.float32).reshape(each, planes, 2 * length)
        updated.append(
            (
                (TAU_PRIOR * prior + total) / jnp.concatenate([under, under], axis=2)
            ).astype(jnp.bfloat16)
        )
    return jnp.concatenate(updated, axis=0)


def solution(mesh):
    placed = (
        P(("batch", "slab"), None, None),
        P(("batch", "slab")),
        P(("batch", "slab"), None),
        P(("batch", "slab")),
        P(),
        P(("batch", "slab"), None),
        P(),
        P("batch", "slab", None),
    )
    return jax.shard_map(
        per_device, mesh=mesh, in_specs=placed, out_specs=P("batch", "slab", None), check_vma=False
    )
```

```python
import math

import jax
import jax.numpy as jnp
import numpy as np
from jax import lax
from jax.experimental import pallas as pl
from jax.experimental.pallas import tpu as pltpu
from jax.sharding import PartitionSpec as P

TAU_PRIOR = 4.0
PHASE_OFFSET = 0.1
CHUNKS = 3
META_BASE = 32
META_ROWS = 16
VMEM_LIMIT = 48 * 1024 * 1024


def dft_tables(length):
    index = np.arange(length, dtype=np.int32)
    turns = index[:, None] * index[None, :] % length
    angle = np.float32(2.0 * math.pi / length) * turns.astype(np.float32)
    factor = np.float32(1.0 / math.sqrt(length))
    cosine = np.cos(angle) * factor
    sine = np.sin(angle) * factor
    upper_rows = np.concatenate([cosine, -sine], axis=1)
    lower_rows = np.concatenate([sine, cosine], axis=1)
    table_right = np.concatenate([upper_rows, lower_rows], axis=0)
    return cosine, -sine, table_right


def spectrum_kernel(images, left, right, row_factors, col_factors, *rest):
    *meta, out, joined = rest
    particles, length = images.shape[0], images.shape[1]
    owners = out.shape[0]
    rows = row_factors.shape[0]
    rows_each = rows // owners
    for block in meta:
        for d in range(owners):
            out[d, particles * rows_each :, :] = block[...]
    table = left[...]
    for p in range(particles):
        section = jnp.dot(table, images[p], preferred_element_type=jnp.float32)
        section = section.astype(jnp.bfloat16)
        joined[p * rows : (p + 1) * rows, :length] = section[:rows]
        joined[p * rows : (p + 1) * rows, length:] = section[rows:]
    factors = row_factors[...]
    for first in range(0, particles, 2):
        spectrum = jnp.dot(
            joined[first * rows : (first + 2) * rows, :],
            right[...],
            preferred_element_type=jnp.float32,
        )
        for p in range(first, first + 2):
            part = spectrum[(p - first) * rows : (p - first + 1) * rows]
            real_part, imag_part = part[:, :length], part[:, length:]

            def row(q):
                at = q * particles + p
                return factors[:, at : at + 1]

            def col(q):
                at = q * particles + p
                return col_factors[at : at + 1, :]

            transfer = -(row(2) * col(3) + row(3) * col(2))
            cosine = transfer * (row(1) * col(1) - row(0) * col(0))
            sine = transfer * (row(0) * col(1) + row(1) * col(0))
            real_new = real_part * cosine + imag_part * sine
            imag_new = imag_part * cosine - real_part * sine
            weighted = jnp.concatenate([real_new, imag_new], axis=1).astype(jnp.bfloat16)
            out[:, p * rows_each : (p + 1) * rows_each, :] = weighted.reshape(
                owners, rows_each, 2 * length
            )


def insert_kernel(received, codes, out):
    windows, bins, _ = out.shape
    rows = received[...]
    codes_all = codes[...]
    for k in range(windows):
        bin_index = lax.broadcasted_iota(jnp.int32, (bins, 1), 0) + k * bins
        hot = jnp.where(codes_all == bin_index, 1.0, 0.0).astype(jnp.bfloat16)
        out[k] = jnp.dot(hot, rows, preferred_element_type=jnp.float32).astype(out.dtype)


def whole_vmem(count):
    return [pl.BlockSpec(memory_space=pltpu.VMEM)] * count


def lookup(values, indices):
    matches = indices[:, None] == jnp.arange(values.shape[0], dtype=jnp.int32)[None, :]
    return jnp.sum(jnp.where(matches, values[None, :], 0.0), axis=1)


def centred_square(freq, length):
    half_length = length // 2
    value = ((freq + half_length) % length - half_length).astype(jnp.float32) / length
    return value * value


def trig_factors(shift, focus, freq, offset, length, axis):
    if axis == 0:
        freq, shift, focus = freq[:, None], shift[None, :], focus[None, :]
    else:
        freq, shift, focus = freq[None, :], shift[:, None], focus[:, None]
    turns = (freq * shift) % length
    phase = 2.0 * math.pi / length * turns.astype(jnp.float32)
    angle = focus * centred_square(freq, length) + offset
    return jnp.concatenate(
        [jnp.sin(phase), jnp.cos(phase), jnp.sin(angle), jnp.cos(angle)], axis=1 - axis
    )


def slab_sums(parts, place, slab_count, mirror_count):
    def permute(block, pairs):
        perm = []
        for b in range(2 * mirror_count):
            for source, target in pairs:
                if b >= mirror_count:
                    source, target = slab_count - 1 - source, slab_count - 1 - target
                perm.append((b * slab_count + source, b * slab_count + target))
        return lax.ppermute(block, ("batch", "slab"), perm)

    near_in = permute(jnp.where(place == 2, parts[1], parts[0]), [(3, 2), (2, 1), (1, 0)])
    out_in = permute(jnp.where(place == 0, parts[1], parts[2]), [(0, 1), (1, 2)])
    merged = (parts[0].astype(jnp.float32) + near_in.astype(jnp.float32)).astype(jnp.bfloat16)
    far = jnp.where(place == 0, parts[2], jnp.where(place == 3, parts[1], merged))
    far, last = lax.optimization_barrier((far, parts[2]))
    far_in = permute(far, [(3, 1), (2, 0), (0, 2)])
    last_in = permute(last, [(3, 2)])
    own = jnp.where(place == 0, parts[0], jnp.where(place == 1, parts[1], parts[2]))
    total = jnp.where(place == 3, 0.0, own.astype(jnp.float32))
    total = total + jnp.where(place == 2, 0.0, near_in.astype(jnp.float32))
    total = total + out_in.astype(jnp.float32) + last_in.astype(jnp.float32)
    return total + far_in.astype(jnp.float32)


def per_device(images, classes, shifts, defocus_class, defocus, run_counts, dest_map, ref):
    particles, length, _ = images.shape
    batch_count = lax.axis_size("batch")
    slab_count = lax.axis_size("slab")
    batch = lax.axis_index("batch")
    slab = lax.axis_index("slab")
    rows, planes, _ = ref.shape
    each = rows // CHUNKS
    chunk_rows = batch_count * each
    freq = jnp.arange(length, dtype=jnp.int32)

    ends = jnp.cumsum(run_counts, axis=1)[:, : slab_count - 1]
    meta = jnp.concatenate([classes[:, None], defocus_class[:, None], ends], axis=1)
    fields = meta.shape[1]
    digits = jnp.concatenate([meta // META_BASE, meta % META_BASE], axis=1).astype(jnp.bfloat16)
    digits = jnp.pad(digits, ((0, META_ROWS - particles), (0, 2 * length - 2 * fields)))

    cosine, minus_sine, table_right = dft_tables(length)
    order = np.arange(length).reshape(batch_count, CHUNKS, each).transpose(1, 0, 2)
    order = order.reshape(CHUNKS, chunk_rows)
    table_right = jnp.asarray(table_right.astype(jnp.bfloat16))
    focus = lookup(defocus, defocus_class)
    row_factors = trig_factors(shifts[:, 1], focus, freq, PHASE_OFFSET, length, 0)
    col_factors = trig_factors(shifts[:, 0], focus, freq, 0.0, length, 1)
    row_factors = row_factors.reshape(batch_count, CHUNKS, each, 4 * particles)
    row_factors = row_factors.transpose(1, 0, 2, 3).reshape(CHUNKS, chunk_rows, 4 * particles)
    received = []
    for c in range(CHUNKS):
        left = np.concatenate([cosine[order[c]], minus_sine[order[c]]], axis=0)
        extra = (digits,) if c == 0 else ()
        block_rows = particles * each + META_ROWS * len(extra)
        weighted = pl.pallas_call(
            spectrum_kernel,
            out_shape=jax.ShapeDtypeStruct((batch_count, block_rows, 2 * length), jnp.bfloat16),
            in_specs=whole_vmem(5 + len(extra)),
            out_specs=pl.BlockSpec(memory_space=pltpu.VMEM),
            scratch_shapes=[pltpu.VMEM((particles * chunk_rows, 2 * length), jnp.bfloat16)],
            compiler_params=pltpu.CompilerParams(vmem_limit_bytes=VMEM_LIMIT),
            cost_estimate=pl.CostEstimate(
                flops=0,
                bytes_accessed=0,
                transcendentals=0,
            ),
            name="spectrum",
        )(
            images,
            jnp.asarray(left.astype(jnp.bfloat16)),
            table_right,
            row_factors[c],
            col_factors,
            *extra,
        )
        received.append(lax.all_to_all(weighted, "batch", 0, 0, tiled=True))

    digits_in = received[0][:, particles * each : particles * (each + 1), : 2 * fields]
    digits_in = digits_in.astype(jnp.int32).reshape(-1, 2 * fields)
    meta_layer = digits_in[:, :fields] * META_BASE + digits_in[:, fields:]
    meta_all = [meta_layer]
    for step in range(1, slab_count):
        ring = [(s, (s + step) % slab_count) for s in range(slab_count)]
        meta_all.append(lax.ppermute(meta_layer, "slab", ring))
    meta_all = jnp.concatenate(meta_all, axis=0)

    class_count = dest_map.shape[0]
    own_dest = lax.dynamic_slice_in_dim(dest_map, batch * rows, rows, 1).astype(jnp.bfloat16)
    own_freq = batch * rows + jnp.arange(rows, dtype=jnp.int32)

    def find_planes(table):
        class_hot = (table[:, :1] == jnp.arange(class_count)[None, :]).astype(jnp.bfloat16)
        local_plane = jnp.dot(class_hot, own_dest, preferred_element_type=jnp.float32)
        past = own_freq[None, :, None] >= table[:, None, 2:]
        return jnp.sum(past.astype(jnp.int32), axis=2), local_plane.astype(jnp.int32)

    mirrored = False
    window_slabs = 3 if mirrored else slab_count
    owner, local_plane = find_planes(meta_layer)
    place = slab
    if mirrored:
        upper = batch >= batch_count // 2
        owner = jnp.where(upper, slab_count - 1 - owner, owner)
        place = jnp.where(upper, slab_count - 1 - slab, slab)
    codes = owner * (each * planes) + (jnp.arange(rows) % each)[None, :] * planes + local_plane
    codes = codes.reshape(batch_count * particles, CHUNKS, each).transpose(1, 0, 2)
    codes = codes.reshape(CHUNKS, batch_count, particles * each)

    owner, local_plane = find_planes(meta_all)
    focus_count = defocus.shape[0]
    focus_hot = (meta_all[:, 1:2] == jnp.arange(focus_count)[None, :]).astype(jnp.bfloat16)
    own_plane = jnp.where(owner == slab, local_plane, -1)
    bin_hot = (own_plane.T[:, None, :] == jnp.arange(planes)[None, :, None]).astype(jnp.bfloat16)
    counts = jnp.einsum("kzp,pd->kzd", bin_hot, focus_hot, preferred_element_type=jnp.float32)
    row_angle = 2.0 * (
        defocus[None, :] * centred_square(own_freq, length)[:, None] + PHASE_OFFSET
    )
    col_angle = 2.0 * (defocus[:, None] * centred_square(freq, length)[None, :])
    row_side = jnp.concatenate(
        [counts * jnp.cos(row_angle)[:, None, :], counts * jnp.sin(row_angle)[:, None, :]], axis=2
    )
    col_side = jnp.concatenate([jnp.cos(col_angle), -jnp.sin(col_angle)], axis=0)
    double = jnp.einsum("kzd,dx->kzx", row_side, col_side, precision=lax.Precision.HIGHEST)
    weights = 0.5 * (jnp.sum(counts, axis=2, keepdims=True) - double)
    denom = weights + TAU_PRIOR

    bins = each * planes
    sums = []
    for c in range(CHUNKS):
        rows_in = received[c].reshape(-1, 2 * length)
        codes_in = codes[c]
        if c == 0:
            codes_in = jnp.pad(codes_in, ((0, 0), (0, META_ROWS)), constant_values=-1)
        codes_in = codes_in.reshape(1, -1)
        if c > 0 and mirrored:
            codes_in, sums[-1] = lax.optimization_barrier((codes_in, sums[-1]))
        parts = pl.pallas_call(
            insert_kernel,
            out_shape=jax.ShapeDtypeStruct((window_slabs, bins, 2 * length), jnp.bfloat16),
            in_specs=whole_vmem(2),
            out_specs=pl.BlockSpec(memory_space=pltpu.VMEM),
            compiler_params=pltpu.CompilerParams(vmem_limit_bytes=VMEM_LIMIT),
            cost_estimate=pl.CostEstimate(
                flops=0,
                bytes_accessed=0,
                transcendentals=0,
            ),
            name="insert",
        )(rows_in, codes_in)
        if mirrored:
            sums.append(slab_sums(parts, place, slab_count, batch_count // 2))
        else:
            sums.append(lax.psum_scatter(parts, "slab", scatter_dimension=0, tiled=False))
    updated = []
    for c in range(CHUNKS):
        here = slice(c * each, (c + 1) * each)
        prior = ref[here].astype(jnp.float32)
        under = denom[here]
        total = sums[c].astype(jnp.float32).reshape(each, planes, 2 * length)
        updated.append(
            (
                (TAU_PRIOR * prior + total) / jnp.concatenate([under, under], axis=2)
            ).astype(jnp.bfloat16)
        )
    return jnp.concatenate(updated, axis=0)


def solution(mesh):
    placed = (
        P(("batch", "slab"), None, None),
        P(("batch", "slab")),
        P(("batch", "slab"), None),
        P(("batch", "slab")),
        P(),
        P(("batch", "slab"), None),
        P(),
        P("batch", "slab", None),
    )
    return jax.shard_map(
        per_device, mesh=mesh, in_specs=placed, out_specs=P("batch", "slab", None), check_vma=False
    )
```

```python
import math

import jax
import jax.numpy as jnp
import numpy as np
from jax import lax
from jax.experimental import pallas as pl
from jax.experimental.pallas import tpu as pltpu
from jax.sharding import PartitionSpec as P

TAU_PRIOR = 4.0
PHASE_OFFSET = 0.1
CHUNKS = ((2, False), (2, True), (2, False))
SHARES = 6
META_BASE = 32
META_ROWS = 16
VMEM_LIMIT = 48 * 1024 * 1024


def dft_tables(length):
    index = np.arange(length, dtype=np.int32)
    turns = index[:, None] * index[None, :] % length
    angle = np.float32(2.0 * math.pi / length) * turns.astype(np.float32)
    factor = np.float32(1.0 / math.sqrt(length))
    cosine = np.cos(angle) * factor
    sine = np.sin(angle) * factor
    upper_rows = np.concatenate([cosine, -sine], axis=1)
    lower_rows = np.concatenate([sine, cosine], axis=1)
    table_right = np.concatenate([upper_rows, lower_rows], axis=0)
    return cosine, -sine, table_right


def spectrum_kernel(images, left, right, row_factors, col_factors, *rest):
    *meta, out, joined = rest
    particles, length = images.shape[0], images.shape[1]
    owners = out.shape[0]
    rows = row_factors.shape[0]
    rows_each = rows // owners
    for block in meta:
        for d in range(owners):
            out[d, particles * rows_each :, :] = block[...]
    table = left[...]
    for p in range(particles):
        section = jnp.dot(table, images[p], preferred_element_type=jnp.float32)
        section = section.astype(jnp.bfloat16)
        joined[p * rows : (p + 1) * rows, :length] = section[:rows]
        joined[p * rows : (p + 1) * rows, length:] = section[rows:]
    factors = row_factors[...]
    for first in range(0, particles, 2):
        spectrum = jnp.dot(
            joined[first * rows : (first + 2) * rows, :],
            right[...],
            preferred_element_type=jnp.float32,
        )
        for p in range(first, first + 2):
            part = spectrum[(p - first) * rows : (p - first + 1) * rows]
            real_part, imag_part = part[:, :length], part[:, length:]

            def row(q):
                at = q * particles + p
                return factors[:, at : at + 1]

            def col(q):
                at = q * particles + p
                return col_factors[at : at + 1, :]

            transfer = -(row(2) * col(3) + row(3) * col(2))
            cosine = transfer * (row(1) * col(1) - row(0) * col(0))
            sine = transfer * (row(0) * col(1) + row(1) * col(0))
            real_new = real_part * cosine + imag_part * sine
            imag_new = imag_part * cosine - real_part * sine
            weighted = jnp.concatenate([real_new, imag_new], axis=1).astype(jnp.bfloat16)
            out[:, p * rows_each : (p + 1) * rows_each, :] = weighted.reshape(
                owners, rows_each, 2 * length
            )


def insert_kernel(received, codes, out):
    windows, bins, _ = out.shape
    rows = received[...]
    codes_all = codes[...]
    for k in range(windows):
        bin_index = lax.broadcasted_iota(jnp.int32, (bins, 1), 0) + k * bins
        hot = jnp.where(codes_all == bin_index, 1.0, 0.0).astype(jnp.bfloat16)
        out[k] = jnp.dot(hot, rows, preferred_element_type=jnp.float32).astype(out.dtype)


def whole_vmem(count):
    return [pl.BlockSpec(memory_space=pltpu.VMEM)] * count


def lookup(values, indices):
    matches = indices[:, None] == jnp.arange(values.shape[0], dtype=jnp.int32)[None, :]
    return jnp.sum(jnp.where(matches, values[None, :], 0.0), axis=1)


def centred_square(freq, length):
    half_length = length // 2
    value = ((freq + half_length) % length - half_length).astype(jnp.float32) / length
    return value * value


def trig_factors(shift, focus, freq, offset, length, axis):
    if axis == 0:
        freq, shift, focus = freq[:, None], shift[None, :], focus[None, :]
    else:
        freq, shift, focus = freq[None, :], shift[:, None], focus[:, None]
    turns = (freq * shift) % length
    phase = 2.0 * math.pi / length * turns.astype(jnp.float32)
    angle = focus * centred_square(freq, length) + offset
    return jnp.concatenate(
        [jnp.sin(phase), jnp.cos(phase), jnp.sin(angle), jnp.cos(angle)], axis=1 - axis
    )


def slab_sums(parts, place, slab_count, batch_count, swapped):
    total = jnp.where(place == 3, 0.0, choose(parts, place).astype(jnp.float32))
    for shift in range(1, slab_count):
        perm = []
        for b in range(batch_count):
            upper = (b >= batch_count // 2) != swapped
            for source in range(slab_count):
                target = (source + shift) % slab_count
                if target < slab_count - 1:
                    ends = (slab_count - 1 - source, slab_count - 1 - target)
                    ends = ends if upper else (source, target)
                    perm.append((b * slab_count + ends[0], b * slab_count + ends[1]))
        block = choose(parts, (place + shift) % slab_count)
        total = total + lax.ppermute(block, ("batch", "slab"), perm).astype(jnp.float32)
    return total


def choose(parts, index):
    chosen = parts[-1]
    for d in range(parts.shape[0] - 1):
        chosen = jnp.where(index == d, parts[d], chosen)
    return chosen


def per_device(images, classes, shifts, defocus_class, defocus, run_counts, dest_map, ref):
    particles, length, _ = images.shape
    batch_count = lax.axis_size("batch")
    slab_count = lax.axis_size("slab")
    batch = lax.axis_index("batch")
    slab = lax.axis_index("slab")
    rows, planes, _ = ref.shape
    mirrored = slab_count == 4 and batch_count % 2 == 0
    half_batch = batch_count // 2
    sizes = [rows * share // SHARES for share, _ in CHUNKS]
    starts = [sum(sizes[:c]) for c in range(len(CHUNKS))]
    swaps = [mirrored and swapped for _, swapped in CHUNKS]
    freq = jnp.arange(length, dtype=jnp.int32)

    ends = jnp.cumsum(run_counts, axis=1)[:, : slab_count - 1]
    meta = jnp.concatenate([classes[:, None], defocus_class[:, None], ends], axis=1)
    fields = meta.shape[1]
    digits = jnp.concatenate([meta // META_BASE, meta % META_BASE], axis=1).astype(jnp.bfloat16)
    digits = jnp.pad(digits, ((0, META_ROWS - particles), (0, 2 * length - 2 * fields)))

    cosine, minus_sine, table_right = dft_tables(length)
    table_right = jnp.asarray(table_right.astype(jnp.bfloat16))
    focus = lookup(defocus, defocus_class)
    row_factors = trig_factors(shifts[:, 1], focus, freq, PHASE_OFFSET, length, 0)
    col_factors = trig_factors(shifts[:, 0], focus, freq, 0.0, length, 1)
    row_factors = row_factors.reshape(batch_count, rows, 4 * particles)
    received = []
    weighted = []
    for c, each in enumerate(sizes):
        chunk_rows = batch_count * each
        block = np.roll(np.arange(batch_count), -half_batch if swaps[c] else 0)
        order = (block[:, None] * rows + starts[c] + np.arange(each)[None, :]).reshape(-1)
        left = np.concatenate([cosine[order], minus_sine[order]], axis=0)
        factors = row_factors[:, starts[c] : starts[c] + each]
        if swaps[c]:
            factors = jnp.concatenate([factors[half_batch:], factors[:half_batch]], axis=0)
        factors = factors.reshape(chunk_rows, 4 * particles)
        extra = (digits,) if c == 0 else ()
        block_rows = particles * each + META_ROWS * len(extra)
        send = pl.pallas_call(
            spectrum_kernel,
            out_shape=jax.ShapeDtypeStruct((batch_count, block_rows, 2 * length), jnp.bfloat16),
            in_specs=whole_vmem(5 + len(extra)),
            out_specs=pl.BlockSpec(memory_space=pltpu.VMEM),
            scratch_shapes=[pltpu.VMEM((particles * chunk_rows, 2 * length), jnp.bfloat16)],
            compiler_params=pltpu.CompilerParams(vmem_limit_bytes=VMEM_LIMIT),
            cost_estimate=pl.CostEstimate(
                flops=2 * particles * chunk_rows * 2 * length * 3 * length,
                bytes_accessed=6 * 1024 * 1024,
                transcendentals=0,
            ),
            name="spectrum",
        )(
            images,
            jnp.asarray(left.astype(jnp.bfloat16)),
            table_right,
            factors,
            col_factors,
            *extra,
        )
        weighted.append(send)
        received.append(lax.all_to_all(send, "batch", 0, 0, tiled=True))

    digits_in = received[0][:, particles * sizes[0] : particles * (sizes[0] + 1), : 2 * fields]
    digits_in = digits_in.astype(jnp.int32).reshape(-1, 2 * fields)
    meta_layer = digits_in[:, :fields] * META_BASE + digits_in[:, fields:]
    meta_all = [meta_layer]
    for step in range(1, slab_count):
        ring = [(s, (s + step) % slab_count) for s in range(slab_count)]
        meta_all.append(lax.ppermute(meta_layer, "slab", ring))
    meta_all = jnp.concatenate(meta_all, axis=0)

    class_count = dest_map.shape[0]

    def find_planes(table, dest, freq_in):
        class_hot = (table[:, :1] == jnp.arange(class_count)[None, :]).astype(jnp.bfloat16)
        local_plane = jnp.dot(
            class_hot, dest.astype(jnp.bfloat16), preferred_element_type=jnp.float32
        )
        past = freq_in[None, :, None] >= table[:, None, 2:]
        return jnp.sum(past.astype(jnp.int32), axis=2), local_plane.astype(jnp.int32)

    window_slabs = 3 if mirrored else slab_count
    blocks = [(batch + half_batch) % batch_count if swap else batch for swap in swaps]
    begins = [block * rows + start for block, start in zip(blocks, starts)]
    dest_in = jnp.concatenate(
        [lax.dynamic_slice_in_dim(dest_map, at, n, 1) for at, n in zip(begins, sizes)], axis=1
    )
    freq_in = jnp.concatenate(
        [at + jnp.arange(n, dtype=jnp.int32) for at, n in zip(begins, sizes)]
    )
    owner, local_plane = find_planes(meta_layer, dest_in, freq_in)
    places, codes = [], []
    for c, each in enumerate(sizes):
        here = slice(starts[c], starts[c] + each)
        place, owner_place = slab, owner[:, here]
        if mirrored:
            upper = blocks[c] >= half_batch
            owner_place = jnp.where(upper, slab_count - 1 - owner_place, owner_place)
            place = jnp.where(upper, slab_count - 1 - slab, slab)
        places.append(place)
        code = owner_place * (each * planes) + jnp.arange(each)[None, :] * planes
        code = (code + local_plane[:, here]).reshape(batch_count, particles * each)
        if c == 0:
            code = jnp.pad(code, ((0, 0), (0, META_ROWS)), constant_values=-1)
        codes.append(code.reshape(1, -1))

    own_freq = batch * rows + jnp.arange(rows, dtype=jnp.int32)
    own_dest = lax.dynamic_slice_in_dim(dest_map, batch * rows, rows, 1)
    owner, local_plane = find_planes(meta_all, own_dest, own_freq)
    focus_count = defocus.shape[0]
    focus_hot = (meta_all[:, 1:2] == jnp.arange(focus_count)[None, :]).astype(jnp.bfloat16)
    own_plane = jnp.where(owner == slab, local_plane, -1)
    bin_hot = (own_plane.T[:, None, :] == jnp.arange(planes)[None, :, None]).astype(jnp.bfloat16)
    counts = jnp.einsum("kzp,pd->kzd", bin_hot, focus_hot, preferred_element_type=jnp.float32)
    row_angle = 2.0 * (
        defocus[None, :] * centred_square(own_freq, length)[:, None] + PHASE_OFFSET
    )
    col_angle = 2.0 * (defocus[:, None] * centred_square(freq, length)[None, :])
    row_side = jnp.concatenate(
        [counts * jnp.cos(row_angle)[:, None, :], counts * jnp.sin(row_angle)[:, None, :]], axis=2
    )
    col_side = jnp.concatenate([jnp.cos(col_angle), -jnp.sin(col_angle)], axis=0)
    double = jnp.einsum("kzd,dx->kzx", row_side, col_side, precision=lax.Precision.HIGHEST)
    weights = 0.5 * (jnp.sum(counts, axis=2, keepdims=True) - double)
    denom = weights + TAU_PRIOR

    sums = []
    for c, each in enumerate(sizes):
        bins = each * planes
        rows_in = received[c].reshape(-1, 2 * length)
        codes_in = codes[c]
        if c + 1 < len(sizes):
            codes_in, _ = lax.optimization_barrier((codes_in, weighted[c + 1]))
        if c > 1:
            codes_in, sums[c - 2] = lax.optimization_barrier((codes_in, sums[c - 2]))
        parts = pl.pallas_call(
            insert_kernel,
            out_shape=jax.ShapeDtypeStruct((window_slabs, bins, 2 * length), jnp.bfloat16),
            in_specs=whole_vmem(2),
            out_specs=pl.BlockSpec(memory_space=pltpu.VMEM),
            compiler_params=pltpu.CompilerParams(vmem_limit_bytes=VMEM_LIMIT),
            cost_estimate=pl.CostEstimate(
                flops=2 * bins * window_slabs * rows_in.shape[0] * 2 * length,
                bytes_accessed=4 * 1024 * 1024,
                transcendentals=0,
            ),
            name="insert",
        )(rows_in, codes_in)
        if mirrored:
            total = slab_sums(parts, places[c], slab_count, batch_count, swaps[c])
            if swaps[c]:
                over = [(b, (b + half_batch) % batch_count) for b in range(batch_count)]
                total = lax.ppermute(total.astype(jnp.bfloat16), "batch", over)
            sums.append(total)
        else:
            sums.append(lax.psum_scatter(parts, "slab", scatter_dimension=0, tiled=False))
    updated = []
    for c, each in enumerate(sizes):
        here = slice(starts[c], starts[c] + each)
        prior = ref[here].astype(jnp.float32)
        under = denom[here]
        total = sums[c].astype(jnp.float32).reshape(each, planes, 2 * length)
        updated.append(
            (
                (TAU_PRIOR * prior + total) / jnp.concatenate([under, under], axis=2)
            ).astype(jnp.bfloat16)
        )
    return jnp.concatenate(updated, axis=0)


def solution(mesh):
    placed = (
        P(("batch", "slab"), None, None),
        P(("batch", "slab")),
        P(("batch", "slab"), None),
        P(("batch", "slab")),
        P(),
        P(("batch", "slab"), None),
        P(),
        P("batch", "slab", None),
    )
    return jax.shard_map(
        per_device, mesh=mesh, in_specs=placed, out_specs=P("batch", "slab", None), check_vma=False
    )
```

```python
import functools
import math

import jax
import jax.numpy as jnp
import numpy as np
from jax import lax
from jax.experimental import pallas as pl
from jax.experimental.pallas import tpu as pltpu
from jax.sharding import PartitionSpec as P

TAU_PRIOR = 4.0
PHASE_OFFSET = 0.1
CHUNKS = ((2, False), (2, True), (2, False))
SHARES = 6
META_BASE = 32
META_ROWS = 16
LANES = 128
VMEM_LIMIT = 48 * 1024 * 1024


def dft_tables(length):
    index = np.arange(length, dtype=np.int32)
    turns = index[:, None] * index[None, :] % length
    angle = np.float32(2.0 * math.pi / length) * turns.astype(np.float32)
    factor = np.float32(1.0 / math.sqrt(length))
    cosine = np.cos(angle) * factor
    sine = np.sin(angle) * factor
    upper_rows = np.concatenate([cosine, -sine], axis=1)
    lower_rows = np.concatenate([sine, cosine], axis=1)
    table_right = np.concatenate([upper_rows, lower_rows], axis=0)
    return cosine, -sine, table_right


def spectrum_kernel(runs, images, left, right, row_factors, col_factors, *rest):
    *meta, out, joined = rest
    particles, length = images.shape[0], images.shape[1]
    owners = out.shape[0]
    rows_each = runs[0][1] - runs[0][0]
    rows = owners * rows_each
    for block in meta:
        for d in range(owners):
            out[d, particles * rows_each :, :] = block[...]
    table = left[...]
    for p in range(particles):
        section = jnp.dot(table, images[p], preferred_element_type=jnp.float32)
        section = section.astype(jnp.bfloat16)
        joined[p * rows : (p + 1) * rows, :length] = section[:rows]
        joined[p * rows : (p + 1) * rows, length:] = section[rows:]
    factors = jnp.concatenate([row_factors[begin:end, :] for begin, end in runs], axis=0)
    for first in range(0, particles, 2):
        spectrum = jnp.dot(
            joined[first * rows : (first + 2) * rows, :],
            right[...],
            preferred_element_type=jnp.float32,
        )
        for p in range(first, first + 2):
            part = spectrum[(p - first) * rows : (p - first + 1) * rows]
            real_part, imag_part = part[:, :length], part[:, length:]

            def row(q):
                at = q * particles + p
                return factors[:, at : at + 1]

            def col(q):
                at = q * particles + p
                return col_factors[at : at + 1, :]

            transfer = -(row(2) * col(3) + row(3) * col(2))
            cosine = transfer * (row(1) * col(1) - row(0) * col(0))
            sine = transfer * (row(0) * col(1) + row(1) * col(0))
            real_new = real_part * cosine + imag_part * sine
            imag_new = imag_part * cosine - real_part * sine
            weighted = jnp.concatenate([real_new, imag_new], axis=1).astype(jnp.bfloat16)
            out[:, p * rows_each : (p + 1) * rows_each, :] = weighted.reshape(
                owners, rows_each, 2 * length
            )


def insert_kernel(bins, meta_at, received, codes, out):
    sources = received.shape[0]
    rows = received[...].reshape(-1, received.shape[2])
    codes_all = codes[...]
    for k in range(out.shape[0]):
        bin_index = lax.broadcasted_iota(jnp.int32, (bins, 1), 0) + k * bins
        hot = jnp.where(codes_all == bin_index, 1.0, 0.0).astype(jnp.bfloat16)
        total = jnp.dot(hot, rows, preferred_element_type=jnp.float32)
        out[k, :bins, :] = total.astype(out.dtype)
        if out.shape[1] > bins:
            tiles = out.shape[2] // LANES
            first_half = lax.broadcasted_iota(jnp.int32, (META_ROWS, LANES), 0) < META_ROWS // 2
            for i in range(min(sources, tiles)):
                low = received[i, meta_at : meta_at + META_ROWS, :LANES]
                if i + tiles < sources:
                    high = received[i + tiles, meta_at : meta_at + META_ROWS, :LANES]
                    low = jnp.where(
                        first_half, low.astype(jnp.float32), high.astype(jnp.float32)
                    ).astype(low.dtype)
                out[k, bins:, i * LANES : (i + 1) * LANES] = low


def whole_vmem(count):
    return [pl.BlockSpec(memory_space=pltpu.VMEM)] * count


def lookup(values, indices):
    matches = indices[:, None] == jnp.arange(values.shape[0], dtype=jnp.int32)[None, :]
    return jnp.sum(jnp.where(matches, values[None, :], 0.0), axis=1)


def centred_square(freq, length):
    half_length = length // 2
    value = ((freq + half_length) % length - half_length).astype(jnp.float32) / length
    return value * value


def trig_factors(shift, focus, freq, offset, length, axis):
    if axis == 0:
        freq, shift, focus = freq[:, None], shift[None, :], focus[None, :]
    else:
        freq, shift, focus = freq[None, :], shift[:, None], focus[:, None]
    turns = (freq * shift) % length
    phase = 2.0 * math.pi / length * turns.astype(jnp.float32)
    angle = focus * centred_square(freq, length) + offset
    return jnp.concatenate(
        [jnp.sin(phase), jnp.cos(phase), jnp.sin(angle), jnp.cos(angle)], axis=1 - axis
    )


def slab_exchange(parts, place, slab_count, batch_count, swapped):
    arrived = []
    for shift in range(1, slab_count):
        perm = []
        for b in range(batch_count):
            upper = (b >= batch_count // 2) != swapped
            for source in range(slab_count):
                target = (source + shift) % slab_count
                if target < slab_count - 1:
                    ends = (slab_count - 1 - source, slab_count - 1 - target)
                    ends = ends if upper else (source, target)
                    perm.append((b * slab_count + ends[0], b * slab_count + ends[1]))
        block = choose(parts, (place + shift) % slab_count)
        arrived.append(lax.ppermute(block, ("batch", "slab"), perm))
    return arrived


def choose(parts, index):
    chosen = parts[-1]
    for d in range(parts.shape[0] - 1):
        chosen = jnp.where(index == d, parts[d], chosen)
    return chosen


def per_device(images, classes, shifts, defocus_class, defocus, run_counts, dest_map, ref):
    particles, length, _ = images.shape
    batch_count = lax.axis_size("batch")
    slab_count = lax.axis_size("slab")
    batch = lax.axis_index("batch")
    slab = lax.axis_index("slab")
    rows, planes, _ = ref.shape
    mirrored = slab_count == 4 and batch_count % 2 == 0 and 2 * particles <= META_ROWS
    mirrored = mirrored and batch_count * LANES <= 4 * length
    half_batch = batch_count // 2
    sizes = [rows * share // SHARES for share, _ in CHUNKS]
    starts = [sum(sizes[:c]) for c in range(len(CHUNKS))]
    swaps = [mirrored and swapped for _, swapped in CHUNKS]
    freq = jnp.arange(length, dtype=jnp.int32)

    ends = jnp.cumsum(run_counts, axis=1)[:, : slab_count - 1]
    meta = jnp.concatenate([classes[:, None], defocus_class[:, None], ends], axis=1)
    fields = meta.shape[1]
    digits = jnp.concatenate([meta // META_BASE, meta % META_BASE], axis=1).astype(jnp.bfloat16)
    digits = jnp.concatenate([digits] * (META_ROWS // particles), axis=0)
    digits = jnp.pad(digits, ((0, META_ROWS - len(digits)), (0, 2 * length - 2 * fields)))

    cosine, minus_sine, table_right = dft_tables(length)
    table_right = jnp.asarray(table_right.astype(jnp.bfloat16))
    focus = lookup(defocus, defocus_class)
    row_factors = trig_factors(shifts[:, 1], focus, freq, PHASE_OFFSET, length, 0)
    col_factors = trig_factors(shifts[:, 0], focus, freq, 0.0, length, 1)
    received = []
    weighted = []
    for c, each in enumerate(sizes):
        chunk_rows = batch_count * each
        block = np.roll(np.arange(batch_count), -half_batch if swaps[c] else 0)
        order = (block[:, None] * rows + starts[c] + np.arange(each)[None, :]).reshape(-1)
        left = np.concatenate([cosine[order], minus_sine[order]], axis=0)
        runs = [(k * rows + starts[c], k * rows + starts[c] + each) for k in block.tolist()]
        extra = (digits,) if c == 0 else ()
        block_rows = particles * each + META_ROWS * len(extra)
        send = pl.pallas_call(
            functools.partial(spectrum_kernel, runs),
            out_shape=jax.ShapeDtypeStruct((batch_count, block_rows, 2 * length), jnp.bfloat16),
            in_specs=whole_vmem(5 + len(extra)),
            out_specs=pl.BlockSpec(memory_space=pltpu.VMEM),
            scratch_shapes=[pltpu.VMEM((particles * chunk_rows, 2 * length), jnp.bfloat16)],
            compiler_params=pltpu.CompilerParams(vmem_limit_bytes=VMEM_LIMIT),
            cost_estimate=pl.CostEstimate(
                flops=0,
                bytes_accessed=0,
                transcendentals=0,
            ),
            name="spectrum",
        )(
            images,
            jnp.asarray(left.astype(jnp.bfloat16)),
            table_right,
            row_factors,
            col_factors,
            *extra,
        )
        weighted.append(send)
        received.append(lax.all_to_all(send, "batch", 0, 0, tiled=True))

    def read_digits(rows_in):
        whole = rows_in.astype(jnp.int32).reshape(-1, 2 * fields)
        return whole[:, :fields] * META_BASE + whole[:, fields:]

    meta_at = particles * sizes[0]
    meta_layer = read_digits(received[0][:, meta_at : meta_at + particles, : 2 * fields])

    class_count = dest_map.shape[0]

    def find_planes(table, dest, freq_in):
        class_hot = (table[:, :1] == jnp.arange(class_count)[None, :]).astype(jnp.bfloat16)
        local_plane = jnp.dot(
            class_hot, dest.astype(jnp.bfloat16), preferred_element_type=jnp.float32
        )
        past = freq_in[None, :, None] >= table[:, None, 2:]
        return jnp.sum(past.astype(jnp.int32), axis=2), local_plane.astype(jnp.int32)

    window_slabs = 3 if mirrored else slab_count
    blocks = [(batch + half_batch) % batch_count if swap else batch for swap in swaps]
    begins = [block * rows + start for block, start in zip(blocks, starts)]
    dest_in = jnp.concatenate(
        [lax.dynamic_slice_in_dim(dest_map, at, n, 1) for at, n in zip(begins, sizes)], axis=1
    )
    freq_in = jnp.concatenate(
        [at + jnp.arange(n, dtype=jnp.int32) for at, n in zip(begins, sizes)]
    )
    owner, local_plane = find_planes(meta_layer, dest_in, freq_in)
    places, codes = [], []
    for c, each in enumerate(sizes):
        here = slice(starts[c], starts[c] + each)
        place, owner_place = slab, owner[:, here]
        if mirrored:
            upper = blocks[c] >= half_batch
            owner_place = jnp.where(upper, slab_count - 1 - owner_place, owner_place)
            place = jnp.where(upper, slab_count - 1 - slab, slab)
        places.append(place)
        code = owner_place * (each * planes) + jnp.arange(each)[None, :] * planes
        code = (code + local_plane[:, here]).reshape(batch_count, particles * each)
        if c == 0:
            code = jnp.pad(code, ((0, 0), (0, META_ROWS)), constant_values=-1)
        codes.append(code.reshape(1, -1))

    sums = []
    for c, each in enumerate(sizes):
        bins = each * planes
        extra_rows = META_ROWS if c == 0 and mirrored else 0
        codes_in = codes[c]
        if c + 1 < len(sizes):
            codes_in, _ = lax.optimization_barrier((codes_in, weighted[c + 1]))
        if c > 0:
            codes_in, parts = lax.optimization_barrier((codes_in, parts))
        parts = pl.pallas_call(
            functools.partial(insert_kernel, bins, meta_at),
            out_shape=jax.ShapeDtypeStruct(
                (window_slabs, bins + extra_rows, 2 * length), jnp.bfloat16
            ),
            in_specs=whole_vmem(2),
            out_specs=pl.BlockSpec(memory_space=pltpu.VMEM),
            compiler_params=pltpu.CompilerParams(vmem_limit_bytes=VMEM_LIMIT),
            cost_estimate=pl.CostEstimate(
                flops=0,
                bytes_accessed=0,
                transcendentals=0,
            ),
            name="insert",
        )(received[c], codes_in)
        if not mirrored:
            sums.append(lax.psum_scatter(parts, "slab", scatter_dimension=0, tiled=False))
            continue
        arrived = slab_exchange(parts, places[c], slab_count, batch_count, swaps[c])
        total = choose(parts[:, :bins], places[c]).astype(jnp.float32)
        total = jnp.where(places[c] == slab_count - 1, 0.0, total)
        for block in arrived:
            total = total + block[:bins].astype(jnp.float32)
        if swaps[c]:
            over = [(b, (b + half_batch) % batch_count) for b in range(batch_count)]
            total = lax.ppermute(total.astype(jnp.bfloat16), "batch", over)
        sums.append(total)
        if c == 0:
            meta_in = [block[bins:].reshape(META_ROWS, -1, LANES) for block in arrived]

    meta_all = [meta_layer]
    if mirrored:
        for block in meta_in:
            halves = (block[:particles], block[particles : 2 * particles])
            low = jnp.concatenate(halves, axis=1)[:, :batch_count, : 2 * fields]
            meta_all.append(read_digits(low.transpose(1, 0, 2)))
    else:
        for step in range(1, slab_count):
            ring = [(s, (s + step) % slab_count) for s in range(slab_count)]
            meta_all.append(lax.ppermute(meta_layer, "slab", ring))
    meta_all = jnp.concatenate(meta_all, axis=0)

    own_freq = batch * rows + jnp.arange(rows, dtype=jnp.int32)
    own_dest = lax.dynamic_slice_in_dim(dest_map, batch * rows, rows, 1)
    owner, local_plane = find_planes(meta_all, own_dest, own_freq)
    focus_count = defocus.shape[0]
    focus_hot = (meta_all[:, 1:2] == jnp.arange(focus_count)[None, :]).astype(jnp.bfloat16)
    own_plane = jnp.where(owner == slab, local_plane, -1)
    if mirrored:
        own_plane = jnp.where(places[0] == slab_count - 1, -1, own_plane)
    bin_hot = (own_plane.T[:, None, :] == jnp.arange(planes)[None, :, None]).astype(jnp.bfloat16)
    counts = jnp.einsum("kzp,pd->kzd", bin_hot, focus_hot, preferred_element_type=jnp.float32)
    row_angle = 2.0 * (
        defocus[None, :] * centred_square(own_freq, length)[:, None] + PHASE_OFFSET
    )
    col_angle = 2.0 * (defocus[:, None] * centred_square(freq, length)[None, :])
    row_side = jnp.concatenate(
        [counts * jnp.cos(row_angle)[:, None, :], counts * jnp.sin(row_angle)[:, None, :]], axis=2
    )
    col_side = jnp.concatenate([jnp.cos(col_angle), -jnp.sin(col_angle)], axis=0)
    double = jnp.einsum("kzd,dx->kzx", row_side, col_side, precision=lax.Precision.HIGHEST)
    weights = 0.5 * (jnp.sum(counts, axis=2, keepdims=True) - double)
    denom = weights + TAU_PRIOR

    updated = []
    for c, each in enumerate(sizes):
        here = slice(starts[c], starts[c] + each)
        prior = ref[here].astype(jnp.float32)
        under = denom[here]
        total = sums[c].astype(jnp.float32).reshape(each, planes, 2 * length)
        updated.append(
            (
                (TAU_PRIOR * prior + total) / jnp.concatenate([under, under], axis=2)
            ).astype(jnp.bfloat16)
        )
    return jnp.concatenate(updated, axis=0)


def solution(mesh):
    placed = (
        P(("batch", "slab"), None, None),
        P(("batch", "slab")),
        P(("batch", "slab"), None),
        P(("batch", "slab")),
        P(),
        P(("batch", "slab"), None),
        P(),
        P("batch", "slab", None),
    )
    return jax.shard_map(
        per_device, mesh=mesh, in_specs=placed, out_specs=P("batch", "slab", None), check_vma=False
    )
```

```python
import functools
import math

import jax
import jax.numpy as jnp
import numpy as np
from jax import lax
from jax.experimental import pallas as pl
from jax.experimental.pallas import tpu as pltpu
from jax.sharding import PartitionSpec as P

TAU_PRIOR = 4.0
PHASE_OFFSET = 0.1
CHUNKS = ((2, False), (2, True), (2, False))
SHARES = 6
META_BASE = 32
META_ROWS = 16
LANES = 128
VMEM_LIMIT = 48 * 1024 * 1024


def dft_tables(length):
    index = np.arange(length, dtype=np.int32)
    turns = index[:, None] * index[None, :] % length
    angle = np.float32(2.0 * math.pi / length) * turns.astype(np.float32)
    factor = np.float32(1.0 / math.sqrt(length))
    cosine = np.cos(angle) * factor
    sine = np.sin(angle) * factor
    upper_rows = np.concatenate([cosine, -sine], axis=1)
    lower_rows = np.concatenate([sine, cosine], axis=1)
    table_right = np.concatenate([upper_rows, lower_rows], axis=0)
    return cosine, -sine, table_right


def spectrum_kernel(runs, images, left, right, row_factors, col_factors, *rest):
    *meta, out, joined = rest
    particles, length = images.shape[0], images.shape[1]
    owners = out.shape[0]
    rows_each = runs[0][1] - runs[0][0]
    rows = owners * rows_each
    for block in meta:
        for d in range(owners):
            out[d, particles * rows_each :, :] = block[...]
    table = left[...]
    for p in range(particles):
        section = jnp.dot(table, images[p], preferred_element_type=jnp.float32)
        section = section.astype(jnp.bfloat16)
        joined[p * rows : (p + 1) * rows, :length] = section[:rows]
        joined[p * rows : (p + 1) * rows, length:] = section[rows:]
    factors = jnp.concatenate([row_factors[begin:end, :] for begin, end in runs], axis=0)
    for first in range(0, particles, 2):
        spectrum = jnp.dot(
            joined[first * rows : (first + 2) * rows, :],
            right[...],
            preferred_element_type=jnp.float32,
        )
        for p in range(first, first + 2):
            part = spectrum[(p - first) * rows : (p - first + 1) * rows]
            real_part, imag_part = part[:, :length], part[:, length:]

            def row(q):
                at = q * particles + p
                return factors[:, at : at + 1]

            def col(q):
                at = q * particles + p
                return col_factors[at : at + 1, :]

            transfer = -(row(2) * col(3) + row(3) * col(2))
            cosine = transfer * (row(1) * col(1) - row(0) * col(0))
            sine = transfer * (row(0) * col(1) + row(1) * col(0))
            real_new = real_part * cosine + imag_part * sine
            imag_new = imag_part * cosine - real_part * sine
            weighted = jnp.concatenate([real_new, imag_new], axis=1).astype(jnp.bfloat16)
            out[:, p * rows_each : (p + 1) * rows_each, :] = weighted.reshape(
                owners, rows_each, 2 * length
            )


def insert_kernel(bins, meta_at, received, codes, out):
    sources = received.shape[0]
    rows = received[...].reshape(-1, received.shape[2])
    codes_all = codes[...]
    for k in range(out.shape[0]):
        bin_index = lax.broadcasted_iota(jnp.int32, (bins, 1), 0) + k * bins
        hot = jnp.where(codes_all == bin_index, 1.0, 0.0).astype(jnp.bfloat16)
        total = jnp.dot(hot, rows, preferred_element_type=jnp.float32)
        out[k, :bins, :] = total.astype(out.dtype)
        if out.shape[1] > bins:
            tiles = out.shape[2] // LANES
            first_half = lax.broadcasted_iota(jnp.int32, (META_ROWS, LANES), 0) < META_ROWS // 2
            for i in range(min(sources, tiles)):
                low = received[i, meta_at : meta_at + META_ROWS, :LANES]
                if i + tiles < sources:
                    high = received[i + tiles, meta_at : meta_at + META_ROWS, :LANES]
                    low = jnp.where(
                        first_half, low.astype(jnp.float32), high.astype(jnp.float32)
                    ).astype(low.dtype)
                out[k, bins:, i * LANES : (i + 1) * LANES] = low


def whole_vmem(count):
    return [pl.BlockSpec(memory_space=pltpu.VMEM)] * count


def lookup(values, indices):
    matches = indices[:, None] == jnp.arange(values.shape[0], dtype=jnp.int32)[None, :]
    return jnp.sum(jnp.where(matches, values[None, :], 0.0), axis=1)


def centred_square(freq, length):
    half_length = length // 2
    value = ((freq + half_length) % length - half_length).astype(jnp.float32) / length
    return value * value


def trig_factors(shift, focus, freq, offset, length, axis):
    if axis == 0:
        freq, shift, focus = freq[:, None], shift[None, :], focus[None, :]
    else:
        freq, shift, focus = freq[None, :], shift[:, None], focus[:, None]
    turns = (freq * shift) % length
    phase = 2.0 * math.pi / length * turns.astype(jnp.float32)
    angle = focus * centred_square(freq, length) + offset
    return jnp.concatenate(
        [jnp.sin(phase), jnp.cos(phase), jnp.sin(angle), jnp.cos(angle)], axis=1 - axis
    )


def slab_exchange(parts, place, slab_count, batch_count, swapped):
    arrived = []
    for shift in range(1, slab_count):
        perm = []
        for b in range(batch_count):
            upper = (b >= batch_count // 2) != swapped
            for source in range(slab_count):
                target = (source + shift) % slab_count
                if target < slab_count - 1:
                    ends = (slab_count - 1 - source, slab_count - 1 - target)
                    ends = ends if upper else (source, target)
                    perm.append((b * slab_count + ends[0], b * slab_count + ends[1]))
        block = choose(parts, (place + shift) % slab_count)
        arrived.append(lax.ppermute(block, ("batch", "slab"), perm))
    return arrived


def choose(parts, index):
    chosen = parts[-1]
    for d in range(parts.shape[0] - 1):
        chosen = jnp.where(index == d, parts[d], chosen)
    return chosen


def per_device(images, classes, shifts, defocus_class, defocus, run_counts, dest_map, ref):
    particles, length, _ = images.shape
    batch_count = lax.axis_size("batch")
    slab_count = lax.axis_size("slab")
    batch = lax.axis_index("batch")
    slab = lax.axis_index("slab")
    rows, planes, _ = ref.shape
    mirrored = slab_count == 4 and batch_count % 2 == 0 and 2 * particles <= META_ROWS
    mirrored = mirrored and batch_count * LANES <= 4 * length
    half_batch = batch_count // 2
    sizes = [rows * share // SHARES for share, _ in CHUNKS]
    starts = [sum(sizes[:c]) for c in range(len(CHUNKS))]
    swaps = [mirrored and swapped for _, swapped in CHUNKS]
    freq = jnp.arange(length, dtype=jnp.int32)

    ends = jnp.cumsum(run_counts, axis=1)[:, : slab_count - 1]
    meta = jnp.concatenate([classes[:, None], defocus_class[:, None], ends], axis=1)
    fields = meta.shape[1]
    digits = jnp.concatenate([meta // META_BASE, meta % META_BASE], axis=1).astype(jnp.bfloat16)
    digits = jnp.concatenate([digits] * (META_ROWS // particles), axis=0)
    digits = jnp.pad(digits, ((0, META_ROWS - len(digits)), (0, 2 * length - 2 * fields)))

    cosine, minus_sine, table_right = dft_tables(length)
    table_right = jnp.asarray(table_right.astype(jnp.bfloat16))
    focus = lookup(defocus, defocus_class)
    row_factors = trig_factors(shifts[:, 1], focus, freq, PHASE_OFFSET, length, 0)
    col_factors = trig_factors(shifts[:, 0], focus, freq, 0.0, length, 1)
    received = []
    weighted = []
    for c, each in enumerate(sizes):
        chunk_rows = batch_count * each
        block = np.roll(np.arange(batch_count), -half_batch if swaps[c] else 0)
        order = (block[:, None] * rows + starts[c] + np.arange(each)[None, :]).reshape(-1)
        left = np.concatenate([cosine[order], minus_sine[order]], axis=0)
        runs = [(k * rows + starts[c], k * rows + starts[c] + each) for k in block.tolist()]
        extra = (digits,) if c == 0 else ()
        block_rows = particles * each + META_ROWS * len(extra)
        send = pl.pallas_call(
            functools.partial(spectrum_kernel, runs),
            out_shape=jax.ShapeDtypeStruct((batch_count, block_rows, 2 * length), jnp.bfloat16),
            in_specs=whole_vmem(5 + len(extra)),
            out_specs=pl.BlockSpec(memory_space=pltpu.VMEM),
            scratch_shapes=[pltpu.VMEM((particles * chunk_rows, 2 * length), jnp.bfloat16)],
            compiler_params=pltpu.CompilerParams(vmem_limit_bytes=VMEM_LIMIT),
            cost_estimate=pl.CostEstimate(
                flops=0,
                bytes_accessed=0,
                transcendentals=0,
            ),
            name="spectrum",
        )(
            images,
            jnp.asarray(left.astype(jnp.bfloat16)),
            table_right,
            row_factors,
            col_factors,
            *extra,
        )
        weighted.append(send)
        received.append(lax.all_to_all(send, "batch", 0, 0, tiled=True))

    def read_digits(rows_in):
        whole = rows_in.astype(jnp.int32).reshape(-1, 2 * fields)
        return whole[:, :fields] * META_BASE + whole[:, fields:]

    meta_at = particles * sizes[0]
    meta_layer = read_digits(received[0][:, meta_at : meta_at + particles, : 2 * fields])

    class_count = dest_map.shape[0]

    dest_wide = dest_map.astype(jnp.bfloat16)

    def find_planes(table):
        class_hot = (table[:, :1] == jnp.arange(class_count)[None, :]).astype(jnp.bfloat16)
        local_plane = jnp.dot(class_hot, dest_wide, preferred_element_type=jnp.float32)
        past = freq[None, :, None] >= table[:, None, 2:]
        owner = jnp.sum(past.astype(jnp.int32), axis=2)
        return owner * planes + local_plane.astype(jnp.int32)

    def pick_block(table, block):
        return sum(
            jnp.where(block == k, table[:, k * rows : (k + 1) * rows], 0)
            for k in range(batch_count)
        )

    window_slabs = 3 if mirrored else slab_count
    blocks = [(batch + half_batch) % batch_count if swap else batch for swap in swaps]
    layer_planes = find_planes(meta_layer)
    places, codes = [], []
    for c, each in enumerate(sizes):
        here = slice(starts[c], starts[c] + each)
        plane = pick_block(layer_planes, blocks[c])[:, here]
        place, owner_place = slab, plane // planes
        if mirrored:
            upper = blocks[c] >= half_batch
            owner_place = jnp.where(upper, slab_count - 1 - owner_place, owner_place)
            place = jnp.where(upper, slab_count - 1 - slab, slab)
        places.append(place)
        code = owner_place * (each * planes) + jnp.arange(each)[None, :] * planes
        code = (code + plane % planes).reshape(batch_count, particles * each)
        if c == 0:
            code = jnp.pad(code, ((0, 0), (0, META_ROWS)), constant_values=-1)
        codes.append(code.reshape(1, -1))

    sums, arrived = [], []
    for c, each in enumerate(sizes):
        bins = each * planes
        extra_rows = META_ROWS if c == 0 and mirrored else 0
        codes_in = codes[c]
        if c + 1 < len(sizes):
            codes_in, _ = lax.optimization_barrier((codes_in, weighted[c + 1]))
        if c > 0 and mirrored:
            near = [arrived[c - 1][0], arrived[c - 1][2]]
            codes_in, *near = lax.optimization_barrier((codes_in, *near))
            arrived[c - 1][0], arrived[c - 1][2] = near[:2]
        parts = pl.pallas_call(
            functools.partial(insert_kernel, bins, meta_at),
            out_shape=jax.ShapeDtypeStruct(
                (window_slabs, bins + extra_rows, 2 * length), jnp.bfloat16
            ),
            in_specs=whole_vmem(2),
            out_specs=pl.BlockSpec(memory_space=pltpu.VMEM),
            compiler_params=pltpu.CompilerParams(vmem_limit_bytes=VMEM_LIMIT),
            cost_estimate=pl.CostEstimate(
                flops=0,
                bytes_accessed=0,
                transcendentals=0,
            ),
            name="insert",
        )(received[c], codes_in)
        if not mirrored:
            sums.append(lax.psum_scatter(parts, "slab", scatter_dimension=0, tiled=False))
            continue
        for before in arrived:
            before[1], _ = lax.optimization_barrier((before[1], parts))
        arrived.append(slab_exchange(parts, places[c], slab_count, batch_count, swaps[c]))
        own = choose(parts[:, :bins], places[c]).astype(jnp.float32)
        sums.append(jnp.where(places[c] == slab_count - 1, 0.0, own))
    for c, each in enumerate(sizes):
        if not mirrored:
            break
        for block in arrived[c]:
            sums[c] = sums[c] + block[: each * planes].astype(jnp.float32)
        if swaps[c]:
            over = [(b, (b + half_batch) % batch_count) for b in range(batch_count)]
            sums[c] = lax.ppermute(sums[c].astype(jnp.bfloat16), "batch", over)

    meta_all = [meta_layer]
    if mirrored:
        for block in [block[sizes[0] * planes :] for block in arrived[0]]:
            block = block.reshape(META_ROWS, -1, LANES)
            halves = (block[:particles], block[particles : 2 * particles])
            low = jnp.concatenate(halves, axis=1)[:, :batch_count, : 2 * fields]
            meta_all.append(read_digits(low.transpose(1, 0, 2)))
    else:
        for step in range(1, slab_count):
            ring = [(s, (s + step) % slab_count) for s in range(slab_count)]
            meta_all.append(lax.ppermute(meta_layer, "slab", ring))
    meta_all = jnp.concatenate(meta_all, axis=0)

    own_freq = batch * rows + jnp.arange(rows, dtype=jnp.int32)
    own_plane = pick_block(find_planes(meta_all), batch) - slab * planes
    focus_count = defocus.shape[0]
    focus_hot = (meta_all[:, 1:2] == jnp.arange(focus_count)[None, :]).astype(jnp.bfloat16)
    if mirrored:
        own_plane = jnp.where(places[0] == slab_count - 1, -1, own_plane)
    bin_hot = (own_plane.T[:, None, :] == jnp.arange(planes)[None, :, None]).astype(jnp.bfloat16)
    counts = jnp.einsum("kzp,pd->kzd", bin_hot, focus_hot, preferred_element_type=jnp.float32)
    row_angle = 2.0 * (
        defocus[None, :] * centred_square(own_freq, length)[:, None] + PHASE_OFFSET
    )
    col_angle = 2.0 * (defocus[:, None] * centred_square(freq, length)[None, :])
    row_side = jnp.concatenate(
        [counts * jnp.cos(row_angle)[:, None, :], counts * jnp.sin(row_angle)[:, None, :]], axis=2
    )
    col_side = jnp.concatenate([jnp.cos(col_angle), -jnp.sin(col_angle)], axis=0)
    double = jnp.einsum("kzd,dx->kzx", row_side, col_side, precision=lax.Precision.HIGHEST)
    weights = 0.5 * (jnp.sum(counts, axis=2, keepdims=True) - double)
    denom = weights + TAU_PRIOR

    updated = []
    for c, each in enumerate(sizes):
        here = slice(starts[c], starts[c] + each)
        prior = ref[here].astype(jnp.float32)
        under = denom[here]
        total = sums[c].astype(jnp.float32).reshape(each, planes, 2 * length)
        updated.append(
            (
                (TAU_PRIOR * prior + total) / jnp.concatenate([under, under], axis=2)
            ).astype(jnp.bfloat16)
        )
    return jnp.concatenate(updated, axis=0)


def solution(mesh):
    placed = (
        P(("batch", "slab"), None, None),
        P(("batch", "slab")),
        P(("batch", "slab"), None),
        P(("batch", "slab")),
        P(),
        P(("batch", "slab"), None),
        P(),
        P("batch", "slab", None),
    )
    return jax.shard_map(
        per_device, mesh=mesh, in_specs=placed, out_specs=P("batch", "slab", None), check_vma=False
    )
```

```python
import functools
import math

import jax
import jax.numpy as jnp
import numpy as np
from jax import lax
from jax.experimental import pallas as pl
from jax.experimental.pallas import tpu as pltpu
from jax.sharding import PartitionSpec as P

TAU_PRIOR = 4.0
PHASE_OFFSET = 0.1
CHUNKS = ((2, False), (2, True), (2, False))
SHARES = 6
META_BASE = 32
META_ROWS = 16
LANES = 128
VMEM_LIMIT = 48 * 1024 * 1024


def dft_tables(length):
    index = np.arange(length, dtype=np.int32)
    turns = index[:, None] * index[None, :] % length
    angle = np.float32(2.0 * math.pi / length) * turns.astype(np.float32)
    factor = np.float32(1.0 / math.sqrt(length))
    cosine = np.cos(angle) * factor
    sine = np.sin(angle) * factor
    upper_rows = np.concatenate([cosine, -sine], axis=1)
    lower_rows = np.concatenate([sine, cosine], axis=1)
    table_right = np.concatenate([upper_rows, lower_rows], axis=0)
    return cosine, -sine, table_right


def spread(iota, values):
    out = jnp.full(iota.shape, values[0])
    for p in range(1, len(values)):
        out = jnp.where(iota == p, values[p], out)
    return out


def phase_angle(freq, shift, length):
    turns = freq * shift
    turns = turns - length * jnp.floor(turns * (1.0 / length))
    return (2.0 * math.pi / length) * turns


def centred(freq, length):
    return jnp.where(freq < length // 2, freq, freq - length) * (1.0 / length)


def spectrum_kernel(
    runs,
    with_meta,
    classes,
    shifts,
    defocus_class,
    defocus,
    run_counts,
    images_in,
    left_in,
    right_in,
    out,
    images,
    left,
    right,
    joined,
    block,
    load_sems,
    send_sem,
):
    particles, length = images.shape[0], images.shape[1]
    owners = out.shape[0]
    rows_each = runs[0][1] - runs[0][0]
    rows = owners * rows_each
    loads = [pltpu.make_async_copy(left_in, left, load_sems.at[0])]
    for p in range(particles):
        loads.append(pltpu.make_async_copy(images_in.at[p], images.at[p], load_sems.at[1 + p]))
    loads.append(pltpu.make_async_copy(right_in, right, load_sems.at[1 + particles]))
    for load in loads:
        load.start()

    every = range(particles)
    focus = [defocus[defocus_class[p]] for p in every]
    shift_x = [shifts[p, 0].astype(jnp.float32) for p in every]
    shift_y = [shifts[p, 1].astype(jnp.float32) for p in every]
    sublane = lax.broadcasted_iota(jnp.int32, (particles, length), 0)
    freq_x = lax.broadcasted_iota(jnp.int32, (particles, length), 1).astype(jnp.float32)
    phase_x = phase_angle(freq_x, spread(sublane, shift_x), length)
    angle_x = spread(sublane, focus) * centred(freq_x, length) * centred(freq_x, length)
    col = [jnp.sin(phase_x), jnp.cos(phase_x), jnp.sin(angle_x), jnp.cos(angle_x)]
    lane = lax.broadcasted_iota(jnp.int32, (rows, LANES), 1)
    which = lane % particles
    quantity = lane // particles
    row_at = lax.broadcasted_iota(jnp.int32, (rows, LANES), 0)
    owner = row_at // rows_each
    freq_y = row_at - owner * rows_each + spread(owner, [begin for begin, _ in runs])
    freq_y = freq_y.astype(jnp.float32)
    phase_y = phase_angle(freq_y, spread(which, shift_y), length)
    angle_y = spread(which, focus) * centred(freq_y, length) * centred(freq_y, length)
    angles = jnp.where(quantity < 2, phase_y, angle_y + PHASE_OFFSET)
    row = jnp.sin(angles + jnp.where(quantity % 2 == 1, 0.5 * math.pi, 0.0))

    if with_meta:
        digits = jnp.zeros((META_ROWS, LANES), jnp.int32)
        at_row = lax.broadcasted_iota(jnp.int32, (META_ROWS, LANES), 0) % particles
        at_lane = lax.broadcasted_iota(jnp.int32, (META_ROWS, LANES), 1)
        ends = [[run_counts[p, 0] for p in every]]
        for s in range(1, run_counts.shape[1] - 1):
            ends.append([ends[-1][p] + run_counts[p, s] for p in every])
        fields = [[classes[p] for p in every], [defocus_class[p] for p in every], *ends]
        for f, values in enumerate(fields):
            value = spread(at_row, values)
            digits = jnp.where(at_lane == f, value // META_BASE, digits)
            digits = jnp.where(at_lane == f + len(fields), value % META_BASE, digits)
        digits = digits.astype(jnp.float32).astype(jnp.bfloat16)
        for d in range(owners):
            block[d, particles * rows_each :, :] = jnp.zeros(
                (META_ROWS, 2 * length), jnp.bfloat16
            )
            block[d, particles * rows_each :, :LANES] = digits

    loads[0].wait()
    table = left[...]
    for p in range(particles):
        loads[1 + p].wait()
        section = jnp.dot(table, images[p], preferred_element_type=jnp.float32)
        section = section.astype(jnp.bfloat16)
        joined[p * rows : (p + 1) * rows, :length] = section[:rows]
        joined[p * rows : (p + 1) * rows, length:] = section[rows:]
    loads[1 + particles].wait()
    for first in range(0, particles, 2):
        spectrum = jnp.dot(
            joined[first * rows : (first + 2) * rows, :],
            right[...],
            preferred_element_type=jnp.float32,
        )
        for p in range(first, first + 2):
            part = spectrum[(p - first) * rows : (p - first + 1) * rows]
            real_part, imag_part = part[:, :length], part[:, length:]
            row_sin, row_cos, row_ctf_sin, row_ctf_cos = [
                row[:, q * particles + p : q * particles + p + 1] for q in range(4)
            ]
            col_sin, col_cos, col_ctf_sin, col_ctf_cos = [part[p : p + 1, :] for part in col]
            transfer = -(row_ctf_sin * col_ctf_cos + row_ctf_cos * col_ctf_sin)
            cosine = transfer * (row_cos * col_cos - row_sin * col_sin)
            sine = transfer * (row_sin * col_cos + row_cos * col_sin)
            real_new = real_part * cosine + imag_part * sine
            imag_new = imag_part * cosine - real_part * sine
            weighted = jnp.concatenate([real_new, imag_new], axis=1).astype(jnp.bfloat16)
            block[:, p * rows_each : (p + 1) * rows_each, :] = weighted.reshape(
                owners, rows_each, 2 * length
            )
    send = pltpu.make_async_copy(block, out, send_sem)
    send.start()
    send.wait()


def insert_kernel(bins, meta_at, received, codes, out):
    sources = received.shape[0]
    rows = received[...].reshape(-1, received.shape[2])
    codes_all = codes[...]
    for k in range(out.shape[0]):
        bin_index = lax.broadcasted_iota(jnp.int32, (bins, 1), 0) + k * bins
        hot = jnp.where(codes_all == bin_index, 1.0, 0.0).astype(jnp.bfloat16)
        total = jnp.dot(hot, rows, preferred_element_type=jnp.float32)
        out[k, :bins, :] = total.astype(out.dtype)
        if out.shape[1] > bins:
            tiles = out.shape[2] // LANES
            first_half = lax.broadcasted_iota(jnp.int32, (META_ROWS, LANES), 0) < META_ROWS // 2
            for i in range(min(sources, tiles)):
                low = received[i, meta_at : meta_at + META_ROWS, :LANES]
                if i + tiles < sources:
                    high = received[i + tiles, meta_at : meta_at + META_ROWS, :LANES]
                    low = jnp.where(
                        first_half, low.astype(jnp.float32), high.astype(jnp.float32)
                    ).astype(low.dtype)
                out[k, bins:, i * LANES : (i + 1) * LANES] = low


def whole_vmem(count):
    return [pl.BlockSpec(memory_space=pltpu.VMEM)] * count


def centred_square(freq, length):
    half_length = length // 2
    value = ((freq + half_length) % length - half_length).astype(jnp.float32) / length
    return value * value


def slab_exchange(parts, place, slab_count, batch_count, swapped):
    arrived = []
    for shift in range(1, slab_count):
        perm = []
        for b in range(batch_count):
            upper = (b >= batch_count // 2) != swapped
            for source in range(slab_count):
                target = (source + shift) % slab_count
                if target < slab_count - 1:
                    ends = (slab_count - 1 - source, slab_count - 1 - target)
                    ends = ends if upper else (source, target)
                    perm.append((b * slab_count + ends[0], b * slab_count + ends[1]))
        block = choose(parts, (place + shift) % slab_count)
        arrived.append(lax.ppermute(block, ("batch", "slab"), perm))
    return arrived


def choose(parts, index):
    chosen = parts[-1]
    for d in range(parts.shape[0] - 1):
        chosen = jnp.where(index == d, parts[d], chosen)
    return chosen


def per_device(images, classes, shifts, defocus_class, defocus, run_counts, dest_map, ref):
    particles, length, _ = images.shape
    batch_count = lax.axis_size("batch")
    slab_count = lax.axis_size("slab")
    batch = lax.axis_index("batch")
    slab = lax.axis_index("slab")
    rows, planes, _ = ref.shape
    mirrored = slab_count == 4 and batch_count % 2 == 0 and 2 * particles <= META_ROWS
    mirrored = mirrored and batch_count * LANES <= 4 * length
    half_batch = batch_count // 2
    sizes = [rows * share // SHARES for share, _ in CHUNKS]
    starts = [sum(sizes[:c]) for c in range(len(CHUNKS))]
    swaps = [mirrored and swapped for _, swapped in CHUNKS]
    freq = jnp.arange(length, dtype=jnp.int32)

    fields = slab_count + 1

    cosine, minus_sine, table_right = dft_tables(length)
    table_right = jnp.asarray(table_right.astype(jnp.bfloat16))
    received = []
    weighted = []
    for c, each in enumerate(sizes):
        chunk_rows = batch_count * each
        block = np.roll(np.arange(batch_count), -half_batch if swaps[c] else 0)
        order = (block[:, None] * rows + starts[c] + np.arange(each)[None, :]).reshape(-1)
        left = np.concatenate([cosine[order], minus_sine[order]], axis=0)
        runs = [(k * rows + starts[c], k * rows + starts[c] + each) for k in block.tolist()]
        with_meta = c == 0
        block_rows = particles * each + META_ROWS * with_meta
        block_shape = (batch_count, block_rows, 2 * length)
        smem = pl.BlockSpec(memory_space=pltpu.SMEM)
        hbm = pl.BlockSpec(memory_space=pltpu.HBM)
        send = pl.pallas_call(
            functools.partial(spectrum_kernel, runs, with_meta),
            out_shape=jax.ShapeDtypeStruct(block_shape, jnp.bfloat16),
            in_specs=[smem] * 5 + [hbm] * 3,
            out_specs=hbm,
            scratch_shapes=[
                pltpu.VMEM((particles, length, length), jnp.bfloat16),
                pltpu.VMEM((2 * chunk_rows, length), jnp.bfloat16),
                pltpu.VMEM((2 * length, 2 * length), jnp.bfloat16),
                pltpu.VMEM((particles * chunk_rows, 2 * length), jnp.bfloat16),
                pltpu.VMEM(block_shape, jnp.bfloat16),
                pltpu.SemaphoreType.DMA((particles + 2,)),
                pltpu.SemaphoreType.DMA,
            ],
            compiler_params=pltpu.CompilerParams(vmem_limit_bytes=VMEM_LIMIT),
            cost_estimate=pl.CostEstimate(flops=0, bytes_accessed=0, transcendentals=0),
            name="spectrum",
        )(
            classes,
            shifts,
            defocus_class,
            defocus,
            run_counts,
            images,
            jnp.asarray(left.astype(jnp.bfloat16)),
            table_right,
        )
        weighted.append(send)
        received.append(lax.all_to_all(send, "batch", 0, 0, tiled=True))

    def read_digits(rows_in):
        whole = rows_in.astype(jnp.int32).reshape(-1, 2 * fields)
        return whole[:, :fields] * META_BASE + whole[:, fields:]

    meta_at = particles * sizes[0]
    meta_layer = read_digits(received[0][:, meta_at : meta_at + particles, : 2 * fields])

    class_count = dest_map.shape[0]

    dest_wide = dest_map.astype(jnp.bfloat16)

    def find_planes(table):
        class_hot = (table[:, :1] == jnp.arange(class_count)[None, :]).astype(jnp.bfloat16)
        local_plane = jnp.dot(class_hot, dest_wide, preferred_element_type=jnp.float32)
        past = freq[None, :, None] >= table[:, None, 2:]
        owner = jnp.sum(past.astype(jnp.int32), axis=2)
        return owner * planes + local_plane.astype(jnp.int32)

    def pick_block(table, block):
        return sum(
            jnp.where(block == k, table[:, k * rows : (k + 1) * rows], 0)
            for k in range(batch_count)
        )

    window_slabs = 3 if mirrored else slab_count
    blocks = [(batch + half_batch) % batch_count if swap else batch for swap in swaps]
    layer_planes = find_planes(meta_layer)
    places, codes = [], []
    for c, each in enumerate(sizes):
        here = slice(starts[c], starts[c] + each)
        plane = pick_block(layer_planes, blocks[c])[:, here]
        place, owner_place = slab, plane // planes
        if mirrored:
            upper = blocks[c] >= half_batch
            owner_place = jnp.where(upper, slab_count - 1 - owner_place, owner_place)
            place = jnp.where(upper, slab_count - 1 - slab, slab)
        places.append(place)
        code = owner_place * (each * planes) + jnp.arange(each)[None, :] * planes
        code = (code + plane % planes).reshape(batch_count, particles * each)
        if c == 0:
            code = jnp.pad(code, ((0, 0), (0, META_ROWS)), constant_values=-1)
        codes.append(code.reshape(1, -1))

    sums, arrived = [], []
    for c, each in enumerate(sizes):
        bins = each * planes
        extra_rows = META_ROWS if c == 0 and mirrored else 0
        codes_in = codes[c]
        if c + 1 < len(sizes):
            codes_in, _ = lax.optimization_barrier((codes_in, weighted[c + 1]))
        if c > 0 and mirrored:
            codes_in, arrived[c - 1][2] = lax.optimization_barrier((codes_in, arrived[c - 1][2]))
        parts = pl.pallas_call(
            functools.partial(insert_kernel, bins, meta_at),
            out_shape=jax.ShapeDtypeStruct(
                (window_slabs, bins + extra_rows, 2 * length), jnp.bfloat16
            ),
            in_specs=whole_vmem(2),
            out_specs=pl.BlockSpec(memory_space=pltpu.VMEM),
            compiler_params=pltpu.CompilerParams(vmem_limit_bytes=VMEM_LIMIT),
            cost_estimate=pl.CostEstimate(
                flops=0,
                bytes_accessed=0,
                transcendentals=0,
            ),
            name="insert",
        )(received[c], codes_in)
        if not mirrored:
            sums.append(lax.psum_scatter(parts, "slab", scatter_dimension=0, tiled=False))
            continue
        for before in arrived:
            before[1], _ = lax.optimization_barrier((before[1], parts))
        arrived.append(slab_exchange(parts, places[c], slab_count, batch_count, swaps[c]))
        own = choose(parts[:, :bins], places[c]).astype(jnp.float32)
        sums.append(jnp.where(places[c] == slab_count - 1, 0.0, own))
    for c, each in enumerate(sizes):
        if not mirrored:
            break
        for block in arrived[c]:
            sums[c] = sums[c] + block[: each * planes].astype(jnp.float32)
        if swaps[c]:
            if c + 1 < len(sizes):
                sums[c], arrived[-1][0] = lax.optimization_barrier((sums[c], arrived[-1][0]))
            over = [(b, (b + half_batch) % batch_count) for b in range(batch_count)]
            sums[c] = lax.ppermute(sums[c].astype(jnp.bfloat16), "batch", over)

    meta_all = [meta_layer]
    if mirrored:
        for block in [block[sizes[0] * planes :] for block in arrived[0]]:
            block = block.reshape(META_ROWS, -1, LANES)
            halves = (block[:particles], block[particles : 2 * particles])
            low = jnp.concatenate(halves, axis=1)[:, :batch_count, : 2 * fields]
            meta_all.append(read_digits(low.transpose(1, 0, 2)))
    else:
        for step in range(1, slab_count):
            ring = [(s, (s + step) % slab_count) for s in range(slab_count)]
            meta_all.append(lax.ppermute(meta_layer, "slab", ring))
    meta_all = jnp.concatenate(meta_all, axis=0)

    own_freq = batch * rows + jnp.arange(rows, dtype=jnp.int32)
    own_plane = pick_block(find_planes(meta_all), batch) - slab * planes
    focus_count = defocus.shape[0]
    focus_hot = (meta_all[:, 1:2] == jnp.arange(focus_count)[None, :]).astype(jnp.bfloat16)
    if mirrored:
        own_plane = jnp.where(places[0] == slab_count - 1, -1, own_plane)
    bin_hot = (own_plane.T[:, None, :] == jnp.arange(planes)[None, :, None]).astype(jnp.bfloat16)
    counts = jnp.einsum("kzp,pd->kzd", bin_hot, focus_hot, preferred_element_type=jnp.float32)
    row_angle = 2.0 * (
        defocus[None, :] * centred_square(own_freq, length)[:, None] + PHASE_OFFSET
    )
    col_angle = 2.0 * (defocus[:, None] * centred_square(freq, length)[None, :])
    row_side = jnp.concatenate(
        [counts * jnp.cos(row_angle)[:, None, :], counts * jnp.sin(row_angle)[:, None, :]], axis=2
    )
    col_side = jnp.concatenate([jnp.cos(col_angle), -jnp.sin(col_angle)], axis=0)
    double = jnp.einsum("kzd,dx->kzx", row_side, col_side, precision=lax.Precision.HIGHEST)
    weights = 0.5 * (jnp.sum(counts, axis=2, keepdims=True) - double)
    denom = weights + TAU_PRIOR

    updated = []
    for c, each in enumerate(sizes):
        here = slice(starts[c], starts[c] + each)
        prior = ref[here].astype(jnp.float32)
        under = denom[here]
        total = sums[c].astype(jnp.float32).reshape(each, planes, 2 * length)
        updated.append(
            (
                (TAU_PRIOR * prior + total) / jnp.concatenate([under, under], axis=2)
            ).astype(jnp.bfloat16)
        )
    return jnp.concatenate(updated, axis=0)


def solution(mesh):
    placed = (
        P(("batch", "slab"), None, None),
        P(("batch", "slab")),
        P(("batch", "slab"), None),
        P(("batch", "slab")),
        P(),
        P(("batch", "slab"), None),
        P(),
        P("batch", "slab", None),
    )
    return jax.shard_map(
        per_device, mesh=mesh, in_specs=placed, out_specs=P("batch", "slab", None), check_vma=False
    )
```

```python
import functools
import math

import jax
import jax.numpy as jnp
import numpy as np
from jax import lax
from jax.experimental import pallas as pl
from jax.experimental.pallas import tpu as pltpu
from jax.sharding import PartitionSpec as P

TAU_PRIOR = 4.0
PHASE_OFFSET = 0.1
CHUNKS = ((2, False), (2, True), (2, False))
SHARES = 6
META_BASE = 32
META_ROWS = 16
LANES = 128
SPECTRUM_VMEM = 60 * 1024 * 1024
INSERT_VMEM = 32 * 1024 * 1024


def dft_tables(length):
    index = np.arange(length, dtype=np.int32)
    turns = index[:, None] * index[None, :] % length
    angle = np.float32(2.0 * math.pi / length) * turns.astype(np.float32)
    factor = np.float32(1.0 / math.sqrt(length))
    cosine = np.cos(angle) * factor
    sine = np.sin(angle) * factor
    upper_rows = np.concatenate([cosine, -sine], axis=1)
    lower_rows = np.concatenate([sine, cosine], axis=1)
    table_right = np.concatenate([upper_rows, lower_rows], axis=0)
    return cosine, -sine, table_right


def spread(iota, values):
    out = jnp.full(iota.shape, values[0])
    for p in range(1, len(values)):
        out = jnp.where(iota == p, values[p], out)
    return out


def sin_turns(turns):
    half = jnp.floor(2.0 * turns + 0.5)
    x = (2.0 * math.pi) * (turns - 0.5 * half)
    sign = 1.0 - 2.0 * (half - 2.0 * jnp.floor(0.5 * half))
    square = x * x
    series = jnp.full(x.shape, -1.0 / math.factorial(11), jnp.float32)
    for power in (9, 7, 5, 3, 1):
        series = series * square + (1.0 if power % 4 == 1 else -1.0) / math.factorial(power)
    return sign * x * series


def phase_turns(freq, shift, length):
    steps = freq * shift
    steps = steps - length * jnp.floor(steps * (1.0 / length))
    return steps * (1.0 / length)


def centred(freq, length):
    return jnp.where(freq < length // 2, freq, freq - length) * (1.0 / length)


def spectrum_kernel(
    runs,
    with_meta,
    classes,
    shifts,
    defocus_class,
    defocus,
    run_counts,
    images_in,
    left_in,
    right_in,
    out,
    images,
    left,
    right,
    joined,
    block,
    load_sems,
    send_sems,
):
    particles, length = images.shape[0], images.shape[1]
    owners = out.shape[0]
    rows_each = runs[0][1] - runs[0][0]
    rows = owners * rows_each
    loads = [pltpu.make_async_copy(left_in, left, load_sems.at[0])]
    for p in range(particles):
        loads.append(pltpu.make_async_copy(images_in.at[p], images.at[p], load_sems.at[1 + p]))
    loads.append(pltpu.make_async_copy(right_in, right, load_sems.at[1 + particles]))
    for load in loads:
        load.start()

    every = range(particles)
    focus = [defocus[defocus_class[p]] for p in every]
    shift_x = [shifts[0, p].astype(jnp.float32) for p in every]
    shift_y = [shifts[1, p].astype(jnp.float32) for p in every]
    sublane = lax.broadcasted_iota(jnp.int32, (particles, length), 0)
    freq_x = lax.broadcasted_iota(jnp.int32, (particles, length), 1).astype(jnp.float32)
    phase_x = phase_turns(freq_x, spread(sublane, shift_x), length)
    angle_x = spread(sublane, focus) * centred(freq_x, length) * centred(freq_x, length)
    angle_x = angle_x * (0.5 / math.pi)
    col = [sin_turns(at) for at in (phase_x, phase_x + 0.25, angle_x, angle_x + 0.25)]
    lane = lax.broadcasted_iota(jnp.int32, (rows, LANES), 1)
    which = lane % particles
    quantity = lane // particles
    row_at = lax.broadcasted_iota(jnp.int32, (rows, LANES), 0)
    owner = row_at // rows_each
    freq_y = row_at - owner * rows_each + spread(owner, [begin for begin, _ in runs])
    freq_y = freq_y.astype(jnp.float32)
    phase_y = phase_turns(freq_y, spread(which, shift_y), length)
    angle_y = spread(which, focus) * centred(freq_y, length) * centred(freq_y, length)
    angle_y = (angle_y + PHASE_OFFSET) * (0.5 / math.pi)
    row = jnp.where(quantity < 2, phase_y, angle_y)
    row = sin_turns(row + jnp.where(quantity % 2 == 1, 0.25, 0.0))

    if with_meta:
        digits = jnp.zeros((META_ROWS, LANES), jnp.int32)
        at_row = lax.broadcasted_iota(jnp.int32, (META_ROWS, LANES), 0) % particles
        at_lane = lax.broadcasted_iota(jnp.int32, (META_ROWS, LANES), 1)
        ends = [[run_counts[0, p] for p in every]]
        for s in range(1, run_counts.shape[0] - 1):
            ends.append([ends[-1][p] + run_counts[s, p] for p in every])
        fields = [[classes[p] for p in every], [defocus_class[p] for p in every], *ends]
        for f, values in enumerate(fields):
            value = spread(at_row, values)
            digits = jnp.where(at_lane == f, value // META_BASE, digits)
            digits = jnp.where(at_lane == f + len(fields), value % META_BASE, digits)
        digits = digits.astype(jnp.float32).astype(jnp.bfloat16)
        for d in range(owners):
            block[d, particles * rows_each :, :] = jnp.zeros(
                (META_ROWS, 2 * length), jnp.bfloat16
            )
            block[d, particles * rows_each :, :LANES] = digits

    loads[0].wait()
    table = left[...]
    for p in range(particles):
        loads[1 + p].wait()
        section = jnp.dot(table, images[p], preferred_element_type=jnp.float32)
        section = section.astype(jnp.bfloat16)
        joined[p * rows : (p + 1) * rows, :length] = section[:rows]
        joined[p * rows : (p + 1) * rows, length:] = section[rows:]
    loads[1 + particles].wait()
    sends = []
    for first in range(0, particles, 2):
        spectrum = jnp.dot(
            joined[first * rows : (first + 2) * rows, :],
            right[...],
            preferred_element_type=jnp.float32,
        )
        for p in range(first, first + 2):
            part = spectrum[(p - first) * rows : (p - first + 1) * rows]
            real_part, imag_part = part[:, :length], part[:, length:]
            row_sin, row_cos, row_ctf_sin, row_ctf_cos = [
                row[:, q * particles + p : q * particles + p + 1] for q in range(4)
            ]
            col_sin, col_cos, col_ctf_sin, col_ctf_cos = [part[p : p + 1, :] for part in col]
            transfer = -(row_ctf_sin * col_ctf_cos + row_ctf_cos * col_ctf_sin)
            cosine = transfer * (row_cos * col_cos - row_sin * col_sin)
            sine = transfer * (row_sin * col_cos + row_cos * col_sin)
            real_new = real_part * cosine + imag_part * sine
            imag_new = imag_part * cosine - real_part * sine
            weighted = jnp.concatenate([real_new, imag_new], axis=1).astype(jnp.bfloat16)
            block[:, p * rows_each : (p + 1) * rows_each, :] = weighted.reshape(
                owners, rows_each, 2 * length
            )
        done = pl.ds(first * rows_each, 2 * rows_each)
        if with_meta and first + 2 == particles:
            done = pl.ds(first * rows_each, 2 * rows_each + META_ROWS)
        sends.append(
            pltpu.make_async_copy(block.at[:, done], out.at[:, done], send_sems.at[first // 2])
        )
        sends[-1].start()
    for send in sends:
        send.wait()


def insert_kernel(bins, meta_at, received, codes, out):
    sources = received.shape[0]
    rows = received[...].reshape(-1, received.shape[2])
    codes_all = codes[...]
    for k in range(out.shape[0]):
        bin_index = lax.broadcasted_iota(jnp.int32, (bins, 1), 0) + k * bins
        hot = jnp.where(codes_all == bin_index, 1.0, 0.0).astype(jnp.bfloat16)
        total = jnp.dot(hot, rows, preferred_element_type=jnp.float32)
        out[k, :bins, :] = total.astype(out.dtype)
        if out.shape[1] > bins:
            tiles = out.shape[2] // LANES
            first_half = lax.broadcasted_iota(jnp.int32, (META_ROWS, LANES), 0) < META_ROWS // 2
            for i in range(min(sources, tiles)):
                low = received[i, meta_at : meta_at + META_ROWS, :LANES]
                if i + tiles < sources:
                    high = received[i + tiles, meta_at : meta_at + META_ROWS, :LANES]
                    low = jnp.where(
                        first_half, low.astype(jnp.float32), high.astype(jnp.float32)
                    ).astype(low.dtype)
                out[k, bins:, i * LANES : (i + 1) * LANES] = low


def whole_vmem(count):
    return [pl.BlockSpec(memory_space=pltpu.VMEM)] * count


def centred_square(freq, length):
    half_length = length // 2
    value = ((freq + half_length) % length - half_length).astype(jnp.float32) / length
    return value * value


def slab_roles(batch_count, swapped):
    roles = list(range(batch_count))
    half = batch_count // 2
    if swapped:
        for b in range(1, half, 2):
            roles[b], roles[half + b - 1] = half + b - 1, b
    return roles


def slab_exchange(parts, place, slab_count, roles):
    arrived = []
    for shift in range(1, slab_count):
        perm = []
        for b, role in enumerate(roles):
            upper = role >= len(roles) // 2
            for source in range(slab_count):
                target = (source + shift) % slab_count
                if target < slab_count - 1:
                    ends = (slab_count - 1 - source, slab_count - 1 - target)
                    ends = ends if upper else (source, target)
                    perm.append((b * slab_count + ends[0], b * slab_count + ends[1]))
        block = choose(parts, (place + shift) % slab_count)
        arrived.append(lax.ppermute(block, ("batch", "slab"), perm))
    return arrived


def choose(parts, index):
    chosen = parts[-1]
    for d in range(parts.shape[0] - 1):
        chosen = jnp.where(index == d, parts[d], chosen)
    return chosen


def per_device(images, classes, shifts, defocus_class, defocus, run_counts, dest_map, ref):
    particles, length, _ = images.shape
    batch_count = lax.axis_size("batch")
    slab_count = lax.axis_size("slab")
    batch = lax.axis_index("batch")
    slab = lax.axis_index("slab")
    rows, planes, _ = ref.shape
    mirrored = slab_count == 4 and batch_count % 2 == 0 and 2 * particles <= META_ROWS
    mirrored = mirrored and batch_count * LANES <= 4 * length
    half_batch = batch_count // 2
    sizes = [rows * share // SHARES for share, _ in CHUNKS]
    starts = [sum(sizes[:c]) for c in range(len(CHUNKS))]
    roles = [slab_roles(batch_count, mirrored and swapped) for _, swapped in CHUNKS]
    freq = jnp.arange(length, dtype=jnp.int32)

    fields = slab_count + 1

    cosine, minus_sine, table_right = dft_tables(length)
    table_right = jnp.asarray(table_right.astype(jnp.bfloat16))
    received = []
    weighted = []
    for c, each in enumerate(sizes):
        chunk_rows = batch_count * each
        block = np.array(roles[c])
        order = (block[:, None] * rows + starts[c] + np.arange(each)[None, :]).reshape(-1)
        left = np.concatenate([cosine[order], minus_sine[order]], axis=0)
        runs = [(k * rows + starts[c], k * rows + starts[c] + each) for k in block.tolist()]
        with_meta = c == 0
        block_rows = particles * each + META_ROWS * with_meta
        block_shape = (batch_count, block_rows, 2 * length)
        smem = pl.BlockSpec(memory_space=pltpu.SMEM)
        hbm = pl.BlockSpec(memory_space=pltpu.HBM)
        send = pl.pallas_call(
            functools.partial(spectrum_kernel, runs, with_meta),
            out_shape=jax.ShapeDtypeStruct(block_shape, jnp.bfloat16),
            in_specs=[smem] * 5 + [hbm] * 3,
            out_specs=hbm,
            scratch_shapes=[
                pltpu.VMEM((particles, length, length), jnp.bfloat16),
                pltpu.VMEM((2 * chunk_rows, length), jnp.bfloat16),
                pltpu.VMEM((2 * length, 2 * length), jnp.bfloat16),
                pltpu.VMEM((particles * chunk_rows, 2 * length), jnp.bfloat16),
                pltpu.VMEM(block_shape, jnp.bfloat16),
                pltpu.SemaphoreType.DMA((particles + 2,)),
                pltpu.SemaphoreType.DMA((particles // 2,)),
            ],
            compiler_params=pltpu.CompilerParams(vmem_limit_bytes=SPECTRUM_VMEM),
            cost_estimate=pl.CostEstimate(flops=0, bytes_accessed=0, transcendentals=0),
            name="spectrum",
        )(
            classes,
            shifts.T,
            defocus_class,
            defocus,
            run_counts.T,
            images,
            jnp.asarray(left.astype(jnp.bfloat16)),
            table_right,
        )
        weighted.append(send)
        received.append(lax.all_to_all(send, "batch", 0, 0, tiled=True))

    def read_digits(rows_in):
        whole = rows_in.astype(jnp.int32).reshape(-1, 2 * fields)
        return whole[:, :fields] * META_BASE + whole[:, fields:]

    meta_at = particles * sizes[0]
    meta_layer = read_digits(received[0][:, meta_at : meta_at + particles, : 2 * fields])

    class_count = dest_map.shape[0]

    dest_wide = dest_map.astype(jnp.bfloat16)

    def find_planes(table):
        class_hot = (table[:, :1] == jnp.arange(class_count)[None, :]).astype(jnp.bfloat16)
        local_plane = jnp.dot(class_hot, dest_wide, preferred_element_type=jnp.float32)
        past = freq[None, :, None] >= table[:, None, 2:]
        owner = jnp.sum(past.astype(jnp.int32), axis=2)
        return owner * planes + local_plane.astype(jnp.int32)

    def pick_block(table, block):
        return sum(
            jnp.where(block == k, table[:, k * rows : (k + 1) * rows], 0)
            for k in range(batch_count)
        )

    window_slabs = 3 if mirrored else slab_count
    blocks = [
        sum(jnp.where(batch == b, block, 0) for b, block in enumerate(role)) for role in roles
    ]
    layer_planes = find_planes(meta_layer)
    places, codes = [], []
    for c, each in enumerate(sizes):
        here = slice(starts[c], starts[c] + each)
        plane = pick_block(layer_planes, blocks[c])[:, here]
        place, owner_place = slab, plane // planes
        if mirrored:
            upper = blocks[c] >= half_batch
            owner_place = jnp.where(upper, slab_count - 1 - owner_place, owner_place)
            place = jnp.where(upper, slab_count - 1 - slab, slab)
        places.append(place)
        code = owner_place * (each * planes) + jnp.arange(each)[None, :] * planes
        code = (code + plane % planes).reshape(batch_count, particles * each)
        if c == 0:
            code = jnp.pad(code, ((0, 0), (0, META_ROWS)), constant_values=-1)
        codes.append(code.reshape(1, -1))

    sums, arrived = [], []
    for c, each in enumerate(sizes):
        bins = each * planes
        extra_rows = META_ROWS if c == 0 and mirrored else 0
        codes_in = codes[c]
        if c == 0:
            codes_in, _ = lax.optimization_barrier((codes_in, weighted[1:]))
        if c > 0 and mirrored:
            codes_in, arrived[c - 1][0], arrived[c - 1][2] = lax.optimization_barrier(
                (codes_in, arrived[c - 1][0], arrived[c - 1][2])
            )
        parts = pl.pallas_call(
            functools.partial(insert_kernel, bins, meta_at),
            out_shape=jax.ShapeDtypeStruct(
                (window_slabs, bins + extra_rows, 2 * length), jnp.bfloat16
            ),
            in_specs=whole_vmem(2),
            out_specs=pl.BlockSpec(memory_space=pltpu.VMEM),
            compiler_params=pltpu.CompilerParams(vmem_limit_bytes=INSERT_VMEM),
            cost_estimate=pl.CostEstimate(
                flops=0,
                bytes_accessed=0,
                transcendentals=0,
            ),
            name="insert",
        )(received[c], codes_in)
        if not mirrored:
            sums.append(lax.psum_scatter(parts, "slab", scatter_dimension=0, tiled=False))
            continue
        for before in arrived:
            before[1], _ = lax.optimization_barrier((before[1], parts))
        arrived.append(slab_exchange(parts, places[c], slab_count, roles[c]))
        own = choose(parts[:, :bins], places[c]).astype(jnp.float32)
        sums.append(jnp.where(places[c] == slab_count - 1, 0.0, own))
    for c, each in enumerate(sizes):
        if not mirrored:
            break
        for block in arrived[c]:
            sums[c] = sums[c] + block[: each * planes].astype(jnp.float32)
        over = [(b, block) for b, block in enumerate(roles[c]) if b != block]
        if over:
            if c + 1 < len(sizes):
                sums[c], arrived[c + 1][2] = lax.optimization_barrier(
                    (sums[c], arrived[c + 1][2])
                )
            handed = lax.ppermute(sums[c].astype(jnp.bfloat16), "batch", over)
            sums[c] = jnp.where(blocks[c] == batch, sums[c], handed.astype(jnp.float32))

    meta_all = [meta_layer]
    if mirrored:
        for block in [block[sizes[0] * planes :] for block in arrived[0]]:
            block = block.reshape(META_ROWS, -1, LANES)
            halves = (block[:particles], block[particles : 2 * particles])
            low = jnp.concatenate(halves, axis=1)[:, :batch_count, : 2 * fields]
            meta_all.append(read_digits(low.transpose(1, 0, 2)))
    else:
        for step in range(1, slab_count):
            ring = [(s, (s + step) % slab_count) for s in range(slab_count)]
            meta_all.append(lax.ppermute(meta_layer, "slab", ring))
    meta_all = jnp.concatenate(meta_all, axis=0)

    own_freq = batch * rows + jnp.arange(rows, dtype=jnp.int32)
    own_plane = pick_block(find_planes(meta_all), batch) - slab * planes
    focus_count = defocus.shape[0]
    focus_hot = (meta_all[:, 1:2] == jnp.arange(focus_count)[None, :]).astype(jnp.bfloat16)
    if mirrored:
        own_plane = jnp.where(places[0] == slab_count - 1, -1, own_plane)
    bin_hot = (own_plane.T[:, None, :] == jnp.arange(planes)[None, :, None]).astype(jnp.bfloat16)
    counts = jnp.einsum("kzp,pd->kzd", bin_hot, focus_hot, preferred_element_type=jnp.float32)
    row_angle = 2.0 * (
        defocus[None, :] * centred_square(own_freq, length)[:, None] + PHASE_OFFSET
    )
    col_angle = 2.0 * (defocus[:, None] * centred_square(freq, length)[None, :])
    row_side = jnp.concatenate(
        [counts * jnp.cos(row_angle)[:, None, :], counts * jnp.sin(row_angle)[:, None, :]], axis=2
    )
    col_side = jnp.concatenate([jnp.cos(col_angle), -jnp.sin(col_angle)], axis=0)
    double = jnp.einsum("kzd,dx->kzx", row_side, col_side, precision=lax.Precision.HIGHEST)
    weights = 0.5 * (jnp.sum(counts, axis=2, keepdims=True) - double)
    denom = weights + TAU_PRIOR

    updated = []
    for c, each in enumerate(sizes):
        here = slice(starts[c], starts[c] + each)
        prior = ref[here].astype(jnp.float32)
        under = denom[here]
        total = sums[c].astype(jnp.float32).reshape(each, planes, 2 * length)
        updated.append(
            (
                (TAU_PRIOR * prior + total) / jnp.concatenate([under, under], axis=2)
            ).astype(jnp.bfloat16)
        )
    return jnp.concatenate(updated, axis=0)


def solution(mesh):
    placed = (
        P(("batch", "slab"), None, None),
        P(("batch", "slab")),
        P(("batch", "slab"), None),
        P(("batch", "slab")),
        P(),
        P(("batch", "slab"), None),
        P(),
        P("batch", "slab", None),
    )
    return jax.shard_map(
        per_device, mesh=mesh, in_specs=placed, out_specs=P("batch", "slab", None), check_vma=False
    )
```

```python
import functools
import math

import jax
import jax.numpy as jnp
import numpy as np
from jax import lax
from jax.experimental import pallas as pl
from jax.experimental.pallas import tpu as pltpu
from jax.sharding import PartitionSpec as P

TAU_PRIOR = 4.0
PHASE_OFFSET = 0.1
CHUNKS = ((2, True), (2, True), (2, False))
SHARES = 6
META_BASE = 32
META_ROWS = 16
LANES = 128
SPECTRUM_VMEM = 60 * 1024 * 1024
INSERT_VMEM = 32 * 1024 * 1024


def dft_tables(length):
    index = np.arange(length, dtype=np.int32)
    turns = index[:, None] * index[None, :] % length
    angle = np.float32(2.0 * math.pi / length) * turns.astype(np.float32)
    factor = np.float32(1.0 / math.sqrt(length))
    cosine = np.cos(angle) * factor
    sine = np.sin(angle) * factor
    upper_rows = np.concatenate([cosine, -sine], axis=1)
    lower_rows = np.concatenate([sine, cosine], axis=1)
    table_right = np.concatenate([upper_rows, lower_rows], axis=0)
    return cosine, -sine, table_right


def spread(iota, values):
    out = jnp.full(iota.shape, values[0])
    for p in range(1, len(values)):
        out = jnp.where(iota == p, values[p], out)
    return out


def sin_turns(turns):
    half = jnp.floor(2.0 * turns + 0.5)
    x = (2.0 * math.pi) * (turns - 0.5 * half)
    sign = 1.0 - 2.0 * (half - 2.0 * jnp.floor(0.5 * half))
    square = x * x
    series = jnp.full(x.shape, -1.0 / math.factorial(11), jnp.float32)
    for power in (9, 7, 5, 3, 1):
        series = series * square + (1.0 if power % 4 == 1 else -1.0) / math.factorial(power)
    return sign * x * series


def phase_turns(freq, shift, length):
    steps = freq * shift
    steps = steps - length * jnp.floor(steps * (1.0 / length))
    return steps * (1.0 / length)


def centred(freq, length):
    return jnp.where(freq < length // 2, freq, freq - length) * (1.0 / length)


def spectrum_kernel(runs, meta_from, *refs):
    classes, shifts, defocus_class, defocus, run_counts, images_in, left_in, right_in, *refs = refs
    if meta_from == "operand":
        meta_in, *refs = refs
    out, *refs = refs
    if meta_from == "scalars":
        meta_out, *refs = refs
    images, left, right, joined, block, load_sems, send_sems = refs
    particles, length = images.shape[0], images.shape[1]
    owners = out.shape[0]
    rows_each = runs[0][1] - runs[0][0]
    rows = owners * rows_each
    loads = [pltpu.make_async_copy(left_in, left, load_sems.at[0])]
    for p in range(particles):
        loads.append(pltpu.make_async_copy(images_in.at[p], images.at[p], load_sems.at[1 + p]))
    loads.append(pltpu.make_async_copy(right_in, right, load_sems.at[1 + particles]))
    for load in loads:
        load.start()

    every = range(particles)
    focus = [defocus[defocus_class[p]] for p in every]
    shift_x = [shifts[0, p].astype(jnp.float32) for p in every]
    shift_y = [shifts[1, p].astype(jnp.float32) for p in every]
    sublane = lax.broadcasted_iota(jnp.int32, (particles, length), 0)
    freq_x = lax.broadcasted_iota(jnp.int32, (particles, length), 1).astype(jnp.float32)
    phase_x = phase_turns(freq_x, spread(sublane, shift_x), length)
    angle_x = spread(sublane, focus) * centred(freq_x, length) * centred(freq_x, length)
    angle_x = angle_x * (0.5 / math.pi)
    col = [sin_turns(at) for at in (phase_x, phase_x + 0.25, angle_x, angle_x + 0.25)]
    lane = lax.broadcasted_iota(jnp.int32, (rows, LANES), 1)
    which = lane & (particles - 1)
    quantity = (lane - which) * (1.0 / particles)
    row_at = lax.broadcasted_iota(jnp.int32, (rows, LANES), 0)
    freq_y = row_at + runs[0][0]
    for d in range(1, owners):
        freq_y = jnp.where(row_at >= d * rows_each, row_at + (runs[d][0] - d * rows_each), freq_y)
    freq_y = freq_y.astype(jnp.float32)
    phase_y = phase_turns(freq_y, spread(which, shift_y), length)
    angle_y = spread(which, focus) * centred(freq_y, length) * centred(freq_y, length)
    angle_y = (angle_y + PHASE_OFFSET) * (0.5 / math.pi)
    row = jnp.where(quantity < 2.0, phase_y, angle_y)
    row = sin_turns(row + jnp.where((quantity == 1.0) | (quantity == 3.0), 0.25, 0.0))

    if meta_from == "operand":
        for d in range(owners):
            block[d, particles * rows_each :, :] = meta_in[...]
    if meta_from == "scalars":
        digits = jnp.zeros((META_ROWS, LANES), jnp.int32)
        at_row = lax.broadcasted_iota(jnp.int32, (META_ROWS, LANES), 0)
        at_row = at_row & (particles - 1)
        at_lane = lax.broadcasted_iota(jnp.int32, (META_ROWS, LANES), 1)
        ends = [[run_counts[0, p] for p in every]]
        for s in range(1, run_counts.shape[0] - 1):
            ends.append([ends[-1][p] + run_counts[s, p] for p in every])
        fields = [[classes[p] for p in every], [defocus_class[p] for p in every], *ends]
        for f, values in enumerate(fields):
            value = spread(at_row, values)
            digits = jnp.where(at_lane == f, value // META_BASE, digits)
            digits = jnp.where(at_lane == f + len(fields), value % META_BASE, digits)
        digits = digits.astype(jnp.float32).astype(jnp.bfloat16)
        meta_out[...] = digits
        for d in range(owners):
            block[d, particles * rows_each :, :] = jnp.zeros(
                (META_ROWS, 2 * length), jnp.bfloat16
            )
            block[d, particles * rows_each :, :LANES] = digits

    loads[0].wait()
    table = left[...]
    for p in range(particles):
        loads[1 + p].wait()
        section = jnp.dot(table, images[p], preferred_element_type=jnp.float32)
        section = section.astype(jnp.bfloat16)
        joined[p * rows : (p + 1) * rows, :length] = section[:rows]
        joined[p * rows : (p + 1) * rows, length:] = section[rows:]
    loads[1 + particles].wait()
    sends = []
    for first in range(0, particles, 2):
        spectrum = jnp.dot(
            joined[first * rows : (first + 2) * rows, :],
            right[...],
            preferred_element_type=jnp.float32,
        )
        for p in range(first, first + 2):
            part = spectrum[(p - first) * rows : (p - first + 1) * rows]
            real_part, imag_part = part[:, :length], part[:, length:]
            row_sin, row_cos, row_ctf_sin, row_ctf_cos = [
                row[:, q * particles + p : q * particles + p + 1] for q in range(4)
            ]
            col_sin, col_cos, col_ctf_sin, col_ctf_cos = [part[p : p + 1, :] for part in col]
            transfer = -(row_ctf_sin * col_ctf_cos + row_ctf_cos * col_ctf_sin)
            cosine = transfer * (row_cos * col_cos - row_sin * col_sin)
            sine = transfer * (row_sin * col_cos + row_cos * col_sin)
            real_new = real_part * cosine + imag_part * sine
            imag_new = imag_part * cosine - real_part * sine
            weighted = jnp.concatenate([real_new, imag_new], axis=1).astype(jnp.bfloat16)
            block[:, p * rows_each : (p + 1) * rows_each, :] = weighted.reshape(
                owners, rows_each, 2 * length
            )
        done = pl.ds(first * rows_each, 2 * rows_each)
        if meta_from and first + 2 == particles:
            done = pl.ds(first * rows_each, 2 * rows_each + META_ROWS)
        sends.append(
            pltpu.make_async_copy(block.at[:, done], out.at[:, done], send_sems.at[first // 2])
        )
        sends[-1].start()
    for send in sends:
        send.wait()


def insert_kernel(received, codes, out):
    windows, bins, _ = out.shape
    rows = received[...].reshape(-1, received.shape[2])
    codes_all = codes[...]
    for k in range(windows):
        bin_index = lax.broadcasted_iota(jnp.int32, (bins, 1), 0) + k * bins
        hot = jnp.where(codes_all == bin_index, 1.0, 0.0).astype(jnp.bfloat16)
        total = jnp.dot(hot, rows, preferred_element_type=jnp.float32)
        out[k] = total.astype(out.dtype)


def whole_vmem(count):
    return [pl.BlockSpec(memory_space=pltpu.VMEM)] * count


def centred_square(freq, length):
    half_length = length // 2
    value = ((freq + half_length) % length - half_length).astype(jnp.float32) / length
    return value * value


def slab_roles(batch_count, swapped):
    roles = list(range(batch_count))
    half = batch_count // 2
    if swapped:
        for b in range(1, half, 2):
            roles[b], roles[half + b - 1] = half + b - 1, b
    return roles


def slab_exchange(parts, place, slab_count, roles):
    arrived = []
    for shift in range(1, slab_count):
        perm = []
        for b, role in enumerate(roles):
            upper = role >= len(roles) // 2
            for source in range(slab_count):
                target = (source + shift) % slab_count
                if target < slab_count - 1:
                    ends = (slab_count - 1 - source, slab_count - 1 - target)
                    ends = ends if upper else (source, target)
                    perm.append((b * slab_count + ends[0], b * slab_count + ends[1]))
        block = choose(parts, (place + shift) % slab_count)
        arrived.append(lax.ppermute(block, ("batch", "slab"), perm))
    return arrived


def choose(parts, index):
    chosen = parts[-1]
    for d in range(parts.shape[0] - 1):
        chosen = jnp.where(index == d, parts[d], chosen)
    return chosen


def per_device(images, classes, shifts, defocus_class, defocus, run_counts, dest_map, ref):
    particles, length, _ = images.shape
    batch_count = lax.axis_size("batch")
    slab_count = lax.axis_size("slab")
    batch = lax.axis_index("batch")
    slab = lax.axis_index("slab")
    rows, planes, _ = ref.shape
    mirrored = slab_count == 4 and batch_count % 2 == 0
    half_batch = batch_count // 2
    sizes = [rows * share // SHARES for share, _ in CHUNKS]
    starts = [sum(sizes[:c]) for c in range(len(CHUNKS))]
    roles = [slab_roles(batch_count, mirrored and swapped) for _, swapped in CHUNKS]
    freq = jnp.arange(length, dtype=jnp.int32)

    fields = slab_count + 1

    cosine, minus_sine, table_right = dft_tables(length)
    table_right = jnp.asarray(table_right.astype(jnp.bfloat16))
    received = []
    weighted = []
    for c, each in enumerate(sizes):
        chunk_rows = batch_count * each
        block = np.array(roles[c])
        order = (block[:, None] * rows + starts[c] + np.arange(each)[None, :]).reshape(-1)
        left = np.concatenate([cosine[order], minus_sine[order]], axis=0)
        runs = [(k * rows + starts[c], k * rows + starts[c] + each) for k in block.tolist()]
        last = c + 1 == len(sizes)
        meta_from = "scalars" if c == 0 else "operand" if last else None
        block_rows = particles * each + (META_ROWS if meta_from else 0)
        block_shape = (batch_count, block_rows, 2 * length)
        smem = pl.BlockSpec(memory_space=pltpu.SMEM)
        hbm = pl.BlockSpec(memory_space=pltpu.HBM)
        vmem = pl.BlockSpec(memory_space=pltpu.VMEM)
        send, *meta_out = pl.pallas_call(
            functools.partial(spectrum_kernel, runs, meta_from),
            out_shape=[jax.ShapeDtypeStruct(block_shape, jnp.bfloat16)]
            + [jax.ShapeDtypeStruct((META_ROWS, LANES), jnp.bfloat16)] * (c == 0),
            in_specs=[smem] * 5 + [hbm] * 3 + [vmem] * last,
            out_specs=[hbm] + [vmem] * (c == 0),
            scratch_shapes=[
                pltpu.VMEM((particles, length, length), jnp.bfloat16),
                pltpu.VMEM((2 * chunk_rows, length), jnp.bfloat16),
                pltpu.VMEM((2 * length, 2 * length), jnp.bfloat16),
                pltpu.VMEM((particles * chunk_rows, 2 * length), jnp.bfloat16),
                pltpu.VMEM(block_shape, jnp.bfloat16),
                pltpu.SemaphoreType.DMA((particles + 2,)),
                pltpu.SemaphoreType.DMA((particles // 2,)),
            ],
            compiler_params=pltpu.CompilerParams(vmem_limit_bytes=SPECTRUM_VMEM),
            cost_estimate=pl.CostEstimate(flops=0, bytes_accessed=0, transcendentals=0),
            name="spectrum",
        )(
            classes,
            shifts.T,
            defocus_class,
            defocus,
            run_counts.T,
            images,
            jnp.asarray(left.astype(jnp.bfloat16)),
            table_right,
            *([digits] if last else []),
        )
        if c == 0:
            own_digits = meta_out[0]
        if c == 1:
            own_digits, send = lax.optimization_barrier((own_digits, send))
            layers = [own_digits]
            for step in range(1, slab_count):
                ring = [(s, (s + step) % slab_count) for s in range(slab_count)]
                layers.append(lax.ppermute(own_digits, "slab", ring))
            digits = jnp.concatenate([layer[:, : 2 * fields] for layer in layers], axis=1)
            digits = jnp.pad(digits, ((0, 0), (0, 2 * length - digits.shape[1])))
        weighted.append(send)
        received.append(lax.all_to_all(send, "batch", 0, 0, tiled=True))

    def read_digits(rows_in):
        whole = rows_in.astype(jnp.int32).reshape(-1, 2 * fields)
        return whole[:, :fields] * META_BASE + whole[:, fields:]

    at = [particles * each for each in sizes]
    layer_digits = received[0][:, at[0] : at[0] + particles, : 2 * fields]
    meta_layer = read_digits(layer_digits)
    all_digits = received[-1][:, at[-1] : at[-1] + particles, : slab_count * 2 * fields]
    meta_all = read_digits(all_digits)

    class_count = dest_map.shape[0]

    dest_wide = dest_map.astype(jnp.bfloat16)

    def find_planes(table):
        class_hot = (table[:, :1] == jnp.arange(class_count)[None, :]).astype(jnp.bfloat16)
        local_plane = jnp.dot(class_hot, dest_wide, preferred_element_type=jnp.float32)
        past = freq[None, :, None] >= table[:, None, 2:]
        owner = jnp.sum(past.astype(jnp.int32), axis=2)
        return owner * planes + local_plane.astype(jnp.int32)

    def pick_block(table, block):
        return sum(
            jnp.where(block == k, table[:, k * rows : (k + 1) * rows], 0)
            for k in range(batch_count)
        )

    window_slabs = 3 if mirrored else slab_count
    blocks = [
        sum(jnp.where(batch == b, block, 0) for b, block in enumerate(role)) for role in roles
    ]
    layer_planes = find_planes(meta_layer)
    places, codes = [], []
    for c, each in enumerate(sizes):
        here = slice(starts[c], starts[c] + each)
        plane = pick_block(layer_planes, blocks[c])[:, here]
        place, owner_place = slab, plane // planes
        if mirrored:
            upper = blocks[c] >= half_batch
            owner_place = jnp.where(upper, slab_count - 1 - owner_place, owner_place)
            place = jnp.where(upper, slab_count - 1 - slab, slab)
        places.append(place)
        code = owner_place * (each * planes) + jnp.arange(each)[None, :] * planes
        code = (code + plane % planes).reshape(batch_count, particles * each)
        if c in (0, len(sizes) - 1):
            code = jnp.pad(code, ((0, 0), (0, META_ROWS)), constant_values=-1)
        codes.append(code.reshape(1, -1))

    sums, arrived = [], []
    for c, each in enumerate(sizes):
        bins = each * planes
        codes_in = codes[c]
        if c == 0:
            codes_in, _ = lax.optimization_barrier((codes_in, weighted[1:]))
        if c > 0 and mirrored:
            codes_in, arrived[c - 1][2] = lax.optimization_barrier((codes_in, arrived[c - 1][2]))
        parts = pl.pallas_call(
            insert_kernel,
            out_shape=jax.ShapeDtypeStruct((window_slabs, bins, 2 * length), jnp.bfloat16),
            in_specs=whole_vmem(2),
            out_specs=pl.BlockSpec(memory_space=pltpu.VMEM),
            compiler_params=pltpu.CompilerParams(vmem_limit_bytes=INSERT_VMEM),
            cost_estimate=pl.CostEstimate(
                flops=0,
                bytes_accessed=0,
                transcendentals=0,
            ),
            name="insert",
        )(received[c], codes_in)
        if not mirrored:
            sums.append(lax.psum_scatter(parts, "slab", scatter_dimension=0, tiled=False))
            continue
        for before in arrived:
            before[1], _ = lax.optimization_barrier((before[1], parts))
        arrived.append(slab_exchange(parts, places[c], slab_count, roles[c]))
        own = choose(parts, places[c]).astype(jnp.float32)
        sums.append(jnp.where(places[c] == slab_count - 1, 0.0, own))
    for c, each in enumerate(sizes):
        if not mirrored:
            break
        for block in arrived[c]:
            sums[c] = sums[c] + block.astype(jnp.float32)
        over = [(b, block) for b, block in enumerate(roles[c]) if b != block]
        if over:
            if c + 1 < len(sizes):
                sums[c], arrived[c + 1][2] = lax.optimization_barrier(
                    (sums[c], arrived[c + 1][2])
                )
            handed = lax.ppermute(sums[c].astype(jnp.bfloat16), "batch", over)
            sums[c] = jnp.where(blocks[c] == batch, sums[c], handed.astype(jnp.float32))

    own_freq = batch * rows + jnp.arange(rows, dtype=jnp.int32)
    own_plane = pick_block(find_planes(meta_all), batch) - slab * planes
    focus_count = defocus.shape[0]
    focus_hot = (meta_all[:, 1:2] == jnp.arange(focus_count)[None, :]).astype(jnp.bfloat16)
    bin_hot = (own_plane.T[:, None, :] == jnp.arange(planes)[None, :, None]).astype(jnp.bfloat16)
    counts = jnp.einsum("kzp,pd->kzd", bin_hot, focus_hot, preferred_element_type=jnp.float32)
    row_angle = 2.0 * (
        defocus[None, :] * centred_square(own_freq, length)[:, None] + PHASE_OFFSET
    )
    col_angle = 2.0 * (defocus[:, None] * centred_square(freq, length)[None, :])
    row_side = jnp.concatenate(
        [counts * jnp.cos(row_angle)[:, None, :], counts * jnp.sin(row_angle)[:, None, :]], axis=2
    )
    col_side = jnp.concatenate([jnp.cos(col_angle), -jnp.sin(col_angle)], axis=0)
    double = jnp.einsum("kzd,dx->kzx", row_side, col_side, precision=lax.Precision.HIGHEST)
    weights = 0.5 * (jnp.sum(counts, axis=2, keepdims=True) - double)
    denom = weights + TAU_PRIOR

    updated = []
    for c, each in enumerate(sizes):
        here = slice(starts[c], starts[c] + each)
        prior = ref[here].astype(jnp.float32)
        under = denom[here]
        total = sums[c].astype(jnp.float32).reshape(each, planes, 2 * length)
        updated.append(
            (
                (TAU_PRIOR * prior + total) / jnp.concatenate([under, under], axis=2)
            ).astype(jnp.bfloat16)
        )
    return jnp.concatenate(updated, axis=0)


def solution(mesh):
    placed = (
        P(("batch", "slab"), None, None),
        P(("batch", "slab")),
        P(("batch", "slab"), None),
        P(("batch", "slab")),
        P(),
        P(("batch", "slab"), None),
        P(),
        P("batch", "slab", None),
    )
    return jax.shard_map(
        per_device, mesh=mesh, in_specs=placed, out_specs=P("batch", "slab", None), check_vma=False
    )
```

```python
import functools
import math

import jax
import jax.numpy as jnp
import numpy as np
from jax import lax
from jax.experimental import pallas as pl
from jax.experimental.pallas import tpu as pltpu
from jax.sharding import PartitionSpec as P

TAU_PRIOR = 4.0
PHASE_OFFSET = 0.1
CHUNKS = ((2, True), (2, True), (2, False))
SHARES = 6
META_BASE = 32
META_ROWS = 16
LANES = 128
SPECTRUM_VMEM = 60 * 1024 * 1024
INSERT_VMEM = 32 * 1024 * 1024


def dft_table(length):
    index = np.arange(length, dtype=np.int32)
    turns = index[:, None] * index[None, :] % length
    angle = np.float32(2.0 * math.pi / length) * turns.astype(np.float32)
    factor = np.float32(1.0 / math.sqrt(length))
    return np.concatenate([np.cos(angle) * factor, -(np.sin(angle) * factor)], axis=1)


def spread(iota, values):
    out = jnp.full(iota.shape, values[0])
    for p in range(1, len(values)):
        out = jnp.where(iota == p, values[p], out)
    return out


def sin_turns(turns):
    half = jnp.floor(2.0 * turns + 0.5)
    x = (2.0 * math.pi) * (turns - 0.5 * half)
    sign = 1.0 - 2.0 * (half - 2.0 * jnp.floor(0.5 * half))
    square = x * x
    series = jnp.full(x.shape, -1.0 / math.factorial(11), jnp.float32)
    for power in (9, 7, 5, 3, 1):
        series = series * square + (1.0 if power % 4 == 1 else -1.0) / math.factorial(power)
    return sign * x * series


def phase_turns(freq, shift, length):
    steps = freq * shift
    steps = steps - length * jnp.floor(steps * (1.0 / length))
    return steps * (1.0 / length)


def centred(freq, length):
    return jnp.where(freq < length // 2, freq, freq - length) * (1.0 / length)


def spectrum_kernel(runs, meta_from, *refs):
    classes, shifts, defocus_class, defocus, run_counts, images_in, upper_in, *refs = refs
    if meta_from == "operand":
        meta_in, *refs = refs
    out, *refs = refs
    if meta_from == "scalars":
        meta_out, *refs = refs
    images, left, right, joined, block, load_sems, send_sems = refs
    particles, length = images.shape[0], images.shape[1]
    owners = out.shape[0]
    rows_each = runs[0][1] - runs[0][0]
    rows = owners * rows_each
    loads = [pltpu.make_async_copy(upper_in, right.at[:length], load_sems.at[0])]
    for p in range(particles):
        loads.append(pltpu.make_async_copy(images_in.at[p], images.at[p], load_sems.at[1 + p]))
    for load in loads:
        load.start()

    every = range(particles)
    focus = [defocus[defocus_class[p]] for p in every]
    shift_x = [shifts[0, p].astype(jnp.float32) for p in every]
    shift_y = [shifts[1, p].astype(jnp.float32) for p in every]
    sublane = lax.broadcasted_iota(jnp.int32, (particles, length), 0)
    freq_x = lax.broadcasted_iota(jnp.int32, (particles, length), 1).astype(jnp.float32)
    phase_x = phase_turns(freq_x, spread(sublane, shift_x), length)
    angle_x = spread(sublane, focus) * centred(freq_x, length) * centred(freq_x, length)
    angle_x = angle_x * (0.5 / math.pi)
    col = [sin_turns(at) for at in (phase_x, phase_x + 0.25, angle_x, angle_x + 0.25)]
    lane = lax.broadcasted_iota(jnp.int32, (rows, LANES), 1)
    which = lane & (particles - 1)
    quantity = (lane - which) * (1.0 / particles)
    row_at = lax.broadcasted_iota(jnp.int32, (rows, LANES), 0)
    freq_y = row_at + runs[0][0]
    for d in range(1, owners):
        freq_y = jnp.where(row_at >= d * rows_each, row_at + (runs[d][0] - d * rows_each), freq_y)
    freq_y = freq_y.astype(jnp.float32)
    phase_y = phase_turns(freq_y, spread(which, shift_y), length)
    angle_y = spread(which, focus) * centred(freq_y, length) * centred(freq_y, length)
    angle_y = (angle_y + PHASE_OFFSET) * (0.5 / math.pi)
    row = jnp.where(quantity < 2.0, phase_y, angle_y)
    row = sin_turns(row + jnp.where((quantity == 1.0) | (quantity == 3.0), 0.25, 0.0))

    if meta_from == "operand":
        for d in range(owners):
            block[d, particles * rows_each :, :] = meta_in[...]
    if meta_from == "scalars":
        digits = jnp.zeros((META_ROWS, LANES), jnp.int32)
        at_row = lax.broadcasted_iota(jnp.int32, (META_ROWS, LANES), 0)
        at_row = at_row & (particles - 1)
        at_lane = lax.broadcasted_iota(jnp.int32, (META_ROWS, LANES), 1)
        ends = [[run_counts[0, p] for p in every]]
        for s in range(1, run_counts.shape[0] - 1):
            ends.append([ends[-1][p] + run_counts[s, p] for p in every])
        fields = [[classes[p] for p in every], [defocus_class[p] for p in every], *ends]
        for f, values in enumerate(fields):
            value = spread(at_row, values)
            digits = jnp.where(at_lane == f, value // META_BASE, digits)
            digits = jnp.where(at_lane == f + len(fields), value % META_BASE, digits)
        digits = digits.astype(jnp.float32).astype(jnp.bfloat16)
        meta_out[...] = digits
        for d in range(owners):
            block[d, particles * rows_each :, :] = jnp.zeros(
                (META_ROWS, 2 * length), jnp.bfloat16
            )
            block[d, particles * rows_each :, :LANES] = digits

    loads[0].wait()
    for d, (begin, end) in enumerate(runs):
        here = slice(d * rows_each, (d + 1) * rows_each)
        left[here, :] = right[begin:end, :length]
        left[rows + here.start : rows + here.stop, :] = right[begin:end, length:]
    right[length:, :length] = -right[:length, length:]
    right[length:, length:] = right[:length, :length]
    table = left[...]
    sends = []
    for first in range(0, particles, 2):
        for p in range(first, first + 2):
            loads[1 + p].wait()
            section = jnp.dot(table, images[p], preferred_element_type=jnp.float32)
            section = section.astype(jnp.bfloat16)
            joined[p * rows : (p + 1) * rows, :length] = section[:rows]
            joined[p * rows : (p + 1) * rows, length:] = section[rows:]
        spectrum = jnp.dot(
            joined[first * rows : (first + 2) * rows, :],
            right[...],
            preferred_element_type=jnp.float32,
        )
        for p in range(first, first + 2):
            part = spectrum[(p - first) * rows : (p - first + 1) * rows]
            real_part, imag_part = part[:, :length], part[:, length:]
            row_sin, row_cos, row_ctf_sin, row_ctf_cos = [
                row[:, q * particles + p : q * particles + p + 1] for q in range(4)
            ]
            col_sin, col_cos, col_ctf_sin, col_ctf_cos = [part[p : p + 1, :] for part in col]
            transfer = -(row_ctf_sin * col_ctf_cos + row_ctf_cos * col_ctf_sin)
            cosine = transfer * (row_cos * col_cos - row_sin * col_sin)
            sine = transfer * (row_sin * col_cos + row_cos * col_sin)
            real_new = real_part * cosine + imag_part * sine
            imag_new = imag_part * cosine - real_part * sine
            weighted = jnp.concatenate([real_new, imag_new], axis=1).astype(jnp.bfloat16)
            block[:, p * rows_each : (p + 1) * rows_each, :] = weighted.reshape(
                owners, rows_each, 2 * length
            )
        done = pl.ds(first * rows_each, 2 * rows_each)
        if meta_from and first + 2 == particles:
            done = pl.ds(first * rows_each, 2 * rows_each + META_ROWS)
        sends.append(
            pltpu.make_async_copy(block.at[:, done], out.at[:, done], send_sems.at[first // 2])
        )
        sends[-1].start()
    for send in sends:
        send.wait()


def insert_kernel(received, codes, out):
    windows, bins, _ = out.shape
    rows = received[...].reshape(-1, received.shape[2])
    codes_all = codes[...]
    for k in range(windows):
        bin_index = lax.broadcasted_iota(jnp.int32, (bins, 1), 0) + k * bins
        hot = jnp.where(codes_all == bin_index, 1.0, 0.0).astype(jnp.bfloat16)
        total = jnp.dot(hot, rows, preferred_element_type=jnp.float32)
        out[k] = total.astype(out.dtype)


def whole_vmem(count):
    return [pl.BlockSpec(memory_space=pltpu.VMEM)] * count


def centred_square(freq, length):
    half_length = length // 2
    value = ((freq + half_length) % length - half_length).astype(jnp.float32) / length
    return value * value


def slab_roles(batch_count, swapped):
    roles = list(range(batch_count))
    half = batch_count // 2
    if swapped:
        for b in range(1, half, 2):
            roles[b], roles[half + b - 1] = half + b - 1, b
    return roles


def slab_exchange(parts, place, slab_count, roles):
    arrived = []
    for shift in range(1, slab_count):
        perm = []
        for b, role in enumerate(roles):
            upper = role >= len(roles) // 2
            for source in range(slab_count):
                target = (source + shift) % slab_count
                if target < slab_count - 1:
                    ends = (slab_count - 1 - source, slab_count - 1 - target)
                    ends = ends if upper else (source, target)
                    perm.append((b * slab_count + ends[0], b * slab_count + ends[1]))
        block = choose(parts, (place + shift) % slab_count)
        arrived.append(lax.ppermute(block, ("batch", "slab"), perm))
    return arrived


def choose(parts, index):
    chosen = parts[-1]
    for d in range(parts.shape[0] - 1):
        chosen = jnp.where(index == d, parts[d], chosen)
    return chosen


def per_device(images, classes, shifts, defocus_class, defocus, run_counts, dest_map, ref):
    particles, length, _ = images.shape
    batch_count = lax.axis_size("batch")
    slab_count = lax.axis_size("slab")
    batch = lax.axis_index("batch")
    slab = lax.axis_index("slab")
    rows, planes, _ = ref.shape
    mirrored = slab_count == 4 and batch_count % 2 == 0
    half_batch = batch_count // 2
    sizes = [rows * share // SHARES for share, _ in CHUNKS]
    starts = [sum(sizes[:c]) for c in range(len(CHUNKS))]
    roles = [slab_roles(batch_count, mirrored and swapped) for _, swapped in CHUNKS]
    freq = jnp.arange(length, dtype=jnp.int32)

    fields = slab_count + 1

    table_upper = jnp.asarray(dft_table(length).astype(jnp.bfloat16))
    received = []
    weighted = []
    for c, each in enumerate(sizes):
        chunk_rows = batch_count * each
        runs = [(k * rows + starts[c], k * rows + starts[c] + each) for k in roles[c]]
        last = c + 1 == len(sizes)
        meta_from = "scalars" if c == 0 else "operand" if last else None
        block_rows = particles * each + (META_ROWS if meta_from else 0)
        block_shape = (batch_count, block_rows, 2 * length)
        smem = pl.BlockSpec(memory_space=pltpu.SMEM)
        hbm = pl.BlockSpec(memory_space=pltpu.HBM)
        vmem = pl.BlockSpec(memory_space=pltpu.VMEM)
        send, *meta_out = pl.pallas_call(
            functools.partial(spectrum_kernel, runs, meta_from),
            out_shape=[jax.ShapeDtypeStruct(block_shape, jnp.bfloat16)]
            + [jax.ShapeDtypeStruct((META_ROWS, LANES), jnp.bfloat16)] * (c == 0),
            in_specs=[smem] * 5 + [hbm] * 2 + [vmem] * last,
            out_specs=[hbm] + [vmem] * (c == 0),
            scratch_shapes=[
                pltpu.VMEM((particles, length, length), jnp.bfloat16),
                pltpu.VMEM((2 * chunk_rows, length), jnp.bfloat16),
                pltpu.VMEM((2 * length, 2 * length), jnp.bfloat16),
                pltpu.VMEM((particles * chunk_rows, 2 * length), jnp.bfloat16),
                pltpu.VMEM(block_shape, jnp.bfloat16),
                pltpu.SemaphoreType.DMA((particles + 1,)),
                pltpu.SemaphoreType.DMA((particles // 2,)),
            ],
            compiler_params=pltpu.CompilerParams(vmem_limit_bytes=SPECTRUM_VMEM),
            cost_estimate=pl.CostEstimate(flops=0, bytes_accessed=0, transcendentals=0),
            name="spectrum",
        )(
            classes,
            shifts.T,
            defocus_class,
            defocus,
            run_counts.T,
            images,
            table_upper,
            *([digits] if last else []),
        )
        if c == 0:
            own_digits = meta_out[0]
        if c == 1:
            own_digits, send = lax.optimization_barrier((own_digits, send))
            layers = [own_digits]
            for step in range(1, slab_count):
                ring = [(s, (s + step) % slab_count) for s in range(slab_count)]
                layers.append(lax.ppermute(own_digits, "slab", ring))
            digits = jnp.concatenate([layer[:, : 2 * fields] for layer in layers], axis=1)
            digits = jnp.pad(digits, ((0, 0), (0, 2 * length - digits.shape[1])))
        if c > 0:
            send, received[-1] = lax.optimization_barrier((send, received[-1]))
        weighted.append(send)
        received.append(lax.all_to_all(send, "batch", 0, 0, tiled=True))

    def read_digits(rows_in):
        whole = rows_in.astype(jnp.int32).reshape(-1, 2 * fields)
        return whole[:, :fields] * META_BASE + whole[:, fields:]

    at = [particles * each for each in sizes]
    layer_digits = received[0][:, at[0] : at[0] + particles, : 2 * fields]
    meta_layer = read_digits(layer_digits)
    all_digits = received[-1][:, at[-1] : at[-1] + particles, : slab_count * 2 * fields]
    meta_all = read_digits(all_digits)

    class_count = dest_map.shape[0]

    dest_wide = dest_map.astype(jnp.bfloat16)

    def find_planes(table):
        class_hot = (table[:, :1] == jnp.arange(class_count)[None, :]).astype(jnp.bfloat16)
        local_plane = jnp.dot(class_hot, dest_wide, preferred_element_type=jnp.float32)
        past = freq[None, :, None] >= table[:, None, 2:]
        owner = jnp.sum(past.astype(jnp.int32), axis=2)
        return owner * planes + local_plane.astype(jnp.int32)

    def pick_block(table, block):
        return sum(
            jnp.where(block == k, table[:, k * rows : (k + 1) * rows], 0)
            for k in range(batch_count)
        )

    window_slabs = 3 if mirrored else slab_count
    blocks = [
        sum(jnp.where(batch == b, block, 0) for b, block in enumerate(role)) for role in roles
    ]
    layer_planes = find_planes(meta_layer)
    places, codes = [], []
    for c, each in enumerate(sizes):
        here = slice(starts[c], starts[c] + each)
        plane = pick_block(layer_planes, blocks[c])[:, here]
        place, owner_place = slab, plane // planes
        if mirrored:
            upper = blocks[c] >= half_batch
            owner_place = jnp.where(upper, slab_count - 1 - owner_place, owner_place)
            place = jnp.where(upper, slab_count - 1 - slab, slab)
        places.append(place)
        code = owner_place * (each * planes) + jnp.arange(each)[None, :] * planes
        code = (code + plane % planes).reshape(batch_count, particles * each)
        if c in (0, len(sizes) - 1):
            code = jnp.pad(code, ((0, 0), (0, META_ROWS)), constant_values=-1)
        codes.append(code.reshape(1, -1))

    sums, arrived = [], []
    for c, each in enumerate(sizes):
        bins = each * planes
        codes_in = codes[c]
        if c == 0:
            codes_in, _ = lax.optimization_barrier((codes_in, weighted[1:]))
        if c > 0 and mirrored:
            codes_in, arrived[c - 1][0], arrived[c - 1][2] = lax.optimization_barrier(
                (codes_in, arrived[c - 1][0], arrived[c - 1][2])
            )
        parts = pl.pallas_call(
            insert_kernel,
            out_shape=jax.ShapeDtypeStruct((window_slabs, bins, 2 * length), jnp.bfloat16),
            in_specs=whole_vmem(2),
            out_specs=pl.BlockSpec(memory_space=pltpu.VMEM),
            compiler_params=pltpu.CompilerParams(vmem_limit_bytes=INSERT_VMEM),
            cost_estimate=pl.CostEstimate(
                flops=0,
                bytes_accessed=0,
                transcendentals=0,
            ),
            name="insert",
        )(received[c], codes_in)
        if not mirrored:
            sums.append(lax.psum_scatter(parts, "slab", scatter_dimension=0, tiled=False))
            continue
        for before in arrived:
            before[1], _ = lax.optimization_barrier((before[1], parts))
        arrived.append(slab_exchange(parts, places[c], slab_count, roles[c]))
        own = choose(parts, places[c]).astype(jnp.float32)
        sums.append(jnp.where(places[c] == slab_count - 1, 0.0, own))
    for c, each in enumerate(sizes):
        if not mirrored:
            break
        for block in arrived[c]:
            sums[c] = sums[c] + block.astype(jnp.float32)
        over = [(b, block) for b, block in enumerate(roles[c]) if b != block]
        if over:
            if c + 1 < len(sizes):
                sums[c], arrived[c + 1][2] = lax.optimization_barrier(
                    (sums[c], arrived[c + 1][2])
                )
            handed = lax.ppermute(sums[c].astype(jnp.bfloat16), "batch", over)
            sums[c] = jnp.where(blocks[c] == batch, sums[c], handed.astype(jnp.float32))

    own_freq = batch * rows + jnp.arange(rows, dtype=jnp.int32)
    own_plane = pick_block(find_planes(meta_all), batch) - slab * planes
    focus_count = defocus.shape[0]
    focus_hot = (meta_all[:, 1:2] == jnp.arange(focus_count)[None, :]).astype(jnp.bfloat16)
    bin_hot = (own_plane.T[:, None, :] == jnp.arange(planes)[None, :, None]).astype(jnp.bfloat16)
    counts = jnp.einsum("kzp,pd->kzd", bin_hot, focus_hot, preferred_element_type=jnp.float32)
    row_angle = 2.0 * (
        defocus[None, :] * centred_square(own_freq, length)[:, None] + PHASE_OFFSET
    )
    col_angle = 2.0 * (defocus[:, None] * centred_square(freq, length)[None, :])
    row_side = jnp.concatenate(
        [counts * jnp.cos(row_angle)[:, None, :], counts * jnp.sin(row_angle)[:, None, :]], axis=2
    )
    col_side = jnp.concatenate([jnp.cos(col_angle), -jnp.sin(col_angle)], axis=0)
    double = jnp.einsum("kzd,dx->kzx", row_side, col_side, precision=lax.Precision.HIGHEST)
    weights = 0.5 * (jnp.sum(counts, axis=2, keepdims=True) - double)
    denom = weights + TAU_PRIOR

    updated = []
    for c, each in enumerate(sizes):
        here = slice(starts[c], starts[c] + each)
        prior = ref[here].astype(jnp.float32)
        under = denom[here]
        total = sums[c].astype(jnp.float32).reshape(each, planes, 2 * length)
        updated.append(
            (
                (TAU_PRIOR * prior + total) / jnp.concatenate([under, under], axis=2)
            ).astype(jnp.bfloat16)
        )
    return jnp.concatenate(updated, axis=0)


def solution(mesh):
    placed = (
        P(("batch", "slab"), None, None),
        P(("batch", "slab")),
        P(("batch", "slab"), None),
        P(("batch", "slab")),
        P(),
        P(("batch", "slab"), None),
        P(),
        P("batch", "slab", None),
    )
    return jax.shard_map(
        per_device, mesh=mesh, in_specs=placed, out_specs=P("batch", "slab", None), check_vma=False
    )
```

```python
import functools
import math

import jax
import jax.numpy as jnp
import numpy as np
from jax import lax
from jax.experimental import pallas as pl
from jax.experimental.pallas import tpu as pltpu
from jax.sharding import PartitionSpec as P

TAU_PRIOR = 4.0
PHASE_OFFSET = 0.1
CHUNKS = ((2, True), (2, True), (2, False))
SHARES = 6
META_BASE = 32
META_ROWS = 16
LANES = 128
SPECTRUM_VMEM = 60 * 1024 * 1024
INSERT_VMEM = 32 * 1024 * 1024


def dft_tables(length):
    index = np.arange(length, dtype=np.int32)
    turns = index[:, None] * index[None, :] % length
    angle = np.float32(2.0 * math.pi / length) * turns.astype(np.float32)
    factor = np.float32(1.0 / math.sqrt(length))
    cosine = np.cos(angle) * factor
    sine = np.sin(angle) * factor
    upper_rows = np.concatenate([cosine, -sine], axis=1)
    lower_rows = np.concatenate([sine, cosine], axis=1)
    table_right = np.concatenate([upper_rows, lower_rows], axis=0)
    return cosine, -sine, table_right


def spread(iota, values):
    out = jnp.full(iota.shape, values[0])
    for p in range(1, len(values)):
        out = jnp.where(iota == p, values[p], out)
    return out


def sin_turns(turns):
    half = jnp.floor(2.0 * turns + 0.5)
    x = (2.0 * math.pi) * (turns - 0.5 * half)
    sign = 1.0 - 2.0 * (half - 2.0 * jnp.floor(0.5 * half))
    square = x * x
    series = jnp.full(x.shape, -1.0 / math.factorial(11), jnp.float32)
    for power in (9, 7, 5, 3, 1):
        series = series * square + (1.0 if power % 4 == 1 else -1.0) / math.factorial(power)
    return sign * x * series


def phase_turns(freq, shift, length):
    steps = freq * shift
    steps = steps - length * jnp.floor(steps * (1.0 / length))
    return steps * (1.0 / length)


def centred(freq, length):
    return jnp.where(freq < length // 2, freq, freq - length) * (1.0 / length)


def spectrum_kernel(runs, meta_from, *refs):
    classes, shifts, defocus_class, defocus, run_counts, images_in, left_in, right_in, *refs = refs
    if meta_from == "operand":
        meta_in, *refs = refs
    out, *refs = refs
    if meta_from == "scalars":
        meta_out, *refs = refs
    images, left, right, joined, block, load_sems, send_sems = refs
    particles, length = images.shape[0], images.shape[1]
    owners = out.shape[0]
    rows_each = runs[0][1] - runs[0][0]
    rows = owners * rows_each
    loads = [pltpu.make_async_copy(left_in, left, load_sems.at[0])]
    for p in range(particles):
        loads.append(pltpu.make_async_copy(images_in.at[p], images.at[p], load_sems.at[1 + p]))
    loads.append(pltpu.make_async_copy(right_in, right, load_sems.at[1 + particles]))
    for load in loads:
        load.start()

    every = range(particles)
    focus = [defocus[defocus_class[p]] for p in every]
    shift_x = [shifts[0, p].astype(jnp.float32) for p in every]
    shift_y = [shifts[1, p].astype(jnp.float32) for p in every]
    sublane = lax.broadcasted_iota(jnp.int32, (particles, length), 0)
    freq_x = lax.broadcasted_iota(jnp.int32, (particles, length), 1).astype(jnp.float32)
    phase_x = phase_turns(freq_x, spread(sublane, shift_x), length)
    angle_x = spread(sublane, focus) * centred(freq_x, length) * centred(freq_x, length)
    angle_x = angle_x * (0.5 / math.pi)
    col = [sin_turns(at) for at in (phase_x, phase_x + 0.25, angle_x, angle_x + 0.25)]
    lane = lax.broadcasted_iota(jnp.int32, (rows, LANES), 1)
    which = lane & (particles - 1)
    quantity = (lane - which) * (1.0 / particles)
    row_at = lax.broadcasted_iota(jnp.int32, (rows, LANES), 0)
    freq_y = row_at + runs[0][0]
    for d in range(1, owners):
        freq_y = jnp.where(row_at >= d * rows_each, row_at + (runs[d][0] - d * rows_each), freq_y)
    freq_y = freq_y.astype(jnp.float32)
    phase_y = phase_turns(freq_y, spread(which, shift_y), length)
    angle_y = spread(which, focus) * centred(freq_y, length) * centred(freq_y, length)
    angle_y = (angle_y + PHASE_OFFSET) * (0.5 / math.pi)
    row = jnp.where(quantity < 2.0, phase_y, angle_y)
    row = sin_turns(row + jnp.where((quantity == 1.0) | (quantity == 3.0), 0.25, 0.0))

    if meta_from == "operand":
        for d in range(owners):
            block[d, particles * rows_each :, :] = meta_in[...]
    if meta_from == "scalars":
        digits = jnp.zeros((META_ROWS, LANES), jnp.int32)
        at_row = lax.broadcasted_iota(jnp.int32, (META_ROWS, LANES), 0)
        at_row = at_row & (particles - 1)
        at_lane = lax.broadcasted_iota(jnp.int32, (META_ROWS, LANES), 1)
        ends = [[run_counts[0, p] for p in every]]
        for s in range(1, run_counts.shape[0] - 1):
            ends.append([ends[-1][p] + run_counts[s, p] for p in every])
        fields = [[classes[p] for p in every], [defocus_class[p] for p in every], *ends]
        for f, values in enumerate(fields):
            value = spread(at_row, values)
            digits = jnp.where(at_lane == f, value // META_BASE, digits)
            digits = jnp.where(at_lane == f + len(fields), value % META_BASE, digits)
        digits = digits.astype(jnp.float32).astype(jnp.bfloat16)
        meta_out[...] = digits
        for d in range(owners):
            block[d, particles * rows_each :, :] = jnp.zeros(
                (META_ROWS, 2 * length), jnp.bfloat16
            )
            block[d, particles * rows_each :, :LANES] = digits

    loads[0].wait()
    table = left[...]
    for p in range(particles):
        loads[1 + p].wait()
        section = jnp.dot(table, images[p], preferred_element_type=jnp.float32)
        section = section.astype(jnp.bfloat16)
        joined[p * rows : (p + 1) * rows, :length] = section[:rows]
        joined[p * rows : (p + 1) * rows, length:] = section[rows:]
    loads[1 + particles].wait()
    sends = []
    for first in range(0, particles, 2):
        spectrum = jnp.dot(
            joined[first * rows : (first + 2) * rows, :],
            right[...],
            preferred_element_type=jnp.float32,
        )
        for p in range(first, first + 2):
            part = spectrum[(p - first) * rows : (p - first + 1) * rows]
            real_part, imag_part = part[:, :length], part[:, length:]
            row_sin, row_cos, row_ctf_sin, row_ctf_cos = [
                row[:, q * particles + p : q * particles + p + 1] for q in range(4)
            ]
            col_sin, col_cos, col_ctf_sin, col_ctf_cos = [part[p : p + 1, :] for part in col]
            transfer = -(row_ctf_sin * col_ctf_cos + row_ctf_cos * col_ctf_sin)
            cosine = transfer * (row_cos * col_cos - row_sin * col_sin)
            sine = transfer * (row_sin * col_cos + row_cos * col_sin)
            real_new = real_part * cosine + imag_part * sine
            imag_new = imag_part * cosine - real_part * sine
            weighted = jnp.concatenate([real_new, imag_new], axis=1).astype(jnp.bfloat16)
            block[:, p * rows_each : (p + 1) * rows_each, :] = weighted.reshape(
                owners, rows_each, 2 * length
            )
        done = pl.ds(first * rows_each, 2 * rows_each)
        if meta_from and first + 2 == particles:
            done = pl.ds(first * rows_each, 2 * rows_each + META_ROWS)
        sends.append(
            pltpu.make_async_copy(block.at[:, done], out.at[:, done], send_sems.at[first // 2])
        )
        sends[-1].start()
    for send in sends:
        send.wait()


def insert_kernel(received, codes, out):
    windows, bins, _ = out.shape
    rows = received[...].reshape(-1, received.shape[2])
    codes_all = codes[...]
    for k in range(windows):
        bin_index = lax.broadcasted_iota(jnp.int32, (bins, 1), 0) + k * bins
        hot = jnp.where(codes_all == bin_index, 1.0, 0.0).astype(jnp.bfloat16)
        total = jnp.dot(hot, rows, preferred_element_type=jnp.float32)
        out[k] = total.astype(out.dtype)


def whole_vmem(count):
    return [pl.BlockSpec(memory_space=pltpu.VMEM)] * count


def centred_square(freq, length):
    half_length = length // 2
    value = ((freq + half_length) % length - half_length).astype(jnp.float32) / length
    return value * value


def slab_roles(batch_count, swapped):
    roles = list(range(batch_count))
    half = batch_count // 2
    if swapped:
        for b in range(1, half, 2):
            roles[b], roles[half + b - 1] = half + b - 1, b
    return roles


def slab_exchange(parts, place, slab_count, roles):
    arrived = []
    for shift in range(1, slab_count):
        perm = []
        for b, role in enumerate(roles):
            upper = role >= len(roles) // 2
            for source in range(slab_count):
                target = (source + shift) % slab_count
                if target < slab_count - 1:
                    ends = (slab_count - 1 - source, slab_count - 1 - target)
                    ends = ends if upper else (source, target)
                    perm.append((b * slab_count + ends[0], b * slab_count + ends[1]))
        block = choose(parts, (place + shift) % slab_count)
        arrived.append(lax.ppermute(block, ("batch", "slab"), perm))
    return arrived


def choose(parts, index):
    chosen = parts[-1]
    for d in range(parts.shape[0] - 1):
        chosen = jnp.where(index == d, parts[d], chosen)
    return chosen


def per_device(images, classes, shifts, defocus_class, defocus, run_counts, dest_map, ref):
    particles, length, _ = images.shape
    batch_count = lax.axis_size("batch")
    slab_count = lax.axis_size("slab")
    batch = lax.axis_index("batch")
    slab = lax.axis_index("slab")
    rows, planes, _ = ref.shape
    mirrored = slab_count == 4 and batch_count % 2 == 0
    half_batch = batch_count // 2
    sizes = [rows * share // SHARES for share, _ in CHUNKS]
    starts = [sum(sizes[:c]) for c in range(len(CHUNKS))]
    roles = [slab_roles(batch_count, mirrored and swapped) for _, swapped in CHUNKS]
    freq = jnp.arange(length, dtype=jnp.int32)

    fields = slab_count + 1

    cosine, minus_sine, table_right = dft_tables(length)
    table_right = jnp.asarray(table_right.astype(jnp.bfloat16))
    weighted = []
    for c, each in enumerate(sizes):
        chunk_rows = batch_count * each
        block = np.array(roles[c])
        order = (block[:, None] * rows + starts[c] + np.arange(each)[None, :]).reshape(-1)
        left = np.concatenate([cosine[order], minus_sine[order]], axis=0)
        runs = [(k * rows + starts[c], k * rows + starts[c] + each) for k in block.tolist()]
        last = c + 1 == len(sizes)
        meta_from = "scalars" if c == 0 else "operand" if last else None
        block_rows = particles * each + (META_ROWS if meta_from else 0)
        block_shape = (batch_count, block_rows, 2 * length)
        smem = pl.BlockSpec(memory_space=pltpu.SMEM)
        hbm = pl.BlockSpec(memory_space=pltpu.HBM)
        vmem = pl.BlockSpec(memory_space=pltpu.VMEM)
        send, *meta_out = pl.pallas_call(
            functools.partial(spectrum_kernel, runs, meta_from),
            out_shape=[jax.ShapeDtypeStruct(block_shape, jnp.bfloat16)]
            + [jax.ShapeDtypeStruct((META_ROWS, LANES), jnp.bfloat16)] * (c == 0),
            in_specs=[smem] * 5 + [hbm] * 3 + [vmem] * last,
            out_specs=[hbm] + [vmem] * (c == 0),
            scratch_shapes=[
                pltpu.VMEM((particles, length, length), jnp.bfloat16),
                pltpu.VMEM((2 * chunk_rows, length), jnp.bfloat16),
                pltpu.VMEM((2 * length, 2 * length), jnp.bfloat16),
                pltpu.VMEM((particles * chunk_rows, 2 * length), jnp.bfloat16),
                pltpu.VMEM(block_shape, jnp.bfloat16),
                pltpu.SemaphoreType.DMA((particles + 2,)),
                pltpu.SemaphoreType.DMA((particles // 2,)),
            ],
            compiler_params=pltpu.CompilerParams(vmem_limit_bytes=SPECTRUM_VMEM),
            cost_estimate=pl.CostEstimate(flops=0, bytes_accessed=0, transcendentals=0),
            name="spectrum",
        )(
            classes,
            shifts.T,
            defocus_class,
            defocus,
            run_counts.T,
            images,
            jnp.asarray(left.astype(jnp.bfloat16)),
            table_right,
            *([digits] if last else []),
        )
        if c == 0:
            own_digits = meta_out[0]
        if c == 1:
            own_digits, send = lax.optimization_barrier((own_digits, send))
            layers = [own_digits]
            for step in range(1, slab_count):
                ring = [(s, (s + step) % slab_count) for s in range(slab_count)]
                layers.append(lax.ppermute(own_digits, "slab", ring))
            digits = jnp.concatenate([layer[:, : 2 * fields] for layer in layers], axis=1)
            digits = jnp.pad(digits, ((0, 0), (0, 2 * length - digits.shape[1])))
        weighted.append(send)

    def exchange(send, behind):
        send, behind = lax.optimization_barrier((send, behind))
        return lax.all_to_all(send, "batch", 0, 0, tiled=True), behind

    first = lax.all_to_all(weighted[0], "batch", 0, 0, tiled=True)
    second, first = exchange(weighted[1], first)
    received = [first, second]

    def read_digits(rows_in):
        whole = rows_in.astype(jnp.int32).reshape(-1, 2 * fields)
        return whole[:, :fields] * META_BASE + whole[:, fields:]

    at = [particles * each for each in sizes]
    layer_digits = received[0][:, at[0] : at[0] + particles, : 2 * fields]
    meta_layer = read_digits(layer_digits)

    class_count = dest_map.shape[0]

    dest_wide = dest_map.astype(jnp.bfloat16)

    def find_planes(table):
        class_hot = (table[:, :1] == jnp.arange(class_count)[None, :]).astype(jnp.bfloat16)
        local_plane = jnp.dot(class_hot, dest_wide, preferred_element_type=jnp.float32)
        past = freq[None, :, None] >= table[:, None, 2:]
        owner = jnp.sum(past.astype(jnp.int32), axis=2)
        return owner * planes + local_plane.astype(jnp.int32)

    def pick_block(table, block):
        return sum(
            jnp.where(block == k, table[:, k * rows : (k + 1) * rows], 0)
            for k in range(batch_count)
        )

    window_slabs = 3 if mirrored else slab_count
    blocks = [
        sum(jnp.where(batch == b, block, 0) for b, block in enumerate(role)) for role in roles
    ]
    layer_planes = find_planes(meta_layer)
    places, codes = [], []
    for c, each in enumerate(sizes):
        here = slice(starts[c], starts[c] + each)
        plane = pick_block(layer_planes, blocks[c])[:, here]
        place, owner_place = slab, plane // planes
        if mirrored:
            upper = blocks[c] >= half_batch
            owner_place = jnp.where(upper, slab_count - 1 - owner_place, owner_place)
            place = jnp.where(upper, slab_count - 1 - slab, slab)
        places.append(place)
        code = owner_place * (each * planes) + jnp.arange(each)[None, :] * planes
        code = (code + plane % planes).reshape(batch_count, particles * each)
        if c in (0, len(sizes) - 1):
            code = jnp.pad(code, ((0, 0), (0, META_ROWS)), constant_values=-1)
        codes.append(code.reshape(1, -1))

    sums, arrived = [], []
    for c, each in enumerate(sizes):
        bins = each * planes
        codes_in = codes[c]
        if c == 0:
            codes_in, _ = lax.optimization_barrier((codes_in, weighted[1:]))
        if c > 0 and mirrored:
            codes_in, arrived[c - 1][0], arrived[c - 1][2] = lax.optimization_barrier(
                (codes_in, arrived[c - 1][0], arrived[c - 1][2])
            )
        parts = pl.pallas_call(
            insert_kernel,
            out_shape=jax.ShapeDtypeStruct((window_slabs, bins, 2 * length), jnp.bfloat16),
            in_specs=whole_vmem(2),
            out_specs=pl.BlockSpec(memory_space=pltpu.VMEM),
            compiler_params=pltpu.CompilerParams(vmem_limit_bytes=INSERT_VMEM),
            cost_estimate=pl.CostEstimate(
                flops=0,
                bytes_accessed=0,
                transcendentals=0,
            ),
            name="insert",
        )(received[c], codes_in)
        if not mirrored:
            sums.append(lax.psum_scatter(parts, "slab", scatter_dimension=0, tiled=False))
            if c + 2 < len(sizes):
                received.append(lax.all_to_all(weighted[c + 2], "batch", 0, 0, tiled=True))
            continue
        for before in arrived:
            before[1], _ = lax.optimization_barrier((before[1], parts))
        arrived.append(slab_exchange(parts, places[c], slab_count, roles[c]))
        if c + 2 < len(sizes):
            third, arrived[c][2] = exchange(weighted[c + 2], arrived[c][2])
            received.append(third)
        own = choose(parts, places[c]).astype(jnp.float32)
        sums.append(jnp.where(places[c] == slab_count - 1, 0.0, own))
    for c, each in enumerate(sizes):
        if not mirrored:
            break
        for block in arrived[c]:
            sums[c] = sums[c] + block.astype(jnp.float32)
        over = [(b, block) for b, block in enumerate(roles[c]) if b != block]
        if over:
            if c + 1 < len(sizes):
                sums[c], arrived[-1][2] = lax.optimization_barrier((sums[c], arrived[-1][2]))
            handed = lax.ppermute(sums[c].astype(jnp.bfloat16), "batch", over)
            sums[c] = jnp.where(blocks[c] == batch, sums[c], handed.astype(jnp.float32))

    all_digits = received[-1][:, at[-1] : at[-1] + particles, : slab_count * 2 * fields]
    meta_all = read_digits(all_digits)

    own_freq = batch * rows + jnp.arange(rows, dtype=jnp.int32)
    own_plane = pick_block(find_planes(meta_all), batch) - slab * planes
    focus_count = defocus.shape[0]
    focus_hot = (meta_all[:, 1:2] == jnp.arange(focus_count)[None, :]).astype(jnp.bfloat16)
    bin_hot = (own_plane.T[:, None, :] == jnp.arange(planes)[None, :, None]).astype(jnp.bfloat16)
    counts = jnp.einsum("kzp,pd->kzd", bin_hot, focus_hot, preferred_element_type=jnp.float32)
    row_angle = 2.0 * (
        defocus[None, :] * centred_square(own_freq, length)[:, None] + PHASE_OFFSET
    )
    col_angle = 2.0 * (defocus[:, None] * centred_square(freq, length)[None, :])
    row_side = jnp.concatenate(
        [counts * jnp.cos(row_angle)[:, None, :], counts * jnp.sin(row_angle)[:, None, :]], axis=2
    )
    col_side = jnp.concatenate([jnp.cos(col_angle), -jnp.sin(col_angle)], axis=0)
    double = jnp.einsum("kzd,dx->kzx", row_side, col_side, precision=lax.Precision.HIGHEST)
    weights = 0.5 * (jnp.sum(counts, axis=2, keepdims=True) - double)
    denom = weights + TAU_PRIOR

    updated = []
    for c, each in enumerate(sizes):
        here = slice(starts[c], starts[c] + each)
        prior = ref[here].astype(jnp.float32)
        under = denom[here]
        total = sums[c].astype(jnp.float32).reshape(each, planes, 2 * length)
        updated.append(
            (
                (TAU_PRIOR * prior + total) / jnp.concatenate([under, under], axis=2)
            ).astype(jnp.bfloat16)
        )
    return jnp.concatenate(updated, axis=0)


def solution(mesh):
    placed = (
        P(("batch", "slab"), None, None),
        P(("batch", "slab")),
        P(("batch", "slab"), None),
        P(("batch", "slab")),
        P(),
        P(("batch", "slab"), None),
        P(),
        P("batch", "slab", None),
    )
    return jax.shard_map(
        per_device, mesh=mesh, in_specs=placed, out_specs=P("batch", "slab", None), check_vma=False
    )
```

```python
import functools
import math

import jax
import jax.numpy as jnp
import numpy as np
from jax import lax
from jax.experimental import pallas as pl
from jax.experimental.pallas import tpu as pltpu
from jax.sharding import PartitionSpec as P

TAU_PRIOR = 4.0
PHASE_OFFSET = 0.1
CHUNKS = ((2, False), (2, True), (2, False))
SHARES = 6
META_BASE = 32
META_ROWS = 16
LANES = 128
SPECTRUM_VMEM = 60 * 1024 * 1024
INSERT_VMEM = 32 * 1024 * 1024


def dft_tables(length):
    index = np.arange(length, dtype=np.int32)
    turns = index[:, None] * index[None, :] % length
    angle = np.float32(2.0 * math.pi / length) * turns.astype(np.float32)
    factor = np.float32(1.0 / math.sqrt(length))
    cosine = np.cos(angle) * factor
    sine = np.sin(angle) * factor
    upper_rows = np.concatenate([cosine, -sine], axis=1)
    lower_rows = np.concatenate([sine, cosine], axis=1)
    table_right = np.concatenate([upper_rows, lower_rows], axis=0)
    return cosine, -sine, table_right


def spread(iota, values):
    out = jnp.full(iota.shape, values[0])
    for p in range(1, len(values)):
        out = jnp.where(iota == p, values[p], out)
    return out


def sin_turns(turns):
    half = jnp.floor(2.0 * turns + 0.5)
    x = (2.0 * math.pi) * (turns - 0.5 * half)
    sign = 1.0 - 2.0 * (half - 2.0 * jnp.floor(0.5 * half))
    square = x * x
    series = jnp.full(x.shape, -1.0 / math.factorial(11), jnp.float32)
    for power in (9, 7, 5, 3, 1):
        series = series * square + (1.0 if power % 4 == 1 else -1.0) / math.factorial(power)
    return sign * x * series


def phase_turns(freq, shift, length):
    steps = freq * shift
    steps = steps - length * jnp.floor(steps * (1.0 / length))
    return steps * (1.0 / length)


def centred(freq, length):
    return jnp.where(freq < length // 2, freq, freq - length) * (1.0 / length)


def spectrum_kernel(
    runs,
    with_meta,
    classes,
    shifts,
    defocus_class,
    defocus,
    run_counts,
    images_in,
    left_in,
    right_in,
    out,
    images,
    left,
    right,
    joined,
    block,
    load_sems,
    send_sems,
):
    particles, length = images.shape[0], images.shape[1]
    owners = out.shape[0]
    rows_each = runs[0][1] - runs[0][0]
    rows = owners * rows_each
    loads = [pltpu.make_async_copy(left_in, left, load_sems.at[0])]
    for p in range(particles):
        loads.append(pltpu.make_async_copy(images_in.at[p], images.at[p], load_sems.at[1 + p]))
    loads.append(pltpu.make_async_copy(right_in, right, load_sems.at[1 + particles]))
    for load in loads:
        load.start()

    every = range(particles)
    focus = [defocus[defocus_class[p]] for p in every]
    shift_x = [shifts[0, p].astype(jnp.float32) for p in every]
    shift_y = [shifts[1, p].astype(jnp.float32) for p in every]
    sublane = lax.broadcasted_iota(jnp.int32, (particles, length), 0)
    freq_x = lax.broadcasted_iota(jnp.int32, (particles, length), 1).astype(jnp.float32)
    phase_x = phase_turns(freq_x, spread(sublane, shift_x), length)
    angle_x = spread(sublane, focus) * centred(freq_x, length) * centred(freq_x, length)
    angle_x = angle_x * (0.5 / math.pi)
    col = [sin_turns(at) for at in (phase_x, phase_x + 0.25, angle_x, angle_x + 0.25)]
    lane = lax.broadcasted_iota(jnp.int32, (rows, LANES), 1)
    which = lane % particles
    quantity = lane // particles
    row_at = lax.broadcasted_iota(jnp.int32, (rows, LANES), 0)
    owner = row_at // rows_each
    freq_y = row_at - owner * rows_each + spread(owner, [begin for begin, _ in runs])
    freq_y = freq_y.astype(jnp.float32)
    phase_y = phase_turns(freq_y, spread(which, shift_y), length)
    angle_y = spread(which, focus) * centred(freq_y, length) * centred(freq_y, length)
    angle_y = (angle_y + PHASE_OFFSET) * (0.5 / math.pi)
    row = jnp.where(quantity < 2, phase_y, angle_y)
    row = sin_turns(row + jnp.where(quantity % 2 == 1, 0.25, 0.0))

    if with_meta:
        digits = jnp.zeros((META_ROWS, LANES), jnp.int32)
        at_row = lax.broadcasted_iota(jnp.int32, (META_ROWS, LANES), 0) % particles
        at_lane = lax.broadcasted_iota(jnp.int32, (META_ROWS, LANES), 1)
        ends = [[run_counts[0, p] for p in every]]
        for s in range(1, run_counts.shape[0] - 1):
            ends.append([ends[-1][p] + run_counts[s, p] for p in every])
        fields = [[classes[p] for p in every], [defocus_class[p] for p in every], *ends]
        for f, values in enumerate(fields):
            value = spread(at_row, values)
            digits = jnp.where(at_lane == f, value // META_BASE, digits)
            digits = jnp.where(at_lane == f + len(fields), value % META_BASE, digits)
        digits = digits.astype(jnp.float32).astype(jnp.bfloat16)
        for d in range(owners):
            block[d, particles * rows_each :, :] = jnp.zeros(
                (META_ROWS, 2 * length), jnp.bfloat16
            )
            block[d, particles * rows_each :, :LANES] = digits

    loads[0].wait()
    table = left[...]
    for p in range(particles):
        loads[1 + p].wait()
        section = jnp.dot(table, images[p], preferred_element_type=jnp.float32)
        section = section.astype(jnp.bfloat16)
        joined[p * rows : (p + 1) * rows, :length] = section[:rows]
        joined[p * rows : (p + 1) * rows, length:] = section[rows:]
    loads[1 + particles].wait()
    sends = []
    for first in range(0, particles, 2):
        spectrum = jnp.dot(
            joined[first * rows : (first + 2) * rows, :],
            right[...],
            preferred_element_type=jnp.float32,
        )
        for p in range(first, first + 2):
            part = spectrum[(p - first) * rows : (p - first + 1) * rows]
            real_part, imag_part = part[:, :length], part[:, length:]
            row_sin, row_cos, row_ctf_sin, row_ctf_cos = [
                row[:, q * particles + p : q * particles + p + 1] for q in range(4)
            ]
            col_sin, col_cos, col_ctf_sin, col_ctf_cos = [part[p : p + 1, :] for part in col]
            transfer = -(row_ctf_sin * col_ctf_cos + row_ctf_cos * col_ctf_sin)
            cosine = transfer * (row_cos * col_cos - row_sin * col_sin)
            sine = transfer * (row_sin * col_cos + row_cos * col_sin)
            real_new = real_part * cosine + imag_part * sine
            imag_new = imag_part * cosine - real_part * sine
            weighted = jnp.concatenate([real_new, imag_new], axis=1).astype(jnp.bfloat16)
            block[:, p * rows_each : (p + 1) * rows_each, :] = weighted.reshape(
                owners, rows_each, 2 * length
            )
        done = pl.ds(first * rows_each, 2 * rows_each)
        if with_meta and first + 2 == particles:
            done = pl.ds(first * rows_each, 2 * rows_each + META_ROWS)
        sends.append(
            pltpu.make_async_copy(block.at[:, done], out.at[:, done], send_sems.at[first // 2])
        )
        sends[-1].start()
    for send in sends:
        send.wait()


def insert_kernel(bins, meta_at, received, codes, out):
    sources = received.shape[0]
    rows = received[...].reshape(-1, received.shape[2])
    codes_all = codes[...]
    for k in range(out.shape[0]):
        bin_index = lax.broadcasted_iota(jnp.int32, (bins, 1), 0) + k * bins
        hot = jnp.where(codes_all == bin_index, 1.0, 0.0).astype(jnp.bfloat16)
        total = jnp.dot(hot, rows, preferred_element_type=jnp.float32)
        out[k, :bins, :] = total.astype(out.dtype)
        if out.shape[1] > bins:
            tiles = out.shape[2] // LANES
            first_half = lax.broadcasted_iota(jnp.int32, (META_ROWS, LANES), 0) < META_ROWS // 2
            for i in range(min(sources, tiles)):
                low = received[i, meta_at : meta_at + META_ROWS, :LANES]
                if i + tiles < sources:
                    high = received[i + tiles, meta_at : meta_at + META_ROWS, :LANES]
                    low = jnp.where(
                        first_half, low.astype(jnp.float32), high.astype(jnp.float32)
                    ).astype(low.dtype)
                out[k, bins:, i * LANES : (i + 1) * LANES] = low


def whole_vmem(count):
    return [pl.BlockSpec(memory_space=pltpu.VMEM)] * count


def centred_square(freq, length):
    half_length = length // 2
    value = ((freq + half_length) % length - half_length).astype(jnp.float32) / length
    return value * value


def slab_roles(batch_count, swapped):
    roles = list(range(batch_count))
    half = batch_count // 2
    if swapped:
        for b in range(1, half, 2):
            roles[b], roles[half + b - 1] = half + b - 1, b
    return roles


def slab_exchange(parts, place, slab_count, roles):
    arrived = []
    for shift in range(1, slab_count):
        perm = []
        for b, role in enumerate(roles):
            upper = role >= len(roles) // 2
            for source in range(slab_count):
                target = (source + shift) % slab_count
                if target < slab_count - 1:
                    ends = (slab_count - 1 - source, slab_count - 1 - target)
                    ends = ends if upper else (source, target)
                    perm.append((b * slab_count + ends[0], b * slab_count + ends[1]))
        block = choose(parts, (place + shift) % slab_count)
        arrived.append(lax.ppermute(block, ("batch", "slab"), perm))
    return arrived


def choose(parts, index):
    chosen = parts[-1]
    for d in range(parts.shape[0] - 1):
        chosen = jnp.where(index == d, parts[d], chosen)
    return chosen


def per_device(images, classes, shifts, defocus_class, defocus, run_counts, dest_map, ref):
    particles, length, _ = images.shape
    batch_count = lax.axis_size("batch")
    slab_count = lax.axis_size("slab")
    batch = lax.axis_index("batch")
    slab = lax.axis_index("slab")
    rows, planes, _ = ref.shape
    mirrored = slab_count == 4 and batch_count % 2 == 0 and 2 * particles <= META_ROWS
    mirrored = mirrored and batch_count * LANES <= 4 * length
    half_batch = batch_count // 2
    sizes = [rows * share // SHARES for share, _ in CHUNKS]
    starts = [sum(sizes[:c]) for c in range(len(CHUNKS))]
    roles = [slab_roles(batch_count, mirrored and swapped) for _, swapped in CHUNKS]
    freq = jnp.arange(length, dtype=jnp.int32)

    fields = slab_count + 1

    cosine, minus_sine, table_right = dft_tables(length)
    table_right = jnp.asarray(table_right.astype(jnp.bfloat16))
    received = []
    weighted = []
    for c, each in enumerate(sizes):
        chunk_rows = batch_count * each
        block = np.array(roles[c])
        order = (block[:, None] * rows + starts[c] + np.arange(each)[None, :]).reshape(-1)
        left = np.concatenate([cosine[order], minus_sine[order]], axis=0)
        runs = [(k * rows + starts[c], k * rows + starts[c] + each) for k in block.tolist()]
        with_meta = c == 0
        block_rows = particles * each + META_ROWS * with_meta
        block_shape = (batch_count, block_rows, 2 * length)
        smem = pl.BlockSpec(memory_space=pltpu.SMEM)
        hbm = pl.BlockSpec(memory_space=pltpu.HBM)
        send = pl.pallas_call(
            functools.partial(spectrum_kernel, runs, with_meta),
            out_shape=jax.ShapeDtypeStruct(block_shape, jnp.bfloat16),
            in_specs=[smem] * 5 + [hbm] * 3,
            out_specs=hbm,
            scratch_shapes=[
                pltpu.VMEM((particles, length, length), jnp.bfloat16),
                pltpu.VMEM((2 * chunk_rows, length), jnp.bfloat16),
                pltpu.VMEM((2 * length, 2 * length), jnp.bfloat16),
                pltpu.VMEM((particles * chunk_rows, 2 * length), jnp.bfloat16),
                pltpu.VMEM(block_shape, jnp.bfloat16),
                pltpu.SemaphoreType.DMA((particles + 2,)),
                pltpu.SemaphoreType.DMA((particles // 2,)),
            ],
            compiler_params=pltpu.CompilerParams(vmem_limit_bytes=SPECTRUM_VMEM),
            cost_estimate=pl.CostEstimate(flops=0, bytes_accessed=0, transcendentals=0),
            name="spectrum",
        )(
            classes,
            shifts.T,
            defocus_class,
            defocus,
            run_counts.T,
            images,
            jnp.asarray(left.astype(jnp.bfloat16)),
            table_right,
        )
        weighted.append(send)
        received.append(lax.all_to_all(send, "batch", 0, 0, tiled=True))

    def read_digits(rows_in):
        whole = rows_in.astype(jnp.int32).reshape(-1, 2 * fields)
        return whole[:, :fields] * META_BASE + whole[:, fields:]

    meta_at = particles * sizes[0]
    meta_layer = read_digits(received[0][:, meta_at : meta_at + particles, : 2 * fields])

    class_count = dest_map.shape[0]

    dest_wide = dest_map.astype(jnp.bfloat16)

    def find_planes(table):
        class_hot = (table[:, :1] == jnp.arange(class_count)[None, :]).astype(jnp.bfloat16)
        local_plane = jnp.dot(class_hot, dest_wide, preferred_element_type=jnp.float32)
        past = freq[None, :, None] >= table[:, None, 2:]
        owner = jnp.sum(past.astype(jnp.int32), axis=2)
        return owner * planes + local_plane.astype(jnp.int32)

    def pick_block(table, block):
        return sum(
            jnp.where(block == k, table[:, k * rows : (k + 1) * rows], 0)
            for k in range(batch_count)
        )

    window_slabs = 3 if mirrored else slab_count
    blocks = [
        sum(jnp.where(batch == b, block, 0) for b, block in enumerate(role)) for role in roles
    ]
    layer_planes = find_planes(meta_layer)
    places, codes = [], []
    for c, each in enumerate(sizes):
        here = slice(starts[c], starts[c] + each)
        plane = pick_block(layer_planes, blocks[c])[:, here]
        place, owner_place = slab, plane // planes
        if mirrored:
            upper = blocks[c] >= half_batch
            owner_place = jnp.where(upper, slab_count - 1 - owner_place, owner_place)
            place = jnp.where(upper, slab_count - 1 - slab, slab)
        places.append(place)
        code = owner_place * (each * planes) + jnp.arange(each)[None, :] * planes
        code = (code + plane % planes).reshape(batch_count, particles * each)
        if c == 0:
            code = jnp.pad(code, ((0, 0), (0, META_ROWS)), constant_values=-1)
        codes.append(code.reshape(1, -1))

    sums, arrived = [], []
    for c, each in enumerate(sizes):
        bins = each * planes
        extra_rows = META_ROWS if c == 0 and mirrored else 0
        codes_in = codes[c]
        if c == 0:
            codes_in, _ = lax.optimization_barrier((codes_in, weighted[1:]))
        if c > 0 and mirrored:
            codes_in, arrived[c - 1][2] = lax.optimization_barrier((codes_in, arrived[c - 1][2]))
        parts = pl.pallas_call(
            functools.partial(insert_kernel, bins, meta_at),
            out_shape=jax.ShapeDtypeStruct(
                (window_slabs, bins + extra_rows, 2 * length), jnp.bfloat16
            ),
            in_specs=whole_vmem(2),
            out_specs=pl.BlockSpec(memory_space=pltpu.VMEM),
            compiler_params=pltpu.CompilerParams(vmem_limit_bytes=INSERT_VMEM),
            cost_estimate=pl.CostEstimate(
                flops=0,
                bytes_accessed=0,
                transcendentals=0,
            ),
            name="insert",
        )(received[c], codes_in)
        if not mirrored:
            sums.append(lax.psum_scatter(parts, "slab", scatter_dimension=0, tiled=False))
            continue
        for before in arrived:
            before[1], _ = lax.optimization_barrier((before[1], parts))
        arrived.append(slab_exchange(parts, places[c], slab_count, roles[c]))
        own = choose(parts[:, :bins], places[c]).astype(jnp.float32)
        sums.append(jnp.where(places[c] == slab_count - 1, 0.0, own))
    for c, each in enumerate(sizes):
        if not mirrored:
            break
        for block in arrived[c]:
            sums[c] = sums[c] + block[: each * planes].astype(jnp.float32)
        over = [(b, block) for b, block in enumerate(roles[c]) if b != block]
        if over:
            if c + 1 < len(sizes):
                sums[c], arrived[c + 1][2] = lax.optimization_barrier(
                    (sums[c], arrived[c + 1][2])
                )
            handed = lax.ppermute(sums[c].astype(jnp.bfloat16), "batch", over)
            sums[c] = jnp.where(blocks[c] == batch, sums[c], handed.astype(jnp.float32))

    meta_all = [meta_layer]
    if mirrored:
        for block in [block[sizes[0] * planes :] for block in arrived[0]]:
            block = block.reshape(META_ROWS, -1, LANES)
            halves = (block[:particles], block[particles : 2 * particles])
            low = jnp.concatenate(halves, axis=1)[:, :batch_count, : 2 * fields]
            meta_all.append(read_digits(low.transpose(1, 0, 2)))
    else:
        for step in range(1, slab_count):
            ring = [(s, (s + step) % slab_count) for s in range(slab_count)]
            meta_all.append(lax.ppermute(meta_layer, "slab", ring))
    meta_all = jnp.concatenate(meta_all, axis=0)

    own_freq = batch * rows + jnp.arange(rows, dtype=jnp.int32)
    own_plane = pick_block(find_planes(meta_all), batch) - slab * planes
    focus_count = defocus.shape[0]
    focus_hot = (meta_all[:, 1:2] == jnp.arange(focus_count)[None, :]).astype(jnp.bfloat16)
    if mirrored:
        own_plane = jnp.where(places[0] == slab_count - 1, -1, own_plane)
    bin_hot = (own_plane.T[:, None, :] == jnp.arange(planes)[None, :, None]).astype(jnp.bfloat16)
    counts = jnp.einsum("kzp,pd->kzd", bin_hot, focus_hot, preferred_element_type=jnp.float32)
    row_angle = 2.0 * (
        defocus[None, :] * centred_square(own_freq, length)[:, None] + PHASE_OFFSET
    )
    col_angle = 2.0 * (defocus[:, None] * centred_square(freq, length)[None, :])
    row_side = jnp.concatenate(
        [counts * jnp.cos(row_angle)[:, None, :], counts * jnp.sin(row_angle)[:, None, :]], axis=2
    )
    col_side = jnp.concatenate([jnp.cos(col_angle), -jnp.sin(col_angle)], axis=0)
    double = jnp.einsum("kzd,dx->kzx", row_side, col_side, precision=lax.Precision.HIGHEST)
    weights = 0.5 * (jnp.sum(counts, axis=2, keepdims=True) - double)
    denom = weights + TAU_PRIOR

    updated = []
    for c, each in enumerate(sizes):
        here = slice(starts[c], starts[c] + each)
        prior = ref[here].astype(jnp.float32)
        under = denom[here]
        total = sums[c].astype(jnp.float32).reshape(each, planes, 2 * length)
        updated.append(
            (
                (TAU_PRIOR * prior + total) / jnp.concatenate([under, under], axis=2)
            ).astype(jnp.bfloat16)
        )
    return jnp.concatenate(updated, axis=0)


def solution(mesh):
    placed = (
        P(("batch", "slab"), None, None),
        P(("batch", "slab")),
        P(("batch", "slab"), None),
        P(("batch", "slab")),
        P(),
        P(("batch", "slab"), None),
        P(),
        P("batch", "slab", None),
    )
    return jax.shard_map(
        per_device, mesh=mesh, in_specs=placed, out_specs=P("batch", "slab", None), check_vma=False
    )
```

```python
import functools
import math

import jax
import jax.numpy as jnp
import numpy as np
from jax import lax
from jax.experimental import pallas as pl
from jax.experimental.pallas import tpu as pltpu
from jax.sharding import PartitionSpec as P

TAU_PRIOR = 4.0
PHASE_OFFSET = 0.1
CHUNKS = ((2, False), (2, False), (2, False))
SHARES = 6
META_BASE = 32
META_ROWS = 16
LANES = 128
SPECTRUM_VMEM = 60 * 1024 * 1024
INSERT_VMEM = 32 * 1024 * 1024


def dft_tables(length):
    index = np.arange(length, dtype=np.int32)
    turns = index[:, None] * index[None, :] % length
    angle = np.float32(2.0 * math.pi / length) * turns.astype(np.float32)
    factor = np.float32(1.0 / math.sqrt(length))
    cosine = np.cos(angle) * factor
    sine = np.sin(angle) * factor
    upper_rows = np.concatenate([cosine, -sine], axis=1)
    lower_rows = np.concatenate([sine, cosine], axis=1)
    table_right = np.concatenate([upper_rows, lower_rows], axis=0)
    return cosine, -sine, table_right


def spread(iota, values):
    out = jnp.full(iota.shape, values[0])
    for p in range(1, len(values)):
        out = jnp.where(iota == p, values[p], out)
    return out


def sin_turns(turns):
    half = jnp.floor(2.0 * turns + 0.5)
    x = (2.0 * math.pi) * (turns - 0.5 * half)
    sign = 1.0 - 2.0 * (half - 2.0 * jnp.floor(0.5 * half))
    square = x * x
    series = jnp.full(x.shape, -1.0 / math.factorial(11), jnp.float32)
    for power in (9, 7, 5, 3, 1):
        series = series * square + (1.0 if power % 4 == 1 else -1.0) / math.factorial(power)
    return sign * x * series


def phase_turns(freq, shift, length):
    steps = freq * shift
    steps = steps - length * jnp.floor(steps * (1.0 / length))
    return steps * (1.0 / length)


def centred(freq, length):
    return jnp.where(freq < length // 2, freq, freq - length) * (1.0 / length)


def spectrum_kernel(
    runs,
    with_meta,
    classes,
    shifts,
    defocus_class,
    defocus,
    run_counts,
    images_in,
    left_in,
    right_in,
    out,
    images,
    left,
    right,
    joined,
    block,
    load_sems,
    send_sems,
):
    particles, length = images.shape[0], images.shape[1]
    owners = out.shape[0]
    rows_each = runs[0][1] - runs[0][0]
    rows = owners * rows_each
    loads = [pltpu.make_async_copy(left_in, left, load_sems.at[0])]
    for p in range(particles):
        loads.append(pltpu.make_async_copy(images_in.at[p], images.at[p], load_sems.at[1 + p]))
    loads.append(pltpu.make_async_copy(right_in, right, load_sems.at[1 + particles]))
    for load in loads:
        load.start()

    every = range(particles)
    focus = [defocus[defocus_class[p]] for p in every]
    shift_x = [shifts[0, p].astype(jnp.float32) for p in every]
    shift_y = [shifts[1, p].astype(jnp.float32) for p in every]
    sublane = lax.broadcasted_iota(jnp.int32, (particles, length), 0)
    freq_x = lax.broadcasted_iota(jnp.int32, (particles, length), 1).astype(jnp.float32)
    phase_x = phase_turns(freq_x, spread(sublane, shift_x), length)
    angle_x = spread(sublane, focus) * centred(freq_x, length) * centred(freq_x, length)
    angle_x = angle_x * (0.5 / math.pi)
    col = [sin_turns(at) for at in (phase_x, phase_x + 0.25, angle_x, angle_x + 0.25)]
    lane = lax.broadcasted_iota(jnp.int32, (rows, LANES), 1)
    which = lane % particles
    quantity = lane // particles
    row_at = lax.broadcasted_iota(jnp.int32, (rows, LANES), 0)
    owner = row_at // rows_each
    freq_y = row_at - owner * rows_each + spread(owner, [begin for begin, _ in runs])
    freq_y = freq_y.astype(jnp.float32)
    phase_y = phase_turns(freq_y, spread(which, shift_y), length)
    angle_y = spread(which, focus) * centred(freq_y, length) * centred(freq_y, length)
    angle_y = (angle_y + PHASE_OFFSET) * (0.5 / math.pi)
    row = jnp.where(quantity < 2, phase_y, angle_y)
    row = sin_turns(row + jnp.where(quantity % 2 == 1, 0.25, 0.0))

    if with_meta:
        digits = jnp.zeros((META_ROWS, LANES), jnp.int32)
        at_row = lax.broadcasted_iota(jnp.int32, (META_ROWS, LANES), 0) % particles
        at_lane = lax.broadcasted_iota(jnp.int32, (META_ROWS, LANES), 1)
        ends = [[run_counts[0, p] for p in every]]
        for s in range(1, run_counts.shape[0] - 1):
            ends.append([ends[-1][p] + run_counts[s, p] for p in every])
        fields = [[classes[p] for p in every], [defocus_class[p] for p in every], *ends]
        for f, values in enumerate(fields):
            value = spread(at_row, values)
            digits = jnp.where(at_lane == f, value // META_BASE, digits)
            digits = jnp.where(at_lane == f + len(fields), value % META_BASE, digits)
        digits = digits.astype(jnp.float32).astype(jnp.bfloat16)
        for d in range(owners):
            block[d, particles * rows_each :, :] = jnp.zeros(
                (META_ROWS, 2 * length), jnp.bfloat16
            )
            block[d, particles * rows_each :, :LANES] = digits

    loads[0].wait()
    table = left[...]
    for p in range(particles):
        loads[1 + p].wait()
        section = jnp.dot(table, images[p], preferred_element_type=jnp.float32)
        section = section.astype(jnp.bfloat16)
        joined[p * rows : (p + 1) * rows, :length] = section[:rows]
        joined[p * rows : (p + 1) * rows, length:] = section[rows:]
    loads[1 + particles].wait()
    sends = []
    for first in range(0, particles, 2):
        spectrum = jnp.dot(
            joined[first * rows : (first + 2) * rows, :],
            right[...],
            preferred_element_type=jnp.float32,
        )
        for p in range(first, first + 2):
            part = spectrum[(p - first) * rows : (p - first + 1) * rows]
            real_part, imag_part = part[:, :length], part[:, length:]
            row_sin, row_cos, row_ctf_sin, row_ctf_cos = [
                row[:, q * particles + p : q * particles + p + 1] for q in range(4)
            ]
            col_sin, col_cos, col_ctf_sin, col_ctf_cos = [part[p : p + 1, :] for part in col]
            transfer = -(row_ctf_sin * col_ctf_cos + row_ctf_cos * col_ctf_sin)
            cosine = transfer * (row_cos * col_cos - row_sin * col_sin)
            sine = transfer * (row_sin * col_cos + row_cos * col_sin)
            real_new = real_part * cosine + imag_part * sine
            imag_new = imag_part * cosine - real_part * sine
            weighted = jnp.concatenate([real_new, imag_new], axis=1).astype(jnp.bfloat16)
            block[:, p * rows_each : (p + 1) * rows_each, :] = weighted.reshape(
                owners, rows_each, 2 * length
            )
        done = pl.ds(first * rows_each, 2 * rows_each)
        if with_meta and first + 2 == particles:
            done = pl.ds(first * rows_each, 2 * rows_each + META_ROWS)
        sends.append(
            pltpu.make_async_copy(block.at[:, done], out.at[:, done], send_sems.at[first // 2])
        )
        sends[-1].start()
    for send in sends:
        send.wait()


def insert_kernel(bins, meta_at, received, codes, out):
    sources = received.shape[0]
    rows = received[...].reshape(-1, received.shape[2])
    codes_all = codes[...]
    for k in range(out.shape[0]):
        bin_index = lax.broadcasted_iota(jnp.int32, (bins, 1), 0) + k * bins
        hot = jnp.where(codes_all == bin_index, 1.0, 0.0).astype(jnp.bfloat16)
        total = jnp.dot(hot, rows, preferred_element_type=jnp.float32)
        out[k, :bins, :] = total.astype(out.dtype)
        if out.shape[1] > bins:
            tiles = out.shape[2] // LANES
            first_half = lax.broadcasted_iota(jnp.int32, (META_ROWS, LANES), 0) < META_ROWS // 2
            for i in range(min(sources, tiles)):
                low = received[i, meta_at : meta_at + META_ROWS, :LANES]
                if i + tiles < sources:
                    high = received[i + tiles, meta_at : meta_at + META_ROWS, :LANES]
                    low = jnp.where(
                        first_half, low.astype(jnp.float32), high.astype(jnp.float32)
                    ).astype(low.dtype)
                out[k, bins:, i * LANES : (i + 1) * LANES] = low


def whole_vmem(count):
    return [pl.BlockSpec(memory_space=pltpu.VMEM)] * count


def centred_square(freq, length):
    half_length = length // 2
    value = ((freq + half_length) % length - half_length).astype(jnp.float32) / length
    return value * value


def slab_roles(batch_count, swapped):
    roles = list(range(batch_count))
    half = batch_count // 2
    if swapped:
        for b in range(1, half, 2):
            roles[b], roles[half + b - 1] = half + b - 1, b
    return roles


def slab_exchange(parts, place, slab_count, roles):
    arrived = []
    for shift in range(1, slab_count):
        perm = []
        for b, role in enumerate(roles):
            upper = role >= len(roles) // 2
            for source in range(slab_count):
                target = (source + shift) % slab_count
                if target < slab_count - 1:
                    ends = (slab_count - 1 - source, slab_count - 1 - target)
                    ends = ends if upper else (source, target)
                    perm.append((b * slab_count + ends[0], b * slab_count + ends[1]))
        block = choose(parts, (place + shift) % slab_count)
        arrived.append(lax.ppermute(block, ("batch", "slab"), perm))
    return arrived


def choose(parts, index):
    chosen = parts[-1]
    for d in range(parts.shape[0] - 1):
        chosen = jnp.where(index == d, parts[d], chosen)
    return chosen


def per_device(images, classes, shifts, defocus_class, defocus, run_counts, dest_map, ref):
    particles, length, _ = images.shape
    batch_count = lax.axis_size("batch")
    slab_count = lax.axis_size("slab")
    batch = lax.axis_index("batch")
    slab = lax.axis_index("slab")
    rows, planes, _ = ref.shape
    mirrored = slab_count == 4 and batch_count % 2 == 0 and 2 * particles <= META_ROWS
    mirrored = mirrored and batch_count * LANES <= 4 * length
    half_batch = batch_count // 2
    sizes = [rows * share // SHARES for share, _ in CHUNKS]
    starts = [sum(sizes[:c]) for c in range(len(CHUNKS))]
    roles = [slab_roles(batch_count, mirrored and swapped) for _, swapped in CHUNKS]
    freq = jnp.arange(length, dtype=jnp.int32)

    fields = slab_count + 1

    cosine, minus_sine, table_right = dft_tables(length)
    table_right = jnp.asarray(table_right.astype(jnp.bfloat16))
    received = []
    weighted = []
    for c, each in enumerate(sizes):
        chunk_rows = batch_count * each
        block = np.array(roles[c])
        order = (block[:, None] * rows + starts[c] + np.arange(each)[None, :]).reshape(-1)
        left = np.concatenate([cosine[order], minus_sine[order]], axis=0)
        runs = [(k * rows + starts[c], k * rows + starts[c] + each) for k in block.tolist()]
        with_meta = c == 0
        block_rows = particles * each + META_ROWS * with_meta
        block_shape = (batch_count, block_rows, 2 * length)
        smem = pl.BlockSpec(memory_space=pltpu.SMEM)
        hbm = pl.BlockSpec(memory_space=pltpu.HBM)
        send = pl.pallas_call(
            functools.partial(spectrum_kernel, runs, with_meta),
            out_shape=jax.ShapeDtypeStruct(block_shape, jnp.bfloat16),
            in_specs=[smem] * 5 + [hbm] * 3,
            out_specs=hbm,
            scratch_shapes=[
                pltpu.VMEM((particles, length, length), jnp.bfloat16),
                pltpu.VMEM((2 * chunk_rows, length), jnp.bfloat16),
                pltpu.VMEM((2 * length, 2 * length), jnp.bfloat16),
                pltpu.VMEM((particles * chunk_rows, 2 * length), jnp.bfloat16),
                pltpu.VMEM(block_shape, jnp.bfloat16),
                pltpu.SemaphoreType.DMA((particles + 2,)),
                pltpu.SemaphoreType.DMA((particles // 2,)),
            ],
            compiler_params=pltpu.CompilerParams(vmem_limit_bytes=SPECTRUM_VMEM),
            cost_estimate=pl.CostEstimate(flops=0, bytes_accessed=0, transcendentals=0),
            name="spectrum",
        )(
            classes,
            shifts.T,
            defocus_class,
            defocus,
            run_counts.T,
            images,
            jnp.asarray(left.astype(jnp.bfloat16)),
            table_right,
        )
        weighted.append(send)
        received.append(lax.all_to_all(send, "batch", 0, 0, tiled=True))

    def read_digits(rows_in):
        whole = rows_in.astype(jnp.int32).reshape(-1, 2 * fields)
        return whole[:, :fields] * META_BASE + whole[:, fields:]

    meta_at = particles * sizes[0]
    meta_layer = read_digits(received[0][:, meta_at : meta_at + particles, : 2 * fields])

    class_count = dest_map.shape[0]

    dest_wide = dest_map.astype(jnp.bfloat16)

    def find_planes(table):
        class_hot = (table[:, :1] == jnp.arange(class_count)[None, :]).astype(jnp.bfloat16)
        local_plane = jnp.dot(class_hot, dest_wide, preferred_element_type=jnp.float32)
        past = freq[None, :, None] >= table[:, None, 2:]
        owner = jnp.sum(past.astype(jnp.int32), axis=2)
        return owner * planes + local_plane.astype(jnp.int32)

    def pick_block(table, block):
        return sum(
            jnp.where(block == k, table[:, k * rows : (k + 1) * rows], 0)
            for k in range(batch_count)
        )

    window_slabs = 3 if mirrored else slab_count
    blocks = [
        sum(jnp.where(batch == b, block, 0) for b, block in enumerate(role)) for role in roles
    ]
    layer_planes = find_planes(meta_layer)
    places, codes = [], []
    for c, each in enumerate(sizes):
        here = slice(starts[c], starts[c] + each)
        plane = pick_block(layer_planes, blocks[c])[:, here]
        place, owner_place = slab, plane // planes
        if mirrored:
            upper = blocks[c] >= half_batch
            owner_place = jnp.where(upper, slab_count - 1 - owner_place, owner_place)
            place = jnp.where(upper, slab_count - 1 - slab, slab)
        places.append(place)
        code = owner_place * (each * planes) + jnp.arange(each)[None, :] * planes
        code = (code + plane % planes).reshape(batch_count, particles * each)
        if c == 0:
            code = jnp.pad(code, ((0, 0), (0, META_ROWS)), constant_values=-1)
        codes.append(code.reshape(1, -1))

    sums, arrived = [], []
    for c, each in enumerate(sizes):
        bins = each * planes
        extra_rows = META_ROWS if c == 0 and mirrored else 0
        codes_in = codes[c]
        if c == 0:
            codes_in, _ = lax.optimization_barrier((codes_in, weighted[1:]))
        if c > 0 and mirrored:
            codes_in, arrived[c - 1][2] = lax.optimization_barrier((codes_in, arrived[c - 1][2]))
        parts = pl.pallas_call(
            functools.partial(insert_kernel, bins, meta_at),
            out_shape=jax.ShapeDtypeStruct(
                (window_slabs, bins + extra_rows, 2 * length), jnp.bfloat16
            ),
            in_specs=whole_vmem(2),
            out_specs=pl.BlockSpec(memory_space=pltpu.VMEM),
            compiler_params=pltpu.CompilerParams(vmem_limit_bytes=INSERT_VMEM),
            cost_estimate=pl.CostEstimate(
                flops=0,
                bytes_accessed=0,
                transcendentals=0,
            ),
            name="insert",
        )(received[c], codes_in)
        if not mirrored:
            sums.append(lax.psum_scatter(parts, "slab", scatter_dimension=0, tiled=False))
            continue
        for before in arrived:
            before[1], _ = lax.optimization_barrier((before[1], parts))
        arrived.append(slab_exchange(parts, places[c], slab_count, roles[c]))
        own = choose(parts[:, :bins], places[c]).astype(jnp.float32)
        sums.append(jnp.where(places[c] == slab_count - 1, 0.0, own))
    for c, each in enumerate(sizes):
        if not mirrored:
            break
        for block in arrived[c]:
            sums[c] = sums[c] + block[: each * planes].astype(jnp.float32)
        over = [(b, block) for b, block in enumerate(roles[c]) if b != block]
        if over:
            if c + 1 < len(sizes):
                sums[c], arrived[c + 1][2] = lax.optimization_barrier(
                    (sums[c], arrived[c + 1][2])
                )
            handed = lax.ppermute(sums[c].astype(jnp.bfloat16), "batch", over)
            sums[c] = jnp.where(blocks[c] == batch, sums[c], handed.astype(jnp.float32))

    meta_all = [meta_layer]
    if mirrored:
        for block in [block[sizes[0] * planes :] for block in arrived[0]]:
            block = block.reshape(META_ROWS, -1, LANES)
            halves = (block[:particles], block[particles : 2 * particles])
            low = jnp.concatenate(halves, axis=1)[:, :batch_count, : 2 * fields]
            meta_all.append(read_digits(low.transpose(1, 0, 2)))
    else:
        for step in range(1, slab_count):
            ring = [(s, (s + step) % slab_count) for s in range(slab_count)]
            meta_all.append(lax.ppermute(meta_layer, "slab", ring))
    meta_all = jnp.concatenate(meta_all, axis=0)

    own_freq = batch * rows + jnp.arange(rows, dtype=jnp.int32)
    own_plane = pick_block(find_planes(meta_all), batch) - slab * planes
    focus_count = defocus.shape[0]
    focus_hot = (meta_all[:, 1:2] == jnp.arange(focus_count)[None, :]).astype(jnp.bfloat16)
    if mirrored:
        own_plane = jnp.where(places[0] == slab_count - 1, -1, own_plane)
    bin_hot = (own_plane.T[:, None, :] == jnp.arange(planes)[None, :, None]).astype(jnp.bfloat16)
    counts = jnp.einsum("kzp,pd->kzd", bin_hot, focus_hot, preferred_element_type=jnp.float32)
    row_angle = 2.0 * (
        defocus[None, :] * centred_square(own_freq, length)[:, None] + PHASE_OFFSET
    )
    col_angle = 2.0 * (defocus[:, None] * centred_square(freq, length)[None, :])
    row_side = jnp.concatenate(
        [counts * jnp.cos(row_angle)[:, None, :], counts * jnp.sin(row_angle)[:, None, :]], axis=2
    )
    col_side = jnp.concatenate([jnp.cos(col_angle), -jnp.sin(col_angle)], axis=0)
    double = jnp.einsum("kzd,dx->kzx", row_side, col_side, precision=lax.Precision.HIGHEST)
    weights = 0.5 * (jnp.sum(counts, axis=2, keepdims=True) - double)
    denom = weights + TAU_PRIOR

    updated = []
    for c, each in enumerate(sizes):
        here = slice(starts[c], starts[c] + each)
        prior = ref[here].astype(jnp.float32)
        under = denom[here]
        total = sums[c].astype(jnp.float32).reshape(each, planes, 2 * length)
        updated.append(
            (
                (TAU_PRIOR * prior + total) / jnp.concatenate([under, under], axis=2)
            ).astype(jnp.bfloat16)
        )
    return jnp.concatenate(updated, axis=0)


def solution(mesh):
    placed = (
        P(("batch", "slab"), None, None),
        P(("batch", "slab")),
        P(("batch", "slab"), None),
        P(("batch", "slab")),
        P(),
        P(("batch", "slab"), None),
        P(),
        P("batch", "slab", None),
    )
    return jax.shard_map(
        per_device, mesh=mesh, in_specs=placed, out_specs=P("batch", "slab", None), check_vma=False
    )
```

```python
import functools
import math

import jax
import jax.numpy as jnp
import numpy as np
from jax import lax
from jax.experimental import pallas as pl
from jax.experimental.pallas import tpu as pltpu
from jax.sharding import PartitionSpec as P

TAU_PRIOR = 4.0
PHASE_OFFSET = 0.1
CHUNKS = ((2, False), (3, True), (1, False))
SHARES = 6
META_BASE = 32
META_ROWS = 16
LANES = 128
SPECTRUM_VMEM = 60 * 1024 * 1024
INSERT_VMEM = 32 * 1024 * 1024


def dft_tables(length):
    index = np.arange(length, dtype=np.int32)
    turns = index[:, None] * index[None, :] % length
    angle = np.float32(2.0 * math.pi / length) * turns.astype(np.float32)
    factor = np.float32(1.0 / math.sqrt(length))
    cosine = np.cos(angle) * factor
    sine = np.sin(angle) * factor
    upper_rows = np.concatenate([cosine, -sine], axis=1)
    lower_rows = np.concatenate([sine, cosine], axis=1)
    table_right = np.concatenate([upper_rows, lower_rows], axis=0)
    return cosine, -sine, table_right


def spread(iota, values):
    out = jnp.full(iota.shape, values[0])
    for p in range(1, len(values)):
        out = jnp.where(iota == p, values[p], out)
    return out


def sin_turns(turns):
    half = jnp.floor(2.0 * turns + 0.5)
    x = (2.0 * math.pi) * (turns - 0.5 * half)
    sign = 1.0 - 2.0 * (half - 2.0 * jnp.floor(0.5 * half))
    square = x * x
    series = jnp.full(x.shape, -1.0 / math.factorial(11), jnp.float32)
    for power in (9, 7, 5, 3, 1):
        series = series * square + (1.0 if power % 4 == 1 else -1.0) / math.factorial(power)
    return sign * x * series


def phase_turns(freq, shift, length):
    steps = freq * shift
    steps = steps - length * jnp.floor(steps * (1.0 / length))
    return steps * (1.0 / length)


def centred(freq, length):
    return jnp.where(freq < length // 2, freq, freq - length) * (1.0 / length)


def spectrum_kernel(
    runs,
    with_meta,
    classes,
    shifts,
    defocus_class,
    defocus,
    run_counts,
    images_in,
    left_in,
    right_in,
    out,
    images,
    left,
    right,
    joined,
    block,
    load_sems,
    send_sems,
):
    particles, length = images.shape[0], images.shape[1]
    owners = out.shape[0]
    rows_each = runs[0][1] - runs[0][0]
    rows = owners * rows_each
    loads = [pltpu.make_async_copy(left_in, left, load_sems.at[0])]
    for p in range(particles):
        loads.append(pltpu.make_async_copy(images_in.at[p], images.at[p], load_sems.at[1 + p]))
    loads.append(pltpu.make_async_copy(right_in, right, load_sems.at[1 + particles]))
    for load in loads:
        load.start()

    every = range(particles)
    focus = [defocus[defocus_class[p]] for p in every]
    shift_x = [shifts[0, p].astype(jnp.float32) for p in every]
    shift_y = [shifts[1, p].astype(jnp.float32) for p in every]
    sublane = lax.broadcasted_iota(jnp.int32, (particles, length), 0)
    freq_x = lax.broadcasted_iota(jnp.int32, (particles, length), 1).astype(jnp.float32)
    phase_x = phase_turns(freq_x, spread(sublane, shift_x), length)
    angle_x = spread(sublane, focus) * centred(freq_x, length) * centred(freq_x, length)
    angle_x = angle_x * (0.5 / math.pi)
    col = [sin_turns(at) for at in (phase_x, phase_x + 0.25, angle_x, angle_x + 0.25)]
    lane = lax.broadcasted_iota(jnp.int32, (rows, LANES), 1)
    which = lane % particles
    quantity = lane // particles
    row_at = lax.broadcasted_iota(jnp.int32, (rows, LANES), 0)
    owner = row_at // rows_each
    freq_y = row_at - owner * rows_each + spread(owner, [begin for begin, _ in runs])
    freq_y = freq_y.astype(jnp.float32)
    phase_y = phase_turns(freq_y, spread(which, shift_y), length)
    angle_y = spread(which, focus) * centred(freq_y, length) * centred(freq_y, length)
    angle_y = (angle_y + PHASE_OFFSET) * (0.5 / math.pi)
    row = jnp.where(quantity < 2, phase_y, angle_y)
    row = sin_turns(row + jnp.where(quantity % 2 == 1, 0.25, 0.0))

    if with_meta:
        digits = jnp.zeros((META_ROWS, LANES), jnp.int32)
        at_row = lax.broadcasted_iota(jnp.int32, (META_ROWS, LANES), 0) % particles
        at_lane = lax.broadcasted_iota(jnp.int32, (META_ROWS, LANES), 1)
        ends = [[run_counts[0, p] for p in every]]
        for s in range(1, run_counts.shape[0] - 1):
            ends.append([ends[-1][p] + run_counts[s, p] for p in every])
        fields = [[classes[p] for p in every], [defocus_class[p] for p in every], *ends]
        for f, values in enumerate(fields):
            value = spread(at_row, values)
            digits = jnp.where(at_lane == f, value // META_BASE, digits)
            digits = jnp.where(at_lane == f + len(fields), value % META_BASE, digits)
        digits = digits.astype(jnp.float32).astype(jnp.bfloat16)
        for d in range(owners):
            block[d, particles * rows_each :, :] = jnp.zeros(
                (META_ROWS, 2 * length), jnp.bfloat16
            )
            block[d, particles * rows_each :, :LANES] = digits

    loads[0].wait()
    table = left[...]
    for p in range(particles):
        loads[1 + p].wait()
        section = jnp.dot(table, images[p], preferred_element_type=jnp.float32)
        section = section.astype(jnp.bfloat16)
        joined[p * rows : (p + 1) * rows, :length] = section[:rows]
        joined[p * rows : (p + 1) * rows, length:] = section[rows:]
    loads[1 + particles].wait()
    sends = []
    for first in range(0, particles, 2):
        spectrum = jnp.dot(
            joined[first * rows : (first + 2) * rows, :],
            right[...],
            preferred_element_type=jnp.float32,
        )
        for p in range(first, first + 2):
            part = spectrum[(p - first) * rows : (p - first + 1) * rows]
            real_part, imag_part = part[:, :length], part[:, length:]
            row_sin, row_cos, row_ctf_sin, row_ctf_cos = [
                row[:, q * particles + p : q * particles + p + 1] for q in range(4)
            ]
            col_sin, col_cos, col_ctf_sin, col_ctf_cos = [part[p : p + 1, :] for part in col]
            transfer = -(row_ctf_sin * col_ctf_cos + row_ctf_cos * col_ctf_sin)
            cosine = transfer * (row_cos * col_cos - row_sin * col_sin)
            sine = transfer * (row_sin * col_cos + row_cos * col_sin)
            real_new = real_part * cosine + imag_part * sine
            imag_new = imag_part * cosine - real_part * sine
            weighted = jnp.concatenate([real_new, imag_new], axis=1).astype(jnp.bfloat16)
            block[:, p * rows_each : (p + 1) * rows_each, :] = weighted.reshape(
                owners, rows_each, 2 * length
            )
        done = pl.ds(first * rows_each, 2 * rows_each)
        if with_meta and first + 2 == particles:
            done = pl.ds(first * rows_each, 2 * rows_each + META_ROWS)
        sends.append(
            pltpu.make_async_copy(block.at[:, done], out.at[:, done], send_sems.at[first // 2])
        )
        sends[-1].start()
    for send in sends:
        send.wait()


def insert_kernel(bins, meta_at, received, codes, out):
    sources = received.shape[0]
    rows = received[...].reshape(-1, received.shape[2])
    codes_all = codes[...]
    for k in range(out.shape[0]):
        bin_index = lax.broadcasted_iota(jnp.int32, (bins, 1), 0) + k * bins
        hot = jnp.where(codes_all == bin_index, 1.0, 0.0).astype(jnp.bfloat16)
        total = jnp.dot(hot, rows, preferred_element_type=jnp.float32)
        out[k, :bins, :] = total.astype(out.dtype)
        if out.shape[1] > bins:
            tiles = out.shape[2] // LANES
            first_half = lax.broadcasted_iota(jnp.int32, (META_ROWS, LANES), 0) < META_ROWS // 2
            for i in range(min(sources, tiles)):
                low = received[i, meta_at : meta_at + META_ROWS, :LANES]
                if i + tiles < sources:
                    high = received[i + tiles, meta_at : meta_at + META_ROWS, :LANES]
                    low = jnp.where(
                        first_half, low.astype(jnp.float32), high.astype(jnp.float32)
                    ).astype(low.dtype)
                out[k, bins:, i * LANES : (i + 1) * LANES] = low


def whole_vmem(count):
    return [pl.BlockSpec(memory_space=pltpu.VMEM)] * count


def centred_square(freq, length):
    half_length = length // 2
    value = ((freq + half_length) % length - half_length).astype(jnp.float32) / length
    return value * value


def slab_roles(batch_count, swapped):
    roles = list(range(batch_count))
    half = batch_count // 2
    if swapped:
        for b in range(1, half, 2):
            roles[b], roles[half + b - 1] = half + b - 1, b
    return roles


def slab_exchange(parts, place, slab_count, roles):
    arrived = []
    for shift in range(1, slab_count):
        perm = []
        for b, role in enumerate(roles):
            upper = role >= len(roles) // 2
            for source in range(slab_count):
                target = (source + shift) % slab_count
                if target < slab_count - 1:
                    ends = (slab_count - 1 - source, slab_count - 1 - target)
                    ends = ends if upper else (source, target)
                    perm.append((b * slab_count + ends[0], b * slab_count + ends[1]))
        block = choose(parts, (place + shift) % slab_count)
        arrived.append(lax.ppermute(block, ("batch", "slab"), perm))
    return arrived


def choose(parts, index):
    chosen = parts[-1]
    for d in range(parts.shape[0] - 1):
        chosen = jnp.where(index == d, parts[d], chosen)
    return chosen


def per_device(images, classes, shifts, defocus_class, defocus, run_counts, dest_map, ref):
    particles, length, _ = images.shape
    batch_count = lax.axis_size("batch")
    slab_count = lax.axis_size("slab")
    batch = lax.axis_index("batch")
    slab = lax.axis_index("slab")
    rows, planes, _ = ref.shape
    mirrored = slab_count == 4 and batch_count % 2 == 0 and 2 * particles <= META_ROWS
    mirrored = mirrored and batch_count * LANES <= 4 * length
    half_batch = batch_count // 2
    shares = [share for share, _ in CHUNKS]
    if rows % (8 * SHARES):
        shares = [SHARES // len(CHUNKS)] * len(CHUNKS)
    sizes = [rows * share // SHARES for share in shares]
    starts = [sum(sizes[:c]) for c in range(len(CHUNKS))]
    roles = [slab_roles(batch_count, mirrored and swapped) for _, swapped in CHUNKS]
    freq = jnp.arange(length, dtype=jnp.int32)

    fields = slab_count + 1

    cosine, minus_sine, table_right = dft_tables(length)
    table_right = jnp.asarray(table_right.astype(jnp.bfloat16))
    received = []
    weighted = []
    for c, each in enumerate(sizes):
        chunk_rows = batch_count * each
        block = np.array(roles[c])
        order = (block[:, None] * rows + starts[c] + np.arange(each)[None, :]).reshape(-1)
        left = np.concatenate([cosine[order], minus_sine[order]], axis=0)
        runs = [(k * rows + starts[c], k * rows + starts[c] + each) for k in block.tolist()]
        with_meta = c == 0
        block_rows = particles * each + META_ROWS * with_meta
        block_shape = (batch_count, block_rows, 2 * length)
        smem = pl.BlockSpec(memory_space=pltpu.SMEM)
        hbm = pl.BlockSpec(memory_space=pltpu.HBM)
        send = pl.pallas_call(
            functools.partial(spectrum_kernel, runs, with_meta),
            out_shape=jax.ShapeDtypeStruct(block_shape, jnp.bfloat16),
            in_specs=[smem] * 5 + [hbm] * 3,
            out_specs=hbm,
            scratch_shapes=[
                pltpu.VMEM((particles, length, length), jnp.bfloat16),
                pltpu.VMEM((2 * chunk_rows, length), jnp.bfloat16),
                pltpu.VMEM((2 * length, 2 * length), jnp.bfloat16),
                pltpu.VMEM((particles * chunk_rows, 2 * length), jnp.bfloat16),
                pltpu.VMEM(block_shape, jnp.bfloat16),
                pltpu.SemaphoreType.DMA((particles + 2,)),
                pltpu.SemaphoreType.DMA((particles // 2,)),
            ],
            compiler_params=pltpu.CompilerParams(vmem_limit_bytes=SPECTRUM_VMEM),
            cost_estimate=pl.CostEstimate(flops=0, bytes_accessed=0, transcendentals=0),
            name="spectrum",
        )(
            classes,
            shifts.T,
            defocus_class,
            defocus,
            run_counts.T,
            images,
            jnp.asarray(left.astype(jnp.bfloat16)),
            table_right,
        )
        weighted.append(send)
        received.append(lax.all_to_all(send, "batch", 0, 0, tiled=True))

    def read_digits(rows_in):
        whole = rows_in.astype(jnp.int32).reshape(-1, 2 * fields)
        return whole[:, :fields] * META_BASE + whole[:, fields:]

    meta_at = particles * sizes[0]
    meta_layer = read_digits(received[0][:, meta_at : meta_at + particles, : 2 * fields])

    class_count = dest_map.shape[0]

    dest_wide = dest_map.astype(jnp.bfloat16)

    def find_planes(table):
        class_hot = (table[:, :1] == jnp.arange(class_count)[None, :]).astype(jnp.bfloat16)
        local_plane = jnp.dot(class_hot, dest_wide, preferred_element_type=jnp.float32)
        past = freq[None, :, None] >= table[:, None, 2:]
        owner = jnp.sum(past.astype(jnp.int32), axis=2)
        return owner * planes + local_plane.astype(jnp.int32)

    def pick_block(table, block):
        return sum(
            jnp.where(block == k, table[:, k * rows : (k + 1) * rows], 0)
            for k in range(batch_count)
        )

    window_slabs = 3 if mirrored else slab_count
    blocks = [
        sum(jnp.where(batch == b, block, 0) for b, block in enumerate(role)) for role in roles
    ]
    layer_planes = find_planes(meta_layer)
    places, codes = [], []
    for c, each in enumerate(sizes):
        here = slice(starts[c], starts[c] + each)
        plane = pick_block(layer_planes, blocks[c])[:, here]
        place, owner_place = slab, plane // planes
        if mirrored:
            upper = blocks[c] >= half_batch
            owner_place = jnp.where(upper, slab_count - 1 - owner_place, owner_place)
            place = jnp.where(upper, slab_count - 1 - slab, slab)
        places.append(place)
        code = owner_place * (each * planes) + jnp.arange(each)[None, :] * planes
        code = (code + plane % planes).reshape(batch_count, particles * each)
        if c == 0:
            code = jnp.pad(code, ((0, 0), (0, META_ROWS)), constant_values=-1)
        codes.append(code.reshape(1, -1))

    sums, arrived = [], []
    for c, each in enumerate(sizes):
        bins = each * planes
        extra_rows = META_ROWS if c == 0 and mirrored else 0
        codes_in = codes[c]
        if c == 0:
            codes_in, _ = lax.optimization_barrier((codes_in, weighted[1:]))
        if c > 0 and mirrored:
            codes_in, arrived[c - 1][0], arrived[c - 1][2] = lax.optimization_barrier(
                (codes_in, arrived[c - 1][0], arrived[c - 1][2])
            )
        parts = pl.pallas_call(
            functools.partial(insert_kernel, bins, meta_at),
            out_shape=jax.ShapeDtypeStruct(
                (window_slabs, bins + extra_rows, 2 * length), jnp.bfloat16
            ),
            in_specs=whole_vmem(2),
            out_specs=pl.BlockSpec(memory_space=pltpu.VMEM),
            compiler_params=pltpu.CompilerParams(vmem_limit_bytes=INSERT_VMEM),
            cost_estimate=pl.CostEstimate(
                flops=0,
                bytes_accessed=0,
                transcendentals=0,
            ),
            name="insert",
        )(received[c], codes_in)
        if not mirrored:
            sums.append(lax.psum_scatter(parts, "slab", scatter_dimension=0, tiled=False))
            continue
        for before in arrived:
            before[1], _ = lax.optimization_barrier((before[1], parts))
        arrived.append(slab_exchange(parts, places[c], slab_count, roles[c]))
        own = choose(parts[:, :bins], places[c]).astype(jnp.float32)
        sums.append(jnp.where(places[c] == slab_count - 1, 0.0, own))
    for c, each in enumerate(sizes):
        if not mirrored:
            break
        for block in arrived[c]:
            sums[c] = sums[c] + block[: each * planes].astype(jnp.float32)
        over = [(b, block) for b, block in enumerate(roles[c]) if b != block]
        if over:
            if c + 1 < len(sizes):
                sums[c], arrived[c + 1][2] = lax.optimization_barrier(
                    (sums[c], arrived[c + 1][2])
                )
            handed = lax.ppermute(sums[c].astype(jnp.bfloat16), "batch", over)
            sums[c] = jnp.where(blocks[c] == batch, sums[c], handed.astype(jnp.float32))

    meta_all = [meta_layer]
    if mirrored:
        for block in [block[sizes[0] * planes :] for block in arrived[0]]:
            block = block.reshape(META_ROWS, -1, LANES)
            halves = (block[:particles], block[particles : 2 * particles])
            low = jnp.concatenate(halves, axis=1)[:, :batch_count, : 2 * fields]
            meta_all.append(read_digits(low.transpose(1, 0, 2)))
    else:
        for step in range(1, slab_count):
            ring = [(s, (s + step) % slab_count) for s in range(slab_count)]
            meta_all.append(lax.ppermute(meta_layer, "slab", ring))
    meta_all = jnp.concatenate(meta_all, axis=0)

    own_freq = batch * rows + jnp.arange(rows, dtype=jnp.int32)
    own_plane = pick_block(find_planes(meta_all), batch) - slab * planes
    focus_count = defocus.shape[0]
    focus_hot = (meta_all[:, 1:2] == jnp.arange(focus_count)[None, :]).astype(jnp.bfloat16)
    if mirrored:
        own_plane = jnp.where(places[0] == slab_count - 1, -1, own_plane)
    bin_hot = (own_plane.T[:, None, :] == jnp.arange(planes)[None, :, None]).astype(jnp.bfloat16)
    counts = jnp.einsum("kzp,pd->kzd", bin_hot, focus_hot, preferred_element_type=jnp.float32)
    row_angle = 2.0 * (
        defocus[None, :] * centred_square(own_freq, length)[:, None] + PHASE_OFFSET
    )
    col_angle = 2.0 * (defocus[:, None] * centred_square(freq, length)[None, :])
    row_side = jnp.concatenate(
        [counts * jnp.cos(row_angle)[:, None, :], counts * jnp.sin(row_angle)[:, None, :]], axis=2
    )
    col_side = jnp.concatenate([jnp.cos(col_angle), -jnp.sin(col_angle)], axis=0)
    double = jnp.einsum("kzd,dx->kzx", row_side, col_side, precision=lax.Precision.HIGHEST)
    weights = 0.5 * (jnp.sum(counts, axis=2, keepdims=True) - double)
    denom = weights + TAU_PRIOR

    updated = []
    for c, each in enumerate(sizes):
        here = slice(starts[c], starts[c] + each)
        prior = ref[here].astype(jnp.float32)
        under = denom[here]
        total = sums[c].astype(jnp.float32).reshape(each, planes, 2 * length)
        updated.append(
            (
                (TAU_PRIOR * prior + total) / jnp.concatenate([under, under], axis=2)
            ).astype(jnp.bfloat16)
        )
    return jnp.concatenate(updated, axis=0)


def solution(mesh):
    placed = (
        P(("batch", "slab"), None, None),
        P(("batch", "slab")),
        P(("batch", "slab"), None),
        P(("batch", "slab")),
        P(),
        P(("batch", "slab"), None),
        P(),
        P("batch", "slab", None),
    )
    return jax.shard_map(
        per_device, mesh=mesh, in_specs=placed, out_specs=P("batch", "slab", None), check_vma=False
    )
```

```python
import functools
import math

import jax
import jax.numpy as jnp
import numpy as np
from jax import lax
from jax.experimental import pallas as pl
from jax.experimental.pallas import tpu as pltpu
from jax.sharding import PartitionSpec as P

TAU_PRIOR = 4.0
PHASE_OFFSET = 0.1
CHUNKS = ((2, False), (3, True), (1, False))
SHARES = 6
META_BASE = 32
META_ROWS = 16
LANES = 128
SPECTRUM_VMEM = 60 * 1024 * 1024
INSERT_VMEM = 32 * 1024 * 1024


def dft_tables(length):
    index = np.arange(length, dtype=np.int32)
    turns = index[:, None] * index[None, :] % length
    angle = np.float32(2.0 * math.pi / length) * turns.astype(np.float32)
    factor = np.float32(1.0 / math.sqrt(length))
    cosine = np.cos(angle) * factor
    sine = np.sin(angle) * factor
    upper_rows = np.concatenate([cosine, -sine], axis=1)
    lower_rows = np.concatenate([sine, cosine], axis=1)
    table_right = np.concatenate([upper_rows, lower_rows], axis=0)
    return cosine, -sine, table_right


def spread(iota, values):
    out = jnp.full(iota.shape, values[0])
    for p in range(1, len(values)):
        out = jnp.where(iota == p, values[p], out)
    return out


def sin_turns(turns):
    half = jnp.floor(2.0 * turns + 0.5)
    x = (2.0 * math.pi) * (turns - 0.5 * half)
    sign = 1.0 - 2.0 * (half - 2.0 * jnp.floor(0.5 * half))
    square = x * x
    series = jnp.full(x.shape, -1.0 / math.factorial(11), jnp.float32)
    for power in (9, 7, 5, 3, 1):
        series = series * square + (1.0 if power % 4 == 1 else -1.0) / math.factorial(power)
    return sign * x * series


def phase_turns(freq, shift, length):
    steps = freq * shift
    steps = steps - length * jnp.floor(steps * (1.0 / length))
    return steps * (1.0 / length)


def centred(freq, length):
    return jnp.where(freq < length // 2, freq, freq - length) * (1.0 / length)


def spectrum_kernel(
    runs,
    with_meta,
    classes,
    shifts,
    defocus_class,
    defocus,
    run_counts,
    images_in,
    left_in,
    right_in,
    out,
    images,
    left,
    right,
    joined,
    block,
    load_sems,
    send_sems,
):
    particles, length = images.shape[0], images.shape[1]
    owners = out.shape[0]
    rows_each = runs[0][1] - runs[0][0]
    rows = owners * rows_each
    loads = [pltpu.make_async_copy(left_in, left, load_sems.at[0])]
    for p in range(particles):
        loads.append(pltpu.make_async_copy(images_in.at[p], images.at[p], load_sems.at[1 + p]))
    loads.append(pltpu.make_async_copy(right_in, right, load_sems.at[1 + particles]))
    for load in loads:
        load.start()

    every = range(particles)
    focus = [defocus[defocus_class[p]] for p in every]
    shift_x = [shifts[0, p].astype(jnp.float32) for p in every]
    shift_y = [shifts[1, p].astype(jnp.float32) for p in every]
    sublane = lax.broadcasted_iota(jnp.int32, (particles, length), 0)
    freq_x = lax.broadcasted_iota(jnp.int32, (particles, length), 1).astype(jnp.float32)
    phase_x = phase_turns(freq_x, spread(sublane, shift_x), length)
    angle_x = spread(sublane, focus) * centred(freq_x, length) * centred(freq_x, length)
    angle_x = angle_x * (0.5 / math.pi)
    col = [sin_turns(at) for at in (phase_x, phase_x + 0.25, angle_x, angle_x + 0.25)]
    lane = lax.broadcasted_iota(jnp.int32, (rows, LANES), 1)
    which = lane % particles
    quantity = lane // particles
    row_at = lax.broadcasted_iota(jnp.int32, (rows, LANES), 0)
    owner = row_at // rows_each
    freq_y = row_at - owner * rows_each + spread(owner, [begin for begin, _ in runs])
    freq_y = freq_y.astype(jnp.float32)
    phase_y = phase_turns(freq_y, spread(which, shift_y), length)
    angle_y = spread(which, focus) * centred(freq_y, length) * centred(freq_y, length)
    angle_y = (angle_y + PHASE_OFFSET) * (0.5 / math.pi)
    row = jnp.where(quantity < 2, phase_y, angle_y)
    row = sin_turns(row + jnp.where(quantity % 2 == 1, 0.25, 0.0))

    if with_meta:
        digits = jnp.zeros((META_ROWS, LANES), jnp.int32)
        at_row = lax.broadcasted_iota(jnp.int32, (META_ROWS, LANES), 0) % particles
        at_lane = lax.broadcasted_iota(jnp.int32, (META_ROWS, LANES), 1)
        ends = [[run_counts[0, p] for p in every]]
        for s in range(1, run_counts.shape[0] - 1):
            ends.append([ends[-1][p] + run_counts[s, p] for p in every])
        fields = [[classes[p] for p in every], [defocus_class[p] for p in every], *ends]
        for f, values in enumerate(fields):
            value = spread(at_row, values)
            digits = jnp.where(at_lane == f, value // META_BASE, digits)
            digits = jnp.where(at_lane == f + len(fields), value % META_BASE, digits)
        digits = digits.astype(jnp.float32).astype(jnp.bfloat16)
        for d in range(owners):
            block[d, particles * rows_each :, :] = jnp.zeros(
                (META_ROWS, 2 * length), jnp.bfloat16
            )
            block[d, particles * rows_each :, :LANES] = digits

    loads[0].wait()
    table = left[...]
    for p in range(particles):
        loads[1 + p].wait()
        section = jnp.dot(table, images[p], preferred_element_type=jnp.float32)
        section = section.astype(jnp.bfloat16)
        joined[p * rows : (p + 1) * rows, :length] = section[:rows]
        joined[p * rows : (p + 1) * rows, length:] = section[rows:]
    loads[1 + particles].wait()
    sends = []
    for first in range(0, particles, 2):
        spectrum = jnp.dot(
            joined[first * rows : (first + 2) * rows, :],
            right[...],
            preferred_element_type=jnp.float32,
        )
        for p in range(first, first + 2):
            part = spectrum[(p - first) * rows : (p - first + 1) * rows]
            real_part, imag_part = part[:, :length], part[:, length:]
            row_sin, row_cos, row_ctf_sin, row_ctf_cos = [
                row[:, q * particles + p : q * particles + p + 1] for q in range(4)
            ]
            col_sin, col_cos, col_ctf_sin, col_ctf_cos = [part[p : p + 1, :] for part in col]
            transfer = -(row_ctf_sin * col_ctf_cos + row_ctf_cos * col_ctf_sin)
            cosine = transfer * (row_cos * col_cos - row_sin * col_sin)
            sine = transfer * (row_sin * col_cos + row_cos * col_sin)
            real_new = real_part * cosine + imag_part * sine
            imag_new = imag_part * cosine - real_part * sine
            weighted = jnp.concatenate([real_new, imag_new], axis=1).astype(jnp.bfloat16)
            block[:, p * rows_each : (p + 1) * rows_each, :] = weighted.reshape(
                owners, rows_each, 2 * length
            )
        done = pl.ds(first * rows_each, 2 * rows_each)
        if with_meta and first + 2 == particles:
            done = pl.ds(first * rows_each, 2 * rows_each + META_ROWS)
        sends.append(
            pltpu.make_async_copy(block.at[:, done], out.at[:, done], send_sems.at[first // 2])
        )
        sends[-1].start()
    for send in sends:
        send.wait()


def insert_kernel(bins, meta_at, received, codes, out):
    sources = received.shape[0]
    rows = received[...].reshape(-1, received.shape[2])
    codes_all = codes[...]
    for k in range(out.shape[0]):
        bin_index = lax.broadcasted_iota(jnp.int32, (bins, 1), 0) + k * bins
        hot = jnp.where(codes_all == bin_index, 1.0, 0.0).astype(jnp.bfloat16)
        total = jnp.dot(hot, rows, preferred_element_type=jnp.float32)
        out[k, :bins, :] = total.astype(out.dtype)
        if out.shape[1] > bins:
            tiles = out.shape[2] // LANES
            first_half = lax.broadcasted_iota(jnp.int32, (META_ROWS, LANES), 0) < META_ROWS // 2
            for i in range(min(sources, tiles)):
                low = received[i, meta_at : meta_at + META_ROWS, :LANES]
                if i + tiles < sources:
                    high = received[i + tiles, meta_at : meta_at + META_ROWS, :LANES]
                    low = jnp.where(
                        first_half, low.astype(jnp.float32), high.astype(jnp.float32)
                    ).astype(low.dtype)
                out[k, bins:, i * LANES : (i + 1) * LANES] = low


def whole_vmem(count):
    return [pl.BlockSpec(memory_space=pltpu.VMEM)] * count


def centred_square(freq, length):
    half_length = length // 2
    value = ((freq + half_length) % length - half_length).astype(jnp.float32) / length
    return value * value


def slab_roles(batch_count, swapped):
    roles = list(range(batch_count))
    half = batch_count // 2
    if swapped:
        for b in range(1, half, 2):
            roles[b], roles[half + b - 1] = half + b - 1, b
    return roles


def slab_exchange(parts, place, slab_count, roles):
    arrived = []
    for shift in range(1, slab_count):
        perm = []
        for b, role in enumerate(roles):
            upper = role >= len(roles) // 2
            for source in range(slab_count):
                target = (source + shift) % slab_count
                if target < slab_count - 1:
                    ends = (slab_count - 1 - source, slab_count - 1 - target)
                    ends = ends if upper else (source, target)
                    perm.append((b * slab_count + ends[0], b * slab_count + ends[1]))
        block = choose(parts, (place + shift) % slab_count)
        arrived.append(lax.ppermute(block, ("batch", "slab"), perm))
    return arrived


def choose(parts, index):
    chosen = parts[-1]
    for d in range(parts.shape[0] - 1):
        chosen = jnp.where(index == d, parts[d], chosen)
    return chosen


def per_device(images, classes, shifts, defocus_class, defocus, run_counts, dest_map, ref):
    particles, length, _ = images.shape
    batch_count = lax.axis_size("batch")
    slab_count = lax.axis_size("slab")
    batch = lax.axis_index("batch")
    slab = lax.axis_index("slab")
    rows, planes, _ = ref.shape
    mirrored = slab_count == 4 and batch_count % 2 == 0 and 2 * particles <= META_ROWS
    mirrored = mirrored and batch_count * LANES <= 4 * length
    half_batch = batch_count // 2
    shares = [share for share, _ in CHUNKS]
    if rows % (8 * SHARES):
        shares = [SHARES // len(CHUNKS)] * len(CHUNKS)
    sizes = [rows * share // SHARES for share in shares]
    starts = [sum(sizes[:c]) for c in range(len(CHUNKS))]
    roles = [slab_roles(batch_count, mirrored and swapped) for _, swapped in CHUNKS]
    freq = jnp.arange(length, dtype=jnp.int32)

    fields = slab_count + 1

    cosine, minus_sine, table_right = dft_tables(length)
    table_right = jnp.asarray(table_right.astype(jnp.bfloat16))
    received = []
    weighted = []
    for c, each in enumerate(sizes):
        chunk_rows = batch_count * each
        block = np.array(roles[c])
        order = (block[:, None] * rows + starts[c] + np.arange(each)[None, :]).reshape(-1)
        left = np.concatenate([cosine[order], minus_sine[order]], axis=0)
        runs = [(k * rows + starts[c], k * rows + starts[c] + each) for k in block.tolist()]
        with_meta = c == 0
        block_rows = particles * each + META_ROWS * with_meta
        block_shape = (batch_count, block_rows, 2 * length)
        smem = pl.BlockSpec(memory_space=pltpu.SMEM)
        hbm = pl.BlockSpec(memory_space=pltpu.HBM)
        send = pl.pallas_call(
            functools.partial(spectrum_kernel, runs, with_meta),
            out_shape=jax.ShapeDtypeStruct(block_shape, jnp.bfloat16),
            in_specs=[smem] * 5 + [hbm] * 3,
            out_specs=hbm,
            scratch_shapes=[
                pltpu.VMEM((particles, length, length), jnp.bfloat16),
                pltpu.VMEM((2 * chunk_rows, length), jnp.bfloat16),
                pltpu.VMEM((2 * length, 2 * length), jnp.bfloat16),
                pltpu.VMEM((particles * chunk_rows, 2 * length), jnp.bfloat16),
                pltpu.VMEM(block_shape, jnp.bfloat16),
                pltpu.SemaphoreType.DMA((particles + 2,)),
                pltpu.SemaphoreType.DMA((particles // 2,)),
            ],
            compiler_params=pltpu.CompilerParams(vmem_limit_bytes=SPECTRUM_VMEM),
            cost_estimate=pl.CostEstimate(flops=0, bytes_accessed=0, transcendentals=0),
            name="spectrum",
        )(
            classes,
            shifts.T,
            defocus_class,
            defocus,
            run_counts.T,
            images,
            jnp.asarray(left.astype(jnp.bfloat16)),
            table_right,
        )
        weighted.append(send)
        received.append(lax.all_to_all(send, "batch", 0, 0, tiled=True))

    def read_digits(rows_in):
        whole = rows_in.astype(jnp.int32).reshape(-1, 2 * fields)
        return whole[:, :fields] * META_BASE + whole[:, fields:]

    meta_at = particles * sizes[0]
    meta_layer = read_digits(received[0][:, meta_at : meta_at + particles, : 2 * fields])

    class_count = dest_map.shape[0]

    dest_wide = dest_map.astype(jnp.bfloat16)

    def find_planes(table):
        class_hot = (table[:, :1] == jnp.arange(class_count)[None, :]).astype(jnp.bfloat16)
        local_plane = jnp.dot(class_hot, dest_wide, preferred_element_type=jnp.float32)
        past = freq[None, :, None] >= table[:, None, 2:]
        owner = jnp.sum(past.astype(jnp.int32), axis=2)
        return owner * planes + local_plane.astype(jnp.int32)

    def pick_block(table, block):
        return sum(
            jnp.where(block == k, table[:, k * rows : (k + 1) * rows], 0)
            for k in range(batch_count)
        )

    window_slabs = 3 if mirrored else slab_count
    blocks = [
        sum(jnp.where(batch == b, block, 0) for b, block in enumerate(role)) for role in roles
    ]
    layer_planes = find_planes(meta_layer)
    places, codes = [], []
    for c, each in enumerate(sizes):
        here = slice(starts[c], starts[c] + each)
        plane = pick_block(layer_planes, blocks[c])[:, here]
        place, owner_place = slab, plane // planes
        if mirrored:
            upper = blocks[c] >= half_batch
            owner_place = jnp.where(upper, slab_count - 1 - owner_place, owner_place)
            place = jnp.where(upper, slab_count - 1 - slab, slab)
        places.append(place)
        code = owner_place * (each * planes) + jnp.arange(each)[None, :] * planes
        code = (code + plane % planes).reshape(batch_count, particles * each)
        if c == 0:
            code = jnp.pad(code, ((0, 0), (0, META_ROWS)), constant_values=-1)
        codes.append(code.reshape(1, -1))

    sums, arrived = [], []
    for c, each in enumerate(sizes):
        bins = each * planes
        extra_rows = META_ROWS if c == 0 and mirrored else 0
        codes_in = codes[c]
        if c == 0:
            codes_in, _ = lax.optimization_barrier((codes_in, weighted[1:]))
        if c > 0 and mirrored:
            codes_in, arrived[c - 1][0], arrived[c - 1][2] = lax.optimization_barrier(
                (codes_in, arrived[c - 1][0], arrived[c - 1][2])
            )
        parts = pl.pallas_call(
            functools.partial(insert_kernel, bins, meta_at),
            out_shape=jax.ShapeDtypeStruct(
                (window_slabs, bins + extra_rows, 2 * length), jnp.bfloat16
            ),
            in_specs=whole_vmem(2),
            out_specs=pl.BlockSpec(memory_space=pltpu.VMEM),
            compiler_params=pltpu.CompilerParams(vmem_limit_bytes=INSERT_VMEM),
            cost_estimate=pl.CostEstimate(
                flops=0,
                bytes_accessed=0,
                transcendentals=0,
            ),
            name="insert",
        )(received[c], codes_in)
        if not mirrored:
            sums.append(lax.psum_scatter(parts, "slab", scatter_dimension=0, tiled=False))
            continue
        for before in arrived:
            before[1], _ = lax.optimization_barrier((before[1], parts))
        arrived.append(slab_exchange(parts, places[c], slab_count, roles[c]))
        own = choose(parts[:, :bins], places[c]).astype(jnp.float32)
        sums.append(jnp.where(places[c] == slab_count - 1, 0.0, own))
    for c, each in enumerate(sizes):
        if not mirrored:
            break
        over = [(b, block) for b, block in enumerate(roles[c]) if b != block]
        if over:
            if c + 1 < len(sizes):
                arrived[c][1], *arrived[-1] = lax.optimization_barrier(
                    (arrived[c][1], *arrived[-1])
                )
            for block in arrived[c]:
                sums[c] = sums[c] + block[: each * planes].astype(jnp.float32)
            handed = lax.ppermute(sums[c].astype(jnp.bfloat16), "batch", over)
            sums[c] = jnp.where(blocks[c] == batch, sums[c], handed.astype(jnp.float32))
            continue
        for block in arrived[c]:
            sums[c] = sums[c] + block[: each * planes].astype(jnp.float32)

    meta_all = [meta_layer]
    if mirrored:
        for block in [block[sizes[0] * planes :] for block in arrived[0]]:
            block = block.reshape(META_ROWS, -1, LANES)
            halves = (block[:particles], block[particles : 2 * particles])
            low = jnp.concatenate(halves, axis=1)[:, :batch_count, : 2 * fields]
            meta_all.append(read_digits(low.transpose(1, 0, 2)))
    else:
        for step in range(1, slab_count):
            ring = [(s, (s + step) % slab_count) for s in range(slab_count)]
            meta_all.append(lax.ppermute(meta_layer, "slab", ring))
    meta_all = jnp.concatenate(meta_all, axis=0)

    own_freq = batch * rows + jnp.arange(rows, dtype=jnp.int32)
    own_plane = pick_block(find_planes(meta_all), batch) - slab * planes
    focus_count = defocus.shape[0]
    focus_hot = (meta_all[:, 1:2] == jnp.arange(focus_count)[None, :]).astype(jnp.bfloat16)
    if mirrored:
        own_plane = jnp.where(places[0] == slab_count - 1, -1, own_plane)
    bin_hot = (own_plane.T[:, None, :] == jnp.arange(planes)[None, :, None]).astype(jnp.bfloat16)
    counts = jnp.einsum("kzp,pd->kzd", bin_hot, focus_hot, preferred_element_type=jnp.float32)
    row_angle = 2.0 * (
        defocus[None, :] * centred_square(own_freq, length)[:, None] + PHASE_OFFSET
    )
    col_angle = 2.0 * (defocus[:, None] * centred_square(freq, length)[None, :])
    row_side = jnp.concatenate(
        [counts * jnp.cos(row_angle)[:, None, :], counts * jnp.sin(row_angle)[:, None, :]], axis=2
    )
    col_side = jnp.concatenate([jnp.cos(col_angle), -jnp.sin(col_angle)], axis=0)
    double = jnp.einsum("kzd,dx->kzx", row_side, col_side, precision=lax.Precision.HIGHEST)
    weights = 0.5 * (jnp.sum(counts, axis=2, keepdims=True) - double)
    denom = weights + TAU_PRIOR

    updated = []
    for c, each in enumerate(sizes):
        here = slice(starts[c], starts[c] + each)
        prior = ref[here].astype(jnp.float32)
        under = denom[here]
        total = sums[c].astype(jnp.float32).reshape(each, planes, 2 * length)
        updated.append(
            (
                (TAU_PRIOR * prior + total) / jnp.concatenate([under, under], axis=2)
            ).astype(jnp.bfloat16)
        )
    return jnp.concatenate(updated, axis=0)


def solution(mesh):
    placed = (
        P(("batch", "slab"), None, None),
        P(("batch", "slab")),
        P(("batch", "slab"), None),
        P(("batch", "slab")),
        P(),
        P(("batch", "slab"), None),
        P(),
        P("batch", "slab", None),
    )
    return jax.shard_map(
        per_device, mesh=mesh, in_specs=placed, out_specs=P("batch", "slab", None), check_vma=False
    )
```

```python
import functools
import math

import jax
import jax.numpy as jnp
import numpy as np
from jax import lax
from jax.experimental import pallas as pl
from jax.experimental.pallas import tpu as pltpu
from jax.sharding import PartitionSpec as P

TAU_PRIOR = 4.0
PHASE_OFFSET = 0.1
CHUNKS = ((1, False), (2, True), (3, False))
SHARES = 6
META_BASE = 32
META_ROWS = 16
LANES = 128
SPECTRUM_VMEM = 60 * 1024 * 1024
INSERT_VMEM = 32 * 1024 * 1024


def dft_tables(length):
    index = np.arange(length, dtype=np.int32)
    turns = index[:, None] * index[None, :] % length
    angle = np.float32(2.0 * math.pi / length) * turns.astype(np.float32)
    factor = np.float32(1.0 / math.sqrt(length))
    cosine = np.cos(angle) * factor
    sine = np.sin(angle) * factor
    upper_rows = np.concatenate([cosine, -sine], axis=1)
    lower_rows = np.concatenate([sine, cosine], axis=1)
    table_right = np.concatenate([upper_rows, lower_rows], axis=0)
    return cosine, -sine, table_right


def spread(iota, values):
    out = jnp.full(iota.shape, values[0])
    for p in range(1, len(values)):
        out = jnp.where(iota == p, values[p], out)
    return out


def sin_turns(turns):
    half = jnp.floor(2.0 * turns + 0.5)
    x = (2.0 * math.pi) * (turns - 0.5 * half)
    sign = 1.0 - 2.0 * (half - 2.0 * jnp.floor(0.5 * half))
    square = x * x
    series = jnp.full(x.shape, -1.0 / math.factorial(11), jnp.float32)
    for power in (9, 7, 5, 3, 1):
        series = series * square + (1.0 if power % 4 == 1 else -1.0) / math.factorial(power)
    return sign * x * series


def phase_turns(freq, shift, length):
    steps = freq * shift
    steps = steps - length * jnp.floor(steps * (1.0 / length))
    return steps * (1.0 / length)


def centred(freq, length):
    return jnp.where(freq < length // 2, freq, freq - length) * (1.0 / length)


def spectrum_kernel(
    runs,
    with_meta,
    classes,
    shifts,
    defocus_class,
    defocus,
    run_counts,
    images_in,
    left_in,
    right_in,
    out,
    images,
    left,
    right,
    joined,
    block,
    load_sems,
    send_sems,
):
    particles, length = images.shape[0], images.shape[1]
    owners = out.shape[0]
    rows_each = runs[0][1] - runs[0][0]
    rows = owners * rows_each
    loads = [pltpu.make_async_copy(left_in, left, load_sems.at[0])]
    for p in range(particles):
        loads.append(pltpu.make_async_copy(images_in.at[p], images.at[p], load_sems.at[1 + p]))
    loads.append(pltpu.make_async_copy(right_in, right, load_sems.at[1 + particles]))
    for load in loads:
        load.start()

    every = range(particles)
    focus = [defocus[defocus_class[p]] for p in every]
    shift_x = [shifts[0, p].astype(jnp.float32) for p in every]
    shift_y = [shifts[1, p].astype(jnp.float32) for p in every]
    sublane = lax.broadcasted_iota(jnp.int32, (particles, length), 0)
    freq_x = lax.broadcasted_iota(jnp.int32, (particles, length), 1).astype(jnp.float32)
    phase_x = phase_turns(freq_x, spread(sublane, shift_x), length)
    angle_x = spread(sublane, focus) * centred(freq_x, length) * centred(freq_x, length)
    angle_x = angle_x * (0.5 / math.pi)
    col = [sin_turns(at) for at in (phase_x, phase_x + 0.25, angle_x, angle_x + 0.25)]
    lane = lax.broadcasted_iota(jnp.int32, (rows, LANES), 1)
    which = lane % particles
    quantity = lane // particles
    row_at = lax.broadcasted_iota(jnp.int32, (rows, LANES), 0)
    owner = row_at // rows_each
    freq_y = row_at - owner * rows_each + spread(owner, [begin for begin, _ in runs])
    freq_y = freq_y.astype(jnp.float32)
    phase_y = phase_turns(freq_y, spread(which, shift_y), length)
    angle_y = spread(which, focus) * centred(freq_y, length) * centred(freq_y, length)
    angle_y = (angle_y + PHASE_OFFSET) * (0.5 / math.pi)
    row = jnp.where(quantity < 2, phase_y, angle_y)
    row = sin_turns(row + jnp.where(quantity % 2 == 1, 0.25, 0.0))

    if with_meta:
        digits = jnp.zeros((META_ROWS, LANES), jnp.int32)
        at_row = lax.broadcasted_iota(jnp.int32, (META_ROWS, LANES), 0) % particles
        at_lane = lax.broadcasted_iota(jnp.int32, (META_ROWS, LANES), 1)
        ends = [[run_counts[0, p] for p in every]]
        for s in range(1, run_counts.shape[0] - 1):
            ends.append([ends[-1][p] + run_counts[s, p] for p in every])
        fields = [[classes[p] for p in every], [defocus_class[p] for p in every], *ends]
        for f, values in enumerate(fields):
            value = spread(at_row, values)
            digits = jnp.where(at_lane == f, value // META_BASE, digits)
            digits = jnp.where(at_lane == f + len(fields), value % META_BASE, digits)
        digits = digits.astype(jnp.float32).astype(jnp.bfloat16)
        for d in range(owners):
            block[d, particles * rows_each :, :] = jnp.zeros(
                (META_ROWS, 2 * length), jnp.bfloat16
            )
            block[d, particles * rows_each :, :LANES] = digits

    loads[0].wait()
    table = left[...]
    for p in range(particles):
        loads[1 + p].wait()
        section = jnp.dot(table, images[p], preferred_element_type=jnp.float32)
        section = section.astype(jnp.bfloat16)
        joined[p * rows : (p + 1) * rows, :length] = section[:rows]
        joined[p * rows : (p + 1) * rows, length:] = section[rows:]
    loads[1 + particles].wait()
    sends = []
    for first in range(0, particles, 2):
        spectrum = jnp.dot(
            joined[first * rows : (first + 2) * rows, :],
            right[...],
            preferred_element_type=jnp.float32,
        )
        for p in range(first, first + 2):
            part = spectrum[(p - first) * rows : (p - first + 1) * rows]
            real_part, imag_part = part[:, :length], part[:, length:]
            row_sin, row_cos, row_ctf_sin, row_ctf_cos = [
                row[:, q * particles + p : q * particles + p + 1] for q in range(4)
            ]
            col_sin, col_cos, col_ctf_sin, col_ctf_cos = [part[p : p + 1, :] for part in col]
            transfer = -(row_ctf_sin * col_ctf_cos + row_ctf_cos * col_ctf_sin)
            cosine = transfer * (row_cos * col_cos - row_sin * col_sin)
            sine = transfer * (row_sin * col_cos + row_cos * col_sin)
            real_new = real_part * cosine + imag_part * sine
            imag_new = imag_part * cosine - real_part * sine
            weighted = jnp.concatenate([real_new, imag_new], axis=1).astype(jnp.bfloat16)
            block[:, p * rows_each : (p + 1) * rows_each, :] = weighted.reshape(
                owners, rows_each, 2 * length
            )
        done = pl.ds(first * rows_each, 2 * rows_each)
        if with_meta and first + 2 == particles:
            done = pl.ds(first * rows_each, 2 * rows_each + META_ROWS)
        sends.append(
            pltpu.make_async_copy(block.at[:, done], out.at[:, done], send_sems.at[first // 2])
        )
        sends[-1].start()
    for send in sends:
        send.wait()


def insert_kernel(bins, meta_at, received, codes, out):
    sources = received.shape[0]
    rows = received[...].reshape(-1, received.shape[2])
    codes_all = codes[...]
    for k in range(out.shape[0]):
        bin_index = lax.broadcasted_iota(jnp.int32, (bins, 1), 0) + k * bins
        hot = jnp.where(codes_all == bin_index, 1.0, 0.0).astype(jnp.bfloat16)
        total = jnp.dot(hot, rows, preferred_element_type=jnp.float32)
        out[k, :bins, :] = total.astype(out.dtype)
        if out.shape[1] > bins:
            tiles = out.shape[2] // LANES
            first_half = lax.broadcasted_iota(jnp.int32, (META_ROWS, LANES), 0) < META_ROWS // 2
            for i in range(min(sources, tiles)):
                low = received[i, meta_at : meta_at + META_ROWS, :LANES]
                if i + tiles < sources:
                    high = received[i + tiles, meta_at : meta_at + META_ROWS, :LANES]
                    low = jnp.where(
                        first_half, low.astype(jnp.float32), high.astype(jnp.float32)
                    ).astype(low.dtype)
                out[k, bins:, i * LANES : (i + 1) * LANES] = low


def whole_vmem(count):
    return [pl.BlockSpec(memory_space=pltpu.VMEM)] * count


def centred_square(freq, length):
    half_length = length // 2
    value = ((freq + half_length) % length - half_length).astype(jnp.float32) / length
    return value * value


def slab_roles(batch_count, swapped):
    roles = list(range(batch_count))
    half = batch_count // 2
    if swapped:
        for b in range(1, half, 2):
            roles[b], roles[half + b - 1] = half + b - 1, b
    return roles


def slab_exchange(parts, place, slab_count, roles):
    arrived = []
    for shift in range(1, slab_count):
        perm = []
        for b, role in enumerate(roles):
            upper = role >= len(roles) // 2
            for source in range(slab_count):
                target = (source + shift) % slab_count
                if target < slab_count - 1:
                    ends = (slab_count - 1 - source, slab_count - 1 - target)
                    ends = ends if upper else (source, target)
                    perm.append((b * slab_count + ends[0], b * slab_count + ends[1]))
        block = choose(parts, (place + shift) % slab_count)
        arrived.append(lax.ppermute(block, ("batch", "slab"), perm))
    return arrived


def choose(parts, index):
    chosen = parts[-1]
    for d in range(parts.shape[0] - 1):
        chosen = jnp.where(index == d, parts[d], chosen)
    return chosen


def per_device(images, classes, shifts, defocus_class, defocus, run_counts, dest_map, ref):
    particles, length, _ = images.shape
    batch_count = lax.axis_size("batch")
    slab_count = lax.axis_size("slab")
    batch = lax.axis_index("batch")
    slab = lax.axis_index("slab")
    rows, planes, _ = ref.shape
    mirrored = slab_count == 4 and batch_count % 2 == 0 and 2 * particles <= META_ROWS
    mirrored = mirrored and batch_count * LANES <= 4 * length
    half_batch = batch_count // 2
    shares = [share for share, _ in CHUNKS]
    if rows % (8 * SHARES):
        shares = [SHARES // len(CHUNKS)] * len(CHUNKS)
    sizes = [rows * share // SHARES for share in shares]
    starts = [sum(sizes[:c]) for c in range(len(CHUNKS))]
    roles = [slab_roles(batch_count, mirrored and swapped) for _, swapped in CHUNKS]
    freq = jnp.arange(length, dtype=jnp.int32)

    fields = slab_count + 1

    cosine, minus_sine, table_right = dft_tables(length)
    table_right = jnp.asarray(table_right.astype(jnp.bfloat16))
    received = []
    weighted = []
    for c, each in enumerate(sizes):
        chunk_rows = batch_count * each
        block = np.array(roles[c])
        order = (block[:, None] * rows + starts[c] + np.arange(each)[None, :]).reshape(-1)
        left = np.concatenate([cosine[order], minus_sine[order]], axis=0)
        runs = [(k * rows + starts[c], k * rows + starts[c] + each) for k in block.tolist()]
        with_meta = c == 0
        block_rows = particles * each + META_ROWS * with_meta
        block_shape = (batch_count, block_rows, 2 * length)
        smem = pl.BlockSpec(memory_space=pltpu.SMEM)
        hbm = pl.BlockSpec(memory_space=pltpu.HBM)
        send = pl.pallas_call(
            functools.partial(spectrum_kernel, runs, with_meta),
            out_shape=jax.ShapeDtypeStruct(block_shape, jnp.bfloat16),
            in_specs=[smem] * 5 + [hbm] * 3,
            out_specs=hbm,
            scratch_shapes=[
                pltpu.VMEM((particles, length, length), jnp.bfloat16),
                pltpu.VMEM((2 * chunk_rows, length), jnp.bfloat16),
                pltpu.VMEM((2 * length, 2 * length), jnp.bfloat16),
                pltpu.VMEM((particles * chunk_rows, 2 * length), jnp.bfloat16),
                pltpu.VMEM(block_shape, jnp.bfloat16),
                pltpu.SemaphoreType.DMA((particles + 2,)),
                pltpu.SemaphoreType.DMA((particles // 2,)),
            ],
            compiler_params=pltpu.CompilerParams(vmem_limit_bytes=SPECTRUM_VMEM),
            cost_estimate=pl.CostEstimate(flops=0, bytes_accessed=0, transcendentals=0),
            name="spectrum",
        )(
            classes,
            shifts.T,
            defocus_class,
            defocus,
            run_counts.T,
            images,
            jnp.asarray(left.astype(jnp.bfloat16)),
            table_right,
        )
        weighted.append(send)
        received.append(lax.all_to_all(send, "batch", 0, 0, tiled=True))

    def read_digits(rows_in):
        whole = rows_in.astype(jnp.int32).reshape(-1, 2 * fields)
        return whole[:, :fields] * META_BASE + whole[:, fields:]

    meta_at = particles * sizes[0]
    meta_layer = read_digits(received[0][:, meta_at : meta_at + particles, : 2 * fields])

    class_count = dest_map.shape[0]

    dest_wide = dest_map.astype(jnp.bfloat16)

    def find_planes(table):
        class_hot = (table[:, :1] == jnp.arange(class_count)[None, :]).astype(jnp.bfloat16)
        local_plane = jnp.dot(class_hot, dest_wide, preferred_element_type=jnp.float32)
        past = freq[None, :, None] >= table[:, None, 2:]
        owner = jnp.sum(past.astype(jnp.int32), axis=2)
        return owner * planes + local_plane.astype(jnp.int32)

    def pick_block(table, block):
        return sum(
            jnp.where(block == k, table[:, k * rows : (k + 1) * rows], 0)
            for k in range(batch_count)
        )

    window_slabs = 3 if mirrored else slab_count
    blocks = [
        sum(jnp.where(batch == b, block, 0) for b, block in enumerate(role)) for role in roles
    ]
    layer_planes = find_planes(meta_layer)
    places, codes = [], []
    for c, each in enumerate(sizes):
        here = slice(starts[c], starts[c] + each)
        plane = pick_block(layer_planes, blocks[c])[:, here]
        place, owner_place = slab, plane // planes
        if mirrored:
            upper = blocks[c] >= half_batch
            owner_place = jnp.where(upper, slab_count - 1 - owner_place, owner_place)
            place = jnp.where(upper, slab_count - 1 - slab, slab)
        places.append(place)
        code = owner_place * (each * planes) + jnp.arange(each)[None, :] * planes
        code = (code + plane % planes).reshape(batch_count, particles * each)
        if c == 0:
            code = jnp.pad(code, ((0, 0), (0, META_ROWS)), constant_values=-1)
        codes.append(code.reshape(1, -1))

    sums, arrived = [], []
    for c, each in enumerate(sizes):
        bins = each * planes
        extra_rows = META_ROWS if c == 0 and mirrored else 0
        codes_in = codes[c]
        if c == 0:
            codes_in, _ = lax.optimization_barrier((codes_in, weighted[1:]))
        if c > 0 and mirrored:
            codes_in, arrived[c - 1][0], arrived[c - 1][2] = lax.optimization_barrier(
                (codes_in, arrived[c - 1][0], arrived[c - 1][2])
            )
        parts = pl.pallas_call(
            functools.partial(insert_kernel, bins, meta_at),
            out_shape=jax.ShapeDtypeStruct(
                (window_slabs, bins + extra_rows, 2 * length), jnp.bfloat16
            ),
            in_specs=whole_vmem(2),
            out_specs=pl.BlockSpec(memory_space=pltpu.VMEM),
            compiler_params=pltpu.CompilerParams(vmem_limit_bytes=INSERT_VMEM),
            cost_estimate=pl.CostEstimate(
                flops=0,
                bytes_accessed=0,
                transcendentals=0,
            ),
            name="insert",
        )(received[c], codes_in)
        if not mirrored:
            sums.append(lax.psum_scatter(parts, "slab", scatter_dimension=0, tiled=False))
            continue
        for before in arrived:
            before[1], _ = lax.optimization_barrier((before[1], parts))
        arrived.append(slab_exchange(parts, places[c], slab_count, roles[c]))
        own = choose(parts[:, :bins], places[c]).astype(jnp.float32)
        sums.append(jnp.where(places[c] == slab_count - 1, 0.0, own))
    for c, each in enumerate(sizes):
        if not mirrored:
            break
        for block in arrived[c]:
            sums[c] = sums[c] + block[: each * planes].astype(jnp.float32)
        over = [(b, block) for b, block in enumerate(roles[c]) if b != block]
        if over:
            if c + 1 < len(sizes):
                sums[c], arrived[c + 1][2] = lax.optimization_barrier(
                    (sums[c], arrived[c + 1][2])
                )
            handed = lax.ppermute(sums[c].astype(jnp.bfloat16), "batch", over)
            sums[c] = jnp.where(blocks[c] == batch, sums[c], handed.astype(jnp.float32))

    meta_all = [meta_layer]
    if mirrored:
        for block in [block[sizes[0] * planes :] for block in arrived[0]]:
            block = block.reshape(META_ROWS, -1, LANES)
            halves = (block[:particles], block[particles : 2 * particles])
            low = jnp.concatenate(halves, axis=1)[:, :batch_count, : 2 * fields]
            meta_all.append(read_digits(low.transpose(1, 0, 2)))
    else:
        for step in range(1, slab_count):
            ring = [(s, (s + step) % slab_count) for s in range(slab_count)]
            meta_all.append(lax.ppermute(meta_layer, "slab", ring))
    meta_all = jnp.concatenate(meta_all, axis=0)

    own_freq = batch * rows + jnp.arange(rows, dtype=jnp.int32)
    own_plane = pick_block(find_planes(meta_all), batch) - slab * planes
    focus_count = defocus.shape[0]
    focus_hot = (meta_all[:, 1:2] == jnp.arange(focus_count)[None, :]).astype(jnp.bfloat16)
    if mirrored:
        own_plane = jnp.where(places[0] == slab_count - 1, -1, own_plane)
    bin_hot = (own_plane.T[:, None, :] == jnp.arange(planes)[None, :, None]).astype(jnp.bfloat16)
    counts = jnp.einsum("kzp,pd->kzd", bin_hot, focus_hot, preferred_element_type=jnp.float32)
    row_angle = 2.0 * (
        defocus[None, :] * centred_square(own_freq, length)[:, None] + PHASE_OFFSET
    )
    col_angle = 2.0 * (defocus[:, None] * centred_square(freq, length)[None, :])
    row_side = jnp.concatenate(
        [counts * jnp.cos(row_angle)[:, None, :], counts * jnp.sin(row_angle)[:, None, :]], axis=2
    )
    col_side = jnp.concatenate([jnp.cos(col_angle), -jnp.sin(col_angle)], axis=0)
    double = jnp.einsum("kzd,dx->kzx", row_side, col_side, precision=lax.Precision.HIGHEST)
    weights = 0.5 * (jnp.sum(counts, axis=2, keepdims=True) - double)
    denom = weights + TAU_PRIOR

    updated = []
    for c, each in enumerate(sizes):
        here = slice(starts[c], starts[c] + each)
        prior = ref[here].astype(jnp.float32)
        under = denom[here]
        total = sums[c].astype(jnp.float32).reshape(each, planes, 2 * length)
        updated.append(
            (
                (TAU_PRIOR * prior + total) / jnp.concatenate([under, under], axis=2)
            ).astype(jnp.bfloat16)
        )
    return jnp.concatenate(updated, axis=0)


def solution(mesh):
    placed = (
        P(("batch", "slab"), None, None),
        P(("batch", "slab")),
        P(("batch", "slab"), None),
        P(("batch", "slab")),
        P(),
        P(("batch", "slab"), None),
        P(),
        P("batch", "slab", None),
    )
    return jax.shard_map(
        per_device, mesh=mesh, in_specs=placed, out_specs=P("batch", "slab", None), check_vma=False
    )
```

```python
import functools
import math

import jax
import jax.numpy as jnp
import numpy as np
from jax import lax
from jax.experimental import pallas as pl
from jax.experimental.pallas import tpu as pltpu
from jax.sharding import PartitionSpec as P

TAU_PRIOR = 4.0
PHASE_OFFSET = 0.1
CHUNKS = ((2, False), (2, True), (2, False))
SHARES = 6
META_BASE = 32
META_ROWS = 16
LANES = 128
SPECTRUM_VMEM = 60 * 1024 * 1024
INSERT_VMEM = 32 * 1024 * 1024


def dft_tables(length):
    index = np.arange(length, dtype=np.int32)
    turns = index[:, None] * index[None, :] % length
    angle = np.float32(2.0 * math.pi / length) * turns.astype(np.float32)
    factor = np.float32(1.0 / math.sqrt(length))
    cosine = np.cos(angle) * factor
    sine = np.sin(angle) * factor
    upper_rows = np.concatenate([cosine, -sine], axis=1)
    lower_rows = np.concatenate([sine, cosine], axis=1)
    table_right = np.concatenate([upper_rows, lower_rows], axis=0)
    return cosine, -sine, table_right


def spread(iota, values):
    out = jnp.full(iota.shape, values[0])
    for p in range(1, len(values)):
        out = jnp.where(iota == p, values[p], out)
    return out


def sin_turns(turns):
    half = jnp.floor(2.0 * turns + 0.5)
    x = (2.0 * math.pi) * (turns - 0.5 * half)
    sign = 1.0 - 2.0 * (half - 2.0 * jnp.floor(0.5 * half))
    square = x * x
    series = jnp.full(x.shape, -1.0 / math.factorial(11), jnp.float32)
    for power in (9, 7, 5, 3, 1):
        series = series * square + (1.0 if power % 4 == 1 else -1.0) / math.factorial(power)
    return sign * x * series


def phase_turns(freq, shift, length):
    steps = freq * shift
    steps = steps - length * jnp.floor(steps * (1.0 / length))
    return steps * (1.0 / length)


def centred(freq, length):
    return jnp.where(freq < length // 2, freq, freq - length) * (1.0 / length)


def spectrum_kernel(
    runs,
    with_meta,
    classes,
    shifts,
    defocus_class,
    defocus,
    run_counts,
    images_in,
    left_in,
    right_in,
    out,
    images,
    left,
    right,
    joined,
    block,
    load_sems,
    send_sems,
):
    particles, length = images.shape[0], images.shape[1]
    owners = out.shape[0]
    rows_each = runs[0][1] - runs[0][0]
    rows = owners * rows_each
    loads = [pltpu.make_async_copy(left_in, left, load_sems.at[0])]
    for p in range(particles):
        loads.append(pltpu.make_async_copy(images_in.at[p], images.at[p], load_sems.at[1 + p]))
    loads.append(pltpu.make_async_copy(right_in, right.at[:length], load_sems.at[1 + particles]))
    for load in loads:
        load.start()

    every = range(particles)
    focus = [defocus[defocus_class[p]] for p in every]
    shift_x = [shifts[0, p].astype(jnp.float32) for p in every]
    shift_y = [shifts[1, p].astype(jnp.float32) for p in every]
    sublane = lax.broadcasted_iota(jnp.int32, (particles, length), 0)
    freq_x = lax.broadcasted_iota(jnp.int32, (particles, length), 1).astype(jnp.float32)
    phase_x = phase_turns(freq_x, spread(sublane, shift_x), length)
    angle_x = spread(sublane, focus) * centred(freq_x, length) * centred(freq_x, length)
    angle_x = angle_x * (0.5 / math.pi)
    col = [sin_turns(at) for at in (phase_x, phase_x + 0.25, angle_x, angle_x + 0.25)]
    lane = lax.broadcasted_iota(jnp.int32, (rows, LANES), 1)
    which = lane % particles
    quantity = lane // particles
    row_at = lax.broadcasted_iota(jnp.int32, (rows, LANES), 0)
    owner = row_at // rows_each
    freq_y = row_at - owner * rows_each + spread(owner, [begin for begin, _ in runs])
    freq_y = freq_y.astype(jnp.float32)
    phase_y = phase_turns(freq_y, spread(which, shift_y), length)
    angle_y = spread(which, focus) * centred(freq_y, length) * centred(freq_y, length)
    angle_y = (angle_y + PHASE_OFFSET) * (0.5 / math.pi)
    row = jnp.where(quantity < 2, phase_y, angle_y)
    row = sin_turns(row + jnp.where(quantity % 2 == 1, 0.25, 0.0))

    if with_meta:
        digits = jnp.zeros((META_ROWS, LANES), jnp.int32)
        at_row = lax.broadcasted_iota(jnp.int32, (META_ROWS, LANES), 0) % particles
        at_lane = lax.broadcasted_iota(jnp.int32, (META_ROWS, LANES), 1)
        ends = [[run_counts[0, p] for p in every]]
        for s in range(1, run_counts.shape[0] - 1):
            ends.append([ends[-1][p] + run_counts[s, p] for p in every])
        fields = [[classes[p] for p in every], [defocus_class[p] for p in every], *ends]
        for f, values in enumerate(fields):
            value = spread(at_row, values)
            digits = jnp.where(at_lane == f, value // META_BASE, digits)
            digits = jnp.where(at_lane == f + len(fields), value % META_BASE, digits)
        digits = digits.astype(jnp.float32).astype(jnp.bfloat16)
        for d in range(owners):
            block[d, particles * rows_each :, :] = jnp.zeros(
                (META_ROWS, 2 * length), jnp.bfloat16
            )
            block[d, particles * rows_each :, :LANES] = digits

    loads[0].wait()
    table = left[...]
    for p in range(particles):
        loads[1 + p].wait()
        section = jnp.dot(table, images[p], preferred_element_type=jnp.float32)
        section = section.astype(jnp.bfloat16)
        joined[p * rows : (p + 1) * rows, :length] = section[:rows]
        joined[p * rows : (p + 1) * rows, length:] = section[rows:]
    loads[1 + particles].wait()
    right[length:, :length] = -right[:length, length:]
    right[length:, length:] = right[:length, :length]
    sends = []
    for first in range(0, particles, 2):
        spectrum = jnp.dot(
            joined[first * rows : (first + 2) * rows, :],
            right[...],
            preferred_element_type=jnp.float32,
        )
        for p in range(first, first + 2):
            part = spectrum[(p - first) * rows : (p - first + 1) * rows]
            real_part, imag_part = part[:, :length], part[:, length:]
            row_sin, row_cos, row_ctf_sin, row_ctf_cos = [
                row[:, q * particles + p : q * particles + p + 1] for q in range(4)
            ]
            col_sin, col_cos, col_ctf_sin, col_ctf_cos = [part[p : p + 1, :] for part in col]
            transfer = -(row_ctf_sin * col_ctf_cos + row_ctf_cos * col_ctf_sin)
            cosine = transfer * (row_cos * col_cos - row_sin * col_sin)
            sine = transfer * (row_sin * col_cos + row_cos * col_sin)
            real_new = real_part * cosine + imag_part * sine
            imag_new = imag_part * cosine - real_part * sine
            weighted = jnp.concatenate([real_new, imag_new], axis=1).astype(jnp.bfloat16)
            block[:, p * rows_each : (p + 1) * rows_each, :] = weighted.reshape(
                owners, rows_each, 2 * length
            )
        done = pl.ds(first * rows_each, 2 * rows_each)
        if with_meta and first + 2 == particles:
            done = pl.ds(first * rows_each, 2 * rows_each + META_ROWS)
        sends.append(
            pltpu.make_async_copy(block.at[:, done], out.at[:, done], send_sems.at[first // 2])
        )
        sends[-1].start()
    for send in sends:
        send.wait()


def insert_kernel(bins, meta_at, received, codes, out):
    sources = received.shape[0]
    rows = received[...].reshape(-1, received.shape[2])
    codes_all = codes[...]
    for k in range(out.shape[0]):
        bin_index = lax.broadcasted_iota(jnp.int32, (bins, 1), 0) + k * bins
        hot = jnp.where(codes_all == bin_index, 1.0, 0.0).astype(jnp.bfloat16)
        total = jnp.dot(hot, rows, preferred_element_type=jnp.float32)
        out[k, :bins, :] = total.astype(out.dtype)
        if out.shape[1] > bins:
            tiles = out.shape[2] // LANES
            first_half = lax.broadcasted_iota(jnp.int32, (META_ROWS, LANES), 0) < META_ROWS // 2
            for i in range(min(sources, tiles)):
                low = received[i, meta_at : meta_at + META_ROWS, :LANES]
                if i + tiles < sources:
                    high = received[i + tiles, meta_at : meta_at + META_ROWS, :LANES]
                    low = jnp.where(
                        first_half, low.astype(jnp.float32), high.astype(jnp.float32)
                    ).astype(low.dtype)
                out[k, bins:, i * LANES : (i + 1) * LANES] = low


def whole_vmem(count):
    return [pl.BlockSpec(memory_space=pltpu.VMEM)] * count


def centred_square(freq, length):
    half_length = length // 2
    value = ((freq + half_length) % length - half_length).astype(jnp.float32) / length
    return value * value


def slab_roles(batch_count, swapped):
    roles = list(range(batch_count))
    half = batch_count // 2
    if swapped:
        for b in range(1, half, 2):
            roles[b], roles[half + b - 1] = half + b - 1, b
    return roles


def slab_exchange(parts, place, slab_count, roles):
    arrived = []
    for shift in range(1, slab_count):
        perm = []
        for b, role in enumerate(roles):
            upper = role >= len(roles) // 2
            for source in range(slab_count):
                target = (source + shift) % slab_count
                if target < slab_count - 1:
                    ends = (slab_count - 1 - source, slab_count - 1 - target)
                    ends = ends if upper else (source, target)
                    perm.append((b * slab_count + ends[0], b * slab_count + ends[1]))
        block = choose(parts, (place + shift) % slab_count)
        arrived.append(lax.ppermute(block, ("batch", "slab"), perm))
    return arrived


def choose(parts, index):
    chosen = parts[-1]
    for d in range(parts.shape[0] - 1):
        chosen = jnp.where(index == d, parts[d], chosen)
    return chosen


def per_device(images, classes, shifts, defocus_class, defocus, run_counts, dest_map, ref):
    particles, length, _ = images.shape
    batch_count = lax.axis_size("batch")
    slab_count = lax.axis_size("slab")
    batch = lax.axis_index("batch")
    slab = lax.axis_index("slab")
    rows, planes, _ = ref.shape
    mirrored = slab_count == 4 and batch_count % 2 == 0 and 2 * particles <= META_ROWS
    mirrored = mirrored and batch_count * LANES <= 4 * length
    half_batch = batch_count // 2
    sizes = [rows * share // SHARES for share, _ in CHUNKS]
    starts = [sum(sizes[:c]) for c in range(len(CHUNKS))]
    roles = [slab_roles(batch_count, mirrored and swapped) for _, swapped in CHUNKS]
    freq = jnp.arange(length, dtype=jnp.int32)

    fields = slab_count + 1

    cosine, minus_sine, table_right = dft_tables(length)
    table_right = jnp.asarray(table_right[:length].astype(jnp.bfloat16))
    received = []
    weighted = []
    for c, each in enumerate(sizes):
        chunk_rows = batch_count * each
        block = np.array(roles[c])
        order = (block[:, None] * rows + starts[c] + np.arange(each)[None, :]).reshape(-1)
        left = np.concatenate([cosine[order], minus_sine[order]], axis=0)
        runs = [(k * rows + starts[c], k * rows + starts[c] + each) for k in block.tolist()]
        with_meta = c == 0
        block_rows = particles * each + META_ROWS * with_meta
        block_shape = (batch_count, block_rows, 2 * length)
        smem = pl.BlockSpec(memory_space=pltpu.SMEM)
        hbm = pl.BlockSpec(memory_space=pltpu.HBM)
        send = pl.pallas_call(
            functools.partial(spectrum_kernel, runs, with_meta),
            out_shape=jax.ShapeDtypeStruct(block_shape, jnp.bfloat16),
            in_specs=[smem] * 5 + [hbm] * 3,
            out_specs=hbm,
            scratch_shapes=[
                pltpu.VMEM((particles, length, length), jnp.bfloat16),
                pltpu.VMEM((2 * chunk_rows, length), jnp.bfloat16),
                pltpu.VMEM((2 * length, 2 * length), jnp.bfloat16),
                pltpu.VMEM((particles * chunk_rows, 2 * length), jnp.bfloat16),
                pltpu.VMEM(block_shape, jnp.bfloat16),
                pltpu.SemaphoreType.DMA((particles + 2,)),
                pltpu.SemaphoreType.DMA((particles // 2,)),
            ],
            compiler_params=pltpu.CompilerParams(vmem_limit_bytes=SPECTRUM_VMEM),
            cost_estimate=pl.CostEstimate(flops=0, bytes_accessed=0, transcendentals=0),
            name="spectrum",
        )(
            classes,
            shifts.T,
            defocus_class,
            defocus,
            run_counts.T,
            images,
            jnp.asarray(left.astype(jnp.bfloat16)),
            table_right,
        )
        weighted.append(send)
        received.append(lax.all_to_all(send, "batch", 0, 0, tiled=True))

    def read_digits(rows_in):
        whole = rows_in.astype(jnp.int32).reshape(-1, 2 * fields)
        return whole[:, :fields] * META_BASE + whole[:, fields:]

    meta_at = particles * sizes[0]
    meta_layer = read_digits(received[0][:, meta_at : meta_at + particles, : 2 * fields])

    class_count = dest_map.shape[0]

    dest_wide = dest_map.astype(jnp.bfloat16)

    def find_planes(table):
        class_hot = (table[:, :1] == jnp.arange(class_count)[None, :]).astype(jnp.bfloat16)
        local_plane = jnp.dot(class_hot, dest_wide, preferred_element_type=jnp.float32)
        past = freq[None, :, None] >= table[:, None, 2:]
        owner = jnp.sum(past.astype(jnp.int32), axis=2)
        return owner * planes + local_plane.astype(jnp.int32)

    def pick_block(table, block):
        return sum(
            jnp.where(block == k, table[:, k * rows : (k + 1) * rows], 0)
            for k in range(batch_count)
        )

    window_slabs = 3 if mirrored else slab_count
    blocks = [
        sum(jnp.where(batch == b, block, 0) for b, block in enumerate(role)) for role in roles
    ]
    layer_planes = find_planes(meta_layer)
    places, codes = [], []
    for c, each in enumerate(sizes):
        here = slice(starts[c], starts[c] + each)
        plane = pick_block(layer_planes, blocks[c])[:, here]
        place, owner_place = slab, plane // planes
        if mirrored:
            upper = blocks[c] >= half_batch
            owner_place = jnp.where(upper, slab_count - 1 - owner_place, owner_place)
            place = jnp.where(upper, slab_count - 1 - slab, slab)
        places.append(place)
        code = owner_place * (each * planes) + jnp.arange(each)[None, :] * planes
        code = (code + plane % planes).reshape(batch_count, particles * each)
        if c == 0:
            code = jnp.pad(code, ((0, 0), (0, META_ROWS)), constant_values=-1)
        codes.append(code.reshape(1, -1))

    sums, arrived = [], []
    for c, each in enumerate(sizes):
        bins = each * planes
        extra_rows = META_ROWS if c == 0 and mirrored else 0
        codes_in = codes[c]
        if c == 0:
            codes_in, _ = lax.optimization_barrier((codes_in, weighted[1:]))
        if c > 0 and mirrored:
            codes_in, arrived[c - 1][0], arrived[c - 1][2] = lax.optimization_barrier(
                (codes_in, arrived[c - 1][0], arrived[c - 1][2])
            )
        parts = pl.pallas_call(
            functools.partial(insert_kernel, bins, meta_at),
            out_shape=jax.ShapeDtypeStruct(
                (window_slabs, bins + extra_rows, 2 * length), jnp.bfloat16
            ),
            in_specs=whole_vmem(2),
            out_specs=pl.BlockSpec(memory_space=pltpu.VMEM),
            compiler_params=pltpu.CompilerParams(vmem_limit_bytes=INSERT_VMEM),
            cost_estimate=pl.CostEstimate(
                flops=0,
                bytes_accessed=0,
                transcendentals=0,
            ),
            name="insert",
        )(received[c], codes_in)
        if not mirrored:
            sums.append(lax.psum_scatter(parts, "slab", scatter_dimension=0, tiled=False))
            continue
        for before in arrived:
            before[1], _ = lax.optimization_barrier((before[1], parts))
        arrived.append(slab_exchange(parts, places[c], slab_count, roles[c]))
        own = choose(parts[:, :bins], places[c]).astype(jnp.float32)
        sums.append(jnp.where(places[c] == slab_count - 1, 0.0, own))
    for c, each in enumerate(sizes):
        if not mirrored:
            break
        for block in arrived[c]:
            sums[c] = sums[c] + block[: each * planes].astype(jnp.float32)
        over = [(b, block) for b, block in enumerate(roles[c]) if b != block]
        if over:
            if c + 1 < len(sizes):
                sums[c], arrived[c + 1][2] = lax.optimization_barrier(
                    (sums[c], arrived[c + 1][2])
                )
            handed = lax.ppermute(sums[c].astype(jnp.bfloat16), "batch", over)
            sums[c] = jnp.where(blocks[c] == batch, sums[c], handed.astype(jnp.float32))

    meta_all = [meta_layer]
    if mirrored:
        for block in [block[sizes[0] * planes :] for block in arrived[0]]:
            block = block.reshape(META_ROWS, -1, LANES)
            halves = (block[:particles], block[particles : 2 * particles])
            low = jnp.concatenate(halves, axis=1)[:, :batch_count, : 2 * fields]
            meta_all.append(read_digits(low.transpose(1, 0, 2)))
    else:
        for step in range(1, slab_count):
            ring = [(s, (s + step) % slab_count) for s in range(slab_count)]
            meta_all.append(lax.ppermute(meta_layer, "slab", ring))
    meta_all = jnp.concatenate(meta_all, axis=0)

    own_freq = batch * rows + jnp.arange(rows, dtype=jnp.int32)
    own_plane = pick_block(find_planes(meta_all), batch) - slab * planes
    focus_count = defocus.shape[0]
    focus_hot = (meta_all[:, 1:2] == jnp.arange(focus_count)[None, :]).astype(jnp.bfloat16)
    if mirrored:
        own_plane = jnp.where(places[0] == slab_count - 1, -1, own_plane)
    bin_hot = (own_plane.T[:, None, :] == jnp.arange(planes)[None, :, None]).astype(jnp.bfloat16)
    counts = jnp.einsum("kzp,pd->kzd", bin_hot, focus_hot, preferred_element_type=jnp.float32)
    row_angle = 2.0 * (
        defocus[None, :] * centred_square(own_freq, length)[:, None] + PHASE_OFFSET
    )
    col_angle = 2.0 * (defocus[:, None] * centred_square(freq, length)[None, :])
    row_side = jnp.concatenate(
        [counts * jnp.cos(row_angle)[:, None, :], counts * jnp.sin(row_angle)[:, None, :]], axis=2
    )
    col_side = jnp.concatenate([jnp.cos(col_angle), -jnp.sin(col_angle)], axis=0)
    double = jnp.einsum("kzd,dx->kzx", row_side, col_side, precision=lax.Precision.HIGHEST)
    weights = 0.5 * (jnp.sum(counts, axis=2, keepdims=True) - double)
    denom = weights + TAU_PRIOR

    updated = []
    for c, each in enumerate(sizes):
        here = slice(starts[c], starts[c] + each)
        prior = ref[here].astype(jnp.float32)
        under = denom[here]
        total = sums[c].astype(jnp.float32).reshape(each, planes, 2 * length)
        updated.append(
            (
                (TAU_PRIOR * prior + total) / jnp.concatenate([under, under], axis=2)
            ).astype(jnp.bfloat16)
        )
    return jnp.concatenate(updated, axis=0)


def solution(mesh):
    placed = (
        P(("batch", "slab"), None, None),
        P(("batch", "slab")),
        P(("batch", "slab"), None),
        P(("batch", "slab")),
        P(),
        P(("batch", "slab"), None),
        P(),
        P("batch", "slab", None),
    )
    return jax.shard_map(
        per_device, mesh=mesh, in_specs=placed, out_specs=P("batch", "slab", None), check_vma=False
    )
```
